32 devices in a mesh: batch: 4 (over y, core), chan: 8 (over z, x).
Axes of the slice: x: 2, y: 2, z: 4, core: 2. Of those that a mesh axis runs over, the one named last changes fastest.
Arguments:
- inputs: bfloat16 [512, 65536], P('chan', 'batch'), may hold values from -6 to 6
- lengths: int32 [64], P('batch'), may hold values from 1 to 1024, 49152 in all
- cotangent: bfloat16 [512, 65536], P('chan', 'batch'), may hold values from -6 to 6
- ln_gain: float32 [2, 512], P(None, 'chan'), may hold values from 0.5 to 1.5
- ln_bias: float32 [2, 512], P(None, 'chan'), may hold values from -3 to 3
- log_step: float32 [2, 512], P(None, 'chan'), may hold values from -6.9 to -2.3
- skip_gain: float32 [2, 512], P(None, 'chan'), may hold values from -4 to 4
- lin_bias: float32 [2, 2, 512], P(None, None, 'chan'), may hold values from -3 to 3
- log_decay: float32 [2, 512, 64], P(None, 'chan'), may hold values from -1 to 1
- frequency: float32 [2, 512, 64], P(None, 'chan'), may hold values from 0 to 4
- w_re: float32 [2, 512, 64], P(None, 'chan'), may hold values from -3 to 3
- w_im: float32 [2, 512, 64], P(None, 'chan'), may hold values from -3 to 3
- lin_weight: float32 [2, 512, 2, 512], P(None, 'chan'), may hold values from -0.25 to 0.25
- lin_moment: float32 [2, 512, 2, 512], P(None, 'chan'), may hold values from -24 to 24
- lin_square: float32 [2, 512, 2, 512], P(None, 'chan'), may hold values from 1.114112 to 4.58752
- vec_moment: float32 [2, 6, 512], P(None, None, 'chan'), may hold values from -48 to 48
- vec_square: float32 [2, 6, 512], P(None, None, 'chan'), may hold values from 5.89824 to 23.59296
- state_moment: float32 [2, 4, 512, 64], P(None, None, 'chan'), may hold values from -48 to 48
- state_square: float32 [2, 4, 512, 64], P(None, None, 'chan'), may hold values from 5.89824 to 23.59296
Outputs:
- output: float32 [512, 65536], P('chan', 'batch')
- input_grad: float32 [512, 65536], P('chan', 'batch')
- lin_first: float32 [2, 512, 2, 512], P(None, 'chan')
- lin_second: float32 [2, 512, 2, 512], P(None, 'chan')
- lin_new: float32 [2, 512, 2, 512], P(None, 'chan')
- vec_first: float32 [2, 6, 512], P(None, None, 'chan')
- vec_second: float32 [2, 6, 512], P(None, None, 'chan')
- vec_new: float32 [2, 6, 512], P(None, None, 'chan')
- state_first: float32 [2, 4, 512, 64], P(None, None, 'chan')
- state_second: float32 [2, 4, 512, 64], P(None, None, 'chan')
- state_new: float32 [2, 4, 512, 64], P(None, None, 'chan')
The draws below stay inside these ranges and needn't reach their ends.
Inputs may be any that keep to these rules, and one draw needn't show every extreme that they name: `lengths`: in every draw some sequence has exactly 1024 valid tokens.
All inputs are finite; a program needn't handle non-finite values. No bound on the sum of `lengths` on one device may be relied on, other than what follows from the above.
Results may differ from the reference program's by a relative error of at most 0.0061.
Values may be sent and summed in bfloat16 or wider, within the bound.
A program may use at most 256 MiB of HBM per device.

```python
import math
import jax
import jax.numpy as jnp
import numpy as np
from jax import lax

H = 512
N = 64
LAYERS = 2
BUCKET = 1024
SEQ_DEV = 16
STEP = 10
SEQS = 64
TOKENS = 65536
N_BATCH = 4


def block_scale(key, extent, split, low, top_value):
    loudness, own = 1.0, jax.random.fold_in(key, 6)
    for axis_at, shards_of in split:
        steps = jnp.exp(jax.random.uniform(jax.random.fold_in(own, axis_at), (shards_of,), jnp.float32, low / len(split), top_value / len(split)))
        loudness = loudness * jnp.repeat(steps, extent[axis_at] // shards_of).reshape([-1 if axis == axis_at else 1 for axis in range(len(extent))])
    return loudness


def length_profile(number_of, total, most, slope):
    portions = [(1 << 20) // math.isqrt(rank ** slope) + 1 for rank in range(2, number_of + 1)]
    rest, holding = total - most - (number_of - 1), [1] * (number_of - 1)
    while rest > 0:
        free = [i for i in range(number_of - 1) if holding[i] < most]
        mass, left = sum([portions[i] for i in free]), rest
        for i in free:
            addition = min(most - holding[i], max(1, left * portions[i] // mass), rest)
            holding[i] = holding[i] + addition
            rest = rest - addition
    return np.array([most] + holding)


def uneven_parts(own_key, count, total, most, slope):
    if count == 2:
        one = jax.random.randint(own_key, (), max(1, total - most), min(most, total - 1) + 1)
        return jnp.stack([one, total - one])
    tallies = jnp.asarray(length_profile(count, total, most, slope), jnp.int32)
    couples = (count - 1) // 2
    giver, receiver = tallies[1:1 + 2 * couples:2], tallies[2:2 + 2 * couples:2]
    room = jnp.minimum(giver - 1, most - receiver)
    passed = jax.random.randint(jax.random.fold_in(own_key, 1), (couples,), 0, 1 << 20) % (room + 1)
    tallies = tallies.at[1:1 + 2 * couples:2].set(giver - passed).at[2:2 + 2 * couples:2].set(receiver + passed)
    return tallies[jax.random.permutation(jax.random.fold_in(own_key, 2), count)]


def normal_values(rng, extent, scale, reach, cuts=(), kind=jnp.bfloat16):
    drawn = scale * jax.random.normal(rng, extent, jnp.float32)
    if cuts:
        drawn = drawn * block_scale(rng, extent, cuts, -0.22, 0.18)
    return jnp.clip(drawn, -reach, reach).astype(kind)


def setup_inputs(seed: int = 0) -> dict:
    splits = jax.random.split(jax.random.key(seed), 20)
    inputs = normal_values(splits[0], (H, TOKENS), 1.0, 6.0, ((0, 8), (1, 4)))
    lengths = uneven_parts(splits[1], SEQS, SEQS * BUCKET * 3 // 4, BUCKET, 0).astype(jnp.int32)
    cotangent = normal_values(splits[2], (H, TOKENS), 1.0, 6.0, ((0, 8), (1, 4)))
    ln_gain = jnp.clip(1.0 + 0.1 * jax.random.normal(splits[3], (LAYERS, H), jnp.float32), 0.5, 1.5)
    ln_bias = normal_values(splits[4], (LAYERS, H), 0.3, 3.0, ((1, 8),), jnp.float32)
    log_step = jnp.clip(-6.9 + 4.6000001430511475 * jax.random.uniform(splits[5], (LAYERS, H), jnp.float32) ** block_scale(splits[5], (LAYERS, H), ((1, 8),), -0.2, 0.2), -6.9, -2.3)
    skip_gain = normal_values(splits[6], (LAYERS, H), 1.0, 4.0, ((1, 8),), jnp.float32)
    lin_bias = normal_values(splits[7], (LAYERS, 2, H), 0.3, 3.0, ((2, 8),), jnp.float32)
    log_decay = jnp.clip(jax.random.uniform(splits[8], (LAYERS, H, N), jnp.float32, -1.0, 1.0) * block_scale(splits[8], (LAYERS, H, N), ((1, 8),), -0.4, 0.0), -1.0, 1.0)
    frequency = jnp.clip(4.0 * jax.random.uniform(splits[9], (LAYERS, H, N), jnp.float32) ** block_scale(splits[9], (LAYERS, H, N), ((1, 8),), -0.2, 0.2), 0.0, 4.0)
    w_re = normal_values(splits[10], (LAYERS, H, N), 0.3, 3.0, ((1, 8),), jnp.float32)
    w_im = normal_values(splits[11], (LAYERS, H, N), 0.3, 3.0, ((1, 8),), jnp.float32)
    lin_weight = normal_values(splits[12], (LAYERS, H, 2, H), H ** -0.5, 0.25, ((1, 8),), jnp.float32)
    lin_moment = normal_values(splits[13], (LAYERS, H, 2, H), (0.015 * TOKENS ** 0.5), 24.0, ((1, 8),), jnp.float32)
    lin_square = jnp.clip(jnp.exp(math.log(4.58752) - 1.4152819 * jax.random.uniform(splits[14], (LAYERS, H, 2, H), jnp.float32) ** block_scale(splits[14], (LAYERS, H, 2, H), ((1, 8),), -0.2, 0.2)), 1.114112, 4.58752)
    vec_moment = normal_values(splits[15], (LAYERS, 6, H), (0.033 * TOKENS ** 0.5), 48.0, ((2, 8),), jnp.float32)
    vec_square = jnp.clip(jnp.exp(math.log(23.59296) - 1.3862944 * jax.random.uniform(splits[16], (LAYERS, 6, H), jnp.float32) ** block_scale(splits[16], (LAYERS, 6, H), ((2, 8),), -0.2, 0.2)), 5.89824, 23.59296)
    state_moment = normal_values(splits[17], (LAYERS, 4, H, N), (0.033 * TOKENS ** 0.5), 48.0, ((2, 8),), jnp.float32)
    state_square = jnp.clip(jnp.exp(math.log(23.59296) - 1.3862944 * jax.random.uniform(splits[18], (LAYERS, 4, H, N), jnp.float32) ** block_scale(splits[18], (LAYERS, 4, H, N), ((2, 8),), -0.2, 0.2)), 5.89824, 23.59296)
    return dict(inputs=inputs, lengths=lengths, cotangent=cotangent, ln_gain=ln_gain, ln_bias=ln_bias, log_step=log_step, skip_gain=skip_gain, lin_bias=lin_bias, log_decay=log_decay, frequency=frequency, w_re=w_re, w_im=w_im, lin_weight=lin_weight, lin_moment=lin_moment, lin_square=lin_square, vec_moment=vec_moment, vec_square=vec_square, state_moment=state_moment, state_square=state_square)


@jax.custom_vjp
def low(v):
    return lax.optimization_barrier(v.astype(jnp.bfloat16)).astype(jnp.float32)

@jax.custom_vjp
def low_back(v):
    return v

def low_keep(v):
    return (low(v), None)

def low_pass(kept, grad):
    return (grad,)

def back_keep(v):
    return (v, None)

def back_low(kept, grad):
    return (low(grad),)
low.defvjp(low_keep, low_pass)
low_back.defvjp(back_keep, back_low)

def make_kernel(log_decay, frequency, w_re, w_im, log_step):
    step_size = jnp.exp(log_step)[:, None]
    decay_rate = step_size * jnp.exp(log_decay)
    turn_rate = step_size * frequency
    places = jnp.arange(BUCKET).astype(jnp.float32)
    decay_all = jnp.exp(-decay_rate[..., None] * places)
    soft = decay_all / lax.optimization_barrier(jnp.sum(decay_all, -1, keepdims=True))
    phase_all = turn_rate[..., None] * places
    return lax.optimization_barrier(jnp.sum((w_re[..., None] * jnp.cos(phase_all) - w_im[..., None] * jnp.sin(phase_all)) * soft, 1))

def causal(normed, kernel):
    full_len = 2 * BUCKET
    spectrum = jnp.fft.rfft(normed, n=full_len, axis=1)
    kernel_spec = jnp.fft.rfft(kernel, n=full_len, axis=1).T
    return jnp.fft.irfft(spectrum * kernel_spec[None], n=full_len, axis=1)[:, :BUCKET]

def forward(params, stream, valid):
    ln_gain, ln_bias, log_step, skip_gain, lin_bias, log_decay, frequency, w_re, w_im, lin_weight = params
    top_prec = lax.Precision.HIGHEST
    for layer_idx in range(LAYERS):
        mean_val = lax.optimization_barrier(jnp.mean(stream, -1, keepdims=True))
        variance = lax.optimization_barrier(jnp.mean((stream - mean_val) ** 2, -1, keepdims=True))
        normed = (stream - mean_val) * lax.rsqrt(variance + 1e-05) * ln_gain[layer_idx] + ln_bias[layer_idx]
        kernel = make_kernel(log_decay[layer_idx], frequency[layer_idx], w_re[layer_idx], w_im[layer_idx], log_step[layer_idx])
        pre_act = causal(normed, kernel) + skip_gain[layer_idx] * normed
        activated = low(jax.nn.gelu(pre_act))
        mixed = jnp.einsum('slh,cjh->sljc', activated, low(lin_weight[layer_idx]), precision=top_prec)
        mixed = low_back(mixed + lin_bias[layer_idx])
        stream = stream + valid[..., None] * mixed[..., 0, :] * jax.nn.sigmoid(mixed[..., 1, :])
    return stream

def adam(weight, grad, first, second, rate):
    first_new = 0.9 * first + 0.1 * grad
    second_new = 0.999 * second + 0.001 * grad * grad
    fixed_first = first_new / (1.0 - 0.9 ** STEP)
    fixed_second = second_new / (1.0 - 0.999 ** STEP)
    new_weight = weight - rate * (fixed_first / (jnp.sqrt(fixed_second) + 1e-08) + 0.01 * weight)
    return (first_new, second_new, new_weight)

def reference(inputs, lengths, cotangent, ln_gain, ln_bias, log_step, skip_gain, lin_bias, log_decay, frequency, w_re, w_im, lin_weight, lin_moment, lin_square, vec_moment, vec_square, state_moment, state_square):
    params = (ln_gain, ln_bias, log_step, skip_gain, lin_bias, log_decay, frequency, w_re, w_im, lin_weight)
    places = jnp.arange(BUCKET).astype(jnp.int32)
    valid = (places[None, :] < lengths[:, None]).astype(jnp.float32).reshape(N_BATCH, SEQ_DEV, BUCKET)
    stream_in = inputs.astype(jnp.float32).T.reshape(N_BATCH, SEQ_DEV, BUCKET, H)
    back_in = cotangent.astype(jnp.float32).T.reshape(N_BATCH, SEQ_DEV, BUCKET, H)

    def group_step(grad_total, item):
        group_in, group_back, group_valid = item
        result, pullback = jax.vjp(lambda weights, data: forward(weights, data, group_valid), params, group_in)
        weight_grads, data_grad = pullback(group_back)
        grad_total = jax.tree.map(lambda a, b: a + b, grad_total, weight_grads)
        return (grad_total, (result, data_grad))
    start = jax.tree.map(jnp.zeros_like, params)
    grads, (results, data_grads) = lax.scan(group_step, start, (stream_in, back_in, valid))
    g_gain, g_shift, g_step, g_skip, g_bias, g_decay, g_freq, g_re, g_im, g_lin = grads
    vec_old = jnp.stack([ln_gain, ln_bias, log_step, skip_gain, lin_bias[:, 0], lin_bias[:, 1]], 1)
    vec_grad = jnp.stack([g_gain, g_shift, g_step, g_skip, g_bias[:, 0], g_bias[:, 1]], 1)
    state_old = jnp.stack([log_decay, frequency, w_re, w_im], 1)
    state_grad = jnp.stack([g_decay, g_freq, g_re, g_im], 1)
    lin_first, lin_second, lin_new = adam(lin_weight, g_lin, lin_moment, lin_square, 0.05)
    vec_first, vec_second, vec_new = adam(vec_old, vec_grad, vec_moment, vec_square, 0.2)
    state_first, state_second, state_new = adam(state_old, state_grad, state_moment, state_square, 0.2)
    return (results.reshape(TOKENS, H).T, data_grads.reshape(TOKENS, H).T, lin_first, lin_second, lin_new, vec_first, vec_second, vec_new, state_first, state_second, state_new)
```

```python
import math

import jax
import jax.numpy as jnp
from jax import lax
from jax.sharding import PartitionSpec as P

LAYERS = 2
BUCKET = 1024
STEP = 10


def transforms():
    rows = lax.iota(jnp.int32, BUCKET)[:, None]
    cols = lax.iota(jnp.int32, BUCKET)[None, :]
    turn = (rows * cols % (2 * BUCKET)).astype(jnp.float32) * (math.pi / BUCKET)
    alternate = (1 - 2 * (rows % 2)).astype(jnp.float32)
    cosine = jnp.cos(turn)
    minus_sine = jnp.where(cols == 0, alternate, -jnp.sin(turn))
    forward = jnp.concatenate([cosine, minus_sine], 1)
    weights = jnp.where(cols == 0, 1.0, 2.0) / (2.0 * BUCKET)
    inverse = jnp.concatenate([cosine * weights, minus_sine * weights], 1).T
    return forward.astype(jnp.bfloat16), inverse.astype(jnp.bfloat16)


def dot(a, b):
    return jnp.dot(a.astype(jnp.bfloat16), b, preferred_element_type=jnp.float32)


def powers(decay_rate, turn_rate, places):
    size = jnp.exp(-decay_rate[..., None] * places)
    phase = turn_rate[..., None] * places
    return size * jnp.cos(phase), size * jnp.sin(phase), size


def state_tables(log_decay, frequency, log_step):
    step_size = jnp.exp(log_step)[..., None]
    decay_rate = step_size * jnp.exp(log_decay)
    turn_rate = step_size * frequency
    fine = lax.iota(jnp.float32, 32)
    lo_re, lo_im, lo = powers(decay_rate, turn_rate, fine)
    hi_re, hi_im, hi = powers(decay_rate, turn_rate, fine * 32.0)
    total = jnp.sum(lo, -1) * jnp.sum(hi, -1)
    moment = jnp.sum(lo * fine, -1) * jnp.sum(hi, -1) + jnp.sum(lo, -1) * jnp.sum(hi * (fine * 32.0), -1)
    return decay_rate, turn_rate, lo_re, lo_im, hi_re, hi_im, total, moment


def make_kernel(log_decay, frequency, w_re, w_im, log_step):
    _, _, lo_re, lo_im, hi_re, hi_im, total, _ = state_tables(log_decay, frequency, log_step)
    a_re = (w_re / total)[..., None]
    a_im = (w_im / total)[..., None]
    c_re = a_re * hi_re - a_im * hi_im
    c_im = a_re * hi_im + a_im * hi_re
    out = jnp.sum(c_re[..., :, None] * lo_re[..., None, :] - c_im[..., :, None] * lo_im[..., None, :], -3)
    return out.reshape(out.shape[:-2] + (BUCKET,))


def kernel_back(grad, log_decay, frequency, w_re, w_im, log_step):
    decay_rate, turn_rate, lo_re, lo_im, hi_re, hi_im, total, moment = state_tables(log_decay, frequency, log_step)
    fine = lax.iota(jnp.float32, 32)
    g = grad.reshape(grad.shape[:-1] + (1, 32, 32))
    t_re = jnp.sum(g * lo_re[..., None, :], -1)
    t_im = jnp.sum(g * lo_im[..., None, :], -1)
    g_fine = g * fine
    u_re = jnp.sum(g_fine * lo_re[..., None, :], -1) + t_re * (fine * 32.0)
    u_im = jnp.sum(g_fine * lo_im[..., None, :], -1) + t_im * (fine * 32.0)
    c_re = jnp.sum(t_re * hi_re - t_im * hi_im, -1) / total
    c_im = jnp.sum(t_re * hi_im + t_im * hi_re, -1) / total
    d_re = jnp.sum(u_re * hi_re - u_im * hi_im, -1) / total
    d_im = jnp.sum(u_re * hi_im + u_im * hi_re, -1) / total
    turn_grad = -(w_re * d_im + w_im * d_re)
    decay_grad = (w_re * c_re - w_im * c_im) * (moment / total) - (w_re * d_re - w_im * d_im)
    step_grad = jnp.sum(decay_grad * decay_rate + turn_grad * turn_rate, -1)
    freq_grad = turn_grad * jnp.exp(log_step)[..., None]
    return decay_grad * decay_rate, freq_grad, c_re, -c_im, step_grad


def adam(weight, grad, first, second, rate):
    first_new = 0.9 * first + 0.1 * grad
    second_new = 0.999 * second + 0.001 * grad * grad
    fixed_first = first_new / (1.0 - 0.9**STEP)
    fixed_second = second_new / (1.0 - 0.999**STEP)
    new_weight = weight - rate * (fixed_first / (jnp.sqrt(fixed_second) + 1e-08) + 0.01 * weight)
    return (first_new, second_new, new_weight)


def spread(block, axis):
    count = lax.axis_size(axis)
    return lax.all_to_all(jnp.broadcast_to(block[None], (count,) + block.shape), axis, 0, 0, tiled=True)


def local(
    inputs, lengths, cotangent, ln_gain, ln_bias, log_step, skip_gain, lin_bias, log_decay, frequency,
    w_re, w_im, lin_weight, lin_moment, lin_square, vec_moment, vec_square, state_moment, state_square,
):
    n_chan = lax.axis_size("chan")
    n_batch = lax.axis_size("batch")
    own = inputs.shape[0]
    chans = own * n_chan
    toks = inputs.shape[1] // n_chan
    seqs = toks // BUCKET
    part = own // n_batch
    me = lax.axis_index("chan")
    row = lax.axis_index("batch")
    lens = lax.dynamic_slice_in_dim(lengths, me * seqs, seqs)
    places = lax.iota(jnp.int32, BUCKET)
    valid = (places[None, :] < lens[:, None]).astype(jnp.float32).reshape(1, toks)
    forward, inverse = transforms()
    bin_zero = (lax.iota(jnp.int32, BUCKET) == 0)[None, :]

    def mine(a):
        return lax.dynamic_slice_in_dim(a, row * part, part, 1)

    state_args = [mine(a) for a in (log_decay, frequency, w_re, w_im, log_step)]
    ker_own = make_kernel(*state_args)
    w_own = lax.dynamic_slice_in_dim(lin_weight, row * part, part, 1).reshape(LAYERS, part, 2 * chans)
    pack = jnp.stack([ker_own.reshape(LAYERS, part, BUCKET), w_own.reshape(LAYERS, part, BUCKET)], 1).astype(jnp.bfloat16)
    vec_own = jnp.concatenate([ln_gain, ln_bias, skip_gain, lin_bias.reshape(LAYERS * 2, own)], 0)
    vec_all = spread(vec_own, "chan").transpose(1, 0, 2).reshape(10, chans)
    gains, shifts, skips = vec_all[0:2], vec_all[2:4], vec_all[4:6]
    biases = vec_all[6:10].reshape(LAYERS, 2, chans)
    pack = spread(pack, "chan")
    pack = spread(pack, "batch")
    pack = pack.transpose(2, 3, 1, 0, 4, 5)
    kers = pack[:, 0].reshape(LAYERS, chans, BUCKET)
    weights = pack[:, 1].reshape(LAYERS, chans, 2, chans)

    first_low = lax.all_to_all(inputs, "chan", 1, 0, tiled=True)
    cot_low = lax.all_to_all(cotangent, "chan", 1, 0, tiled=True)
    stream0 = first_low.astype(jnp.float32)
    stream = stream0

    def spectrum(signal):
        halves = [dot(signal[:, s * BUCKET : (s + 1) * BUCKET], forward) for s in range(seqs)]
        return [(h[:, :BUCKET], h[:, BUCKET:]) for h in halves]

    def back_to_time(spec):
        return jnp.concatenate([dot(jnp.concatenate([r, i], 1), inverse) for r, i in spec], 1)

    def times(a, b):
        a_re, a_im = a
        b_re, b_im = b
        cross = a_im * b_im
        return a_re * b_re - jnp.where(bin_zero, 0.0, cross), jnp.where(bin_zero, cross, a_re * b_im + a_im * b_re)

    def times_conj(a, b):
        a_re, a_im = a
        b_re, b_im = b
        cross = a_im * b_im
        return a_re * b_re + jnp.where(bin_zero, 0.0, cross), jnp.where(bin_zero, cross, a_re * b_im - a_im * b_re)

    saved = []
    for i in range(LAYERS):
        mean_val = jnp.mean(stream, 0, keepdims=True)
        variance = jnp.mean(stream * stream, 0, keepdims=True) - mean_val * mean_val
        inv_std = lax.rsqrt(variance + 1e-05)
        centred = (stream - mean_val) * inv_std
        normed = centred * gains[i][:, None] + shifts[i][:, None]
        ker_both = dot(kers[i], forward)
        ker_spec = (ker_both[:, :BUCKET], ker_both[:, BUCKET:])
        sig_spec = spectrum(normed)
        pre = back_to_time([times(s, ker_spec) for s in sig_spec]) + skips[i][:, None] * normed
        act = jax.nn.gelu(pre).astype(jnp.bfloat16)
        mixed = jnp.einsum("jch,ht->cjt", weights[i], act, preferred_element_type=jnp.float32)
        gate_in = mixed[0] + biases[i, 0][:, None]
        gate_val = mixed[1] + biases[i, 1][:, None]
        stream = stream + valid * gate_in * jax.nn.sigmoid(gate_val)
        saved.append((centred, inv_std, normed, ker_spec, sig_spec, pre, act, gate_in, gate_val))
    out_delta = (stream - stream0).astype(jnp.bfloat16)
    out_delta = lax.all_to_all(out_delta, "chan", 0, 1, tiled=True)
    output = inputs.astype(jnp.float32) + out_delta.astype(jnp.float32)

    back0 = cot_low.astype(jnp.float32)
    back = back0
    packs = [None] * LAYERS
    vecs = [None] * LAYERS
    for i in reversed(range(LAYERS)):
        centred, inv_std, normed, ker_spec, sig_spec, pre, act, gate_in, gate_val = saved[i]
        sigma = jax.nn.sigmoid(gate_val)
        gated = back * valid
        grad_in = (gated * sigma).astype(jnp.bfloat16)
        grad_val = (gated * gate_in * sigma * (1.0 - sigma)).astype(jnp.bfloat16)
        grad_mixed = jnp.stack([grad_in, grad_val], 0)
        bias_grad = jnp.sum(grad_mixed.astype(jnp.float32), 2)
        weight_grad = jnp.einsum("cjt,ht->jch", grad_mixed, act, preferred_element_type=jnp.float32)
        act_grad = jnp.einsum("jch,cjt->ht", weights[i], grad_mixed, preferred_element_type=jnp.float32)
        _, gelu_back = jax.vjp(jax.nn.gelu, pre)
        (pre_grad,) = gelu_back(act_grad)
        grad_spec = spectrum(pre_grad)
        normed_grad = back_to_time([times_conj(ker_spec, g) for g in grad_spec]) + skips[i][:, None] * pre_grad
        cross = [times_conj(s, g) for s, g in zip(sig_spec, grad_spec)]
        cross = [(sum(c[0] for c in cross), sum(c[1] for c in cross))]
        ker_grad = back_to_time(cross)
        skip_grad = jnp.sum(pre_grad * normed, 1)
        gain_grad = jnp.sum(normed_grad * centred, 1)
        shift_grad = jnp.sum(normed_grad, 1)
        cent_grad = normed_grad * gains[i][:, None]
        sum_a = jnp.mean(cent_grad, 0, keepdims=True)
        sum_b = jnp.mean(cent_grad * centred, 0, keepdims=True)
        back = back + inv_std * (cent_grad - sum_a - centred * sum_b)
        packs[i] = jnp.stack([ker_grad.reshape(n_chan, n_batch, part, BUCKET), weight_grad.reshape(n_chan, n_batch, part, BUCKET)], 2)
        vecs[i] = jnp.stack([gain_grad, shift_grad, skip_grad, bias_grad[0], bias_grad[1]])
    in_delta = (back - back0).astype(jnp.bfloat16)
    in_delta = lax.all_to_all(in_delta, "chan", 0, 1, tiled=True)
    input_grad = cotangent.astype(jnp.float32) + in_delta.astype(jnp.float32)

    grads = jnp.stack(packs, 2).astype(jnp.bfloat16)
    grads = lax.all_to_all(grads, "batch", 1, 1, tiled=True)
    grads = jnp.sum(grads.astype(jnp.float32), 1).astype(jnp.bfloat16)
    grads = lax.all_to_all(grads, "chan", 0, 0, tiled=True)
    grads = jnp.sum(grads.astype(jnp.float32), 0)
    vec_part = jnp.stack(vecs).reshape(LAYERS, 5, n_chan, own).transpose(2, 0, 1, 3)
    vec_part = jnp.sum(lax.all_to_all(vec_part, "chan", 0, 0, tiled=True), 0)

    state_parts = kernel_back(grads[:, 0], *state_args)
    step_grad = state_parts[4]
    state_grad = jnp.stack(state_parts[:4], 1)
    send = jnp.concatenate(
        [state_grad.reshape(-1), grads[:, 1].reshape(-1), step_grad.reshape(-1), vec_part.reshape(-1)]
    )
    got = spread(send, "batch").reshape(n_batch, -1)
    sizes = [state_grad.size, grads[:, 1].size, step_grad.size, vec_part.size]
    cuts = [sum(sizes[:k]) for k in range(5)]
    state_total = got[:, cuts[0] : cuts[1]].reshape((n_batch,) + state_grad.shape).transpose(1, 2, 0, 3, 4)
    state_total = state_total.reshape(LAYERS, 4, own, -1)
    lin_total = got[:, cuts[1] : cuts[2]].reshape(n_batch, LAYERS, part, 2, chans).transpose(1, 0, 2, 3, 4)
    lin_total = lin_total.reshape(LAYERS, own, 2, chans)
    step_total = got[:, cuts[2] : cuts[3]].reshape(n_batch, LAYERS, part).transpose(1, 0, 2).reshape(LAYERS, own)
    vec_sum = jnp.sum(got[:, cuts[3] : cuts[4]], 0).reshape(LAYERS, 5, own)
    vec_total = jnp.stack([vec_sum[:, 0], vec_sum[:, 1], step_total, vec_sum[:, 2], vec_sum[:, 3], vec_sum[:, 4]], 1)

    vec_old = jnp.stack([ln_gain, ln_bias, log_step, skip_gain, lin_bias[:, 0], lin_bias[:, 1]], 1)
    state_old = jnp.stack([log_decay, frequency, w_re, w_im], 1)
    lin_first, lin_second, lin_new = adam(lin_weight, lin_total, lin_moment, lin_square, 0.05)
    vec_first, vec_second, vec_new = adam(vec_old, vec_total, vec_moment, vec_square, 0.2)
    state_first, state_second, state_new = adam(state_old, state_total, state_moment, state_square, 0.2)
    return (
        output, input_grad, lin_first, lin_second, lin_new, vec_first, vec_second, vec_new,
        state_first, state_second, state_new,
    )


def tables(length):
    full_width = 2 * length
    row_ids = lax.iota(jnp.int32, length)[:, None]
    col_ids = lax.iota(jnp.int32, length)[None, :]
    turn_all = (row_ids * col_ids % full_width).astype(jnp.float32) * (2.0 * math.pi / full_width)
    cosine = jnp.cos(turn_all)
    sine_table = jnp.sin(turn_all)
    weights = jnp.where(lax.iota(jnp.int32, length) == 0, 1.0, 2.0).astype(jnp.float32)[None, :]
    alternate = (1 - 2 * (lax.iota(jnp.int32, length) % 2)).astype(jnp.float32)
    return (cosine, sine_table, cosine * weights, sine_table * weights, alternate)


def mixer(normed, log_decay, frequency, w_re, w_im, log_step, skip_gain):
    top_prec = lax.Precision.HIGHEST
    chan_count = normed.shape[0]
    seq_count = normed.shape[1] // BUCKET
    step_size = jnp.exp(log_step)[:, None]
    decay_rate = step_size * jnp.exp(log_decay)
    turn_rate = step_size * frequency
    places = lax.iota(jnp.float32, BUCKET)
    decay_all = jnp.exp(-decay_rate[..., None] * places)
    soft = decay_all / jnp.sum(decay_all, -1, keepdims=True)
    phase_all = turn_rate[..., None] * places
    kernel = jnp.sum(
        (w_re[..., None] * jnp.cos(phase_all) - w_im[..., None] * jnp.sin(phase_all)) * soft, 1
    )
    cosine, sine_table, cos_back, sin_back, alternate = tables(BUCKET)
    signal = normed.reshape(chan_count, seq_count, BUCKET)
    sig_re = jnp.einsum("csl,lk->csk", signal, cosine, precision=top_prec)
    sig_im = -jnp.einsum("csl,lk->csk", signal, sine_table, precision=top_prec)
    sig_top = jnp.sum(signal * alternate, -1)
    ker_re = jnp.dot(kernel, cosine, precision=top_prec)[:, None, :]
    ker_im = -jnp.dot(kernel, sine_table, precision=top_prec)[:, None, :]
    ker_top = jnp.sum(kernel * alternate, -1)[:, None]
    prod_re = sig_re * ker_re - sig_im * ker_im
    prod_im = sig_re * ker_im + sig_im * ker_re
    prod_top = sig_top * ker_top
    conv_out = jnp.einsum("csk,lk->csl", prod_re, cos_back, precision=top_prec)
    conv_out = conv_out - jnp.einsum("csk,lk->csl", prod_im, sin_back, precision=top_prec)
    conv_out = conv_out + prod_top[..., None] * alternate
    conv_out = conv_out / (2.0 * BUCKET)
    pre_act = conv_out.reshape(normed.shape) + skip_gain[:, None] * normed
    return jax.nn.gelu(pre_act)


def wide_local(
    inputs,
    lengths,
    cotangent,
    ln_gain,
    ln_bias,
    log_step,
    skip_gain,
    lin_bias,
    log_decay,
    frequency,
    w_re,
    w_im,
    lin_weight,
    lin_moment,
    lin_square,
    vec_moment,
    vec_square,
    state_moment,
    state_square,
):
    chan_total = inputs.shape[0] * lax.axis_size("chan")
    tok_count = inputs.shape[1]
    places = lax.iota(jnp.int32, BUCKET)
    valid = (places[None, :] < lengths[:, None]).astype(jnp.float32).reshape(1, tok_count)
    weights_low = lin_weight.astype(jnp.bfloat16)
    stream = inputs.astype(jnp.float32)
    saved = []
    for layer_idx in range(LAYERS):
        sums = lax.psum((jnp.sum(stream, 0), jnp.sum(stream * stream, 0)), "chan")
        mean_val = sums[0] / chan_total
        variance = sums[1] / chan_total - mean_val * mean_val
        inv_std = lax.rsqrt(variance + 1e-05)[None, :]
        centred = (stream - mean_val[None, :]) * inv_std
        normed = centred * ln_gain[layer_idx][:, None] + ln_bias[layer_idx][:, None]
        activated, mixer_back = jax.vjp(
            mixer,
            normed,
            log_decay[layer_idx],
            frequency[layer_idx],
            w_re[layer_idx],
            w_im[layer_idx],
            log_step[layer_idx],
            skip_gain[layer_idx],
        )
        act_low = activated.astype(jnp.bfloat16)
        act_all = lax.all_gather(act_low, "chan", axis=0, tiled=True)
        mixed = jnp.einsum(
            "ht,cjh->cjt", act_all, weights_low[layer_idx], preferred_element_type=jnp.float32
        )
        kept = act_all
        mixed = mixed + lin_bias[layer_idx].T[:, :, None]
        gate_in = mixed[:, 0]
        gate_val = mixed[:, 1]
        stream = stream + valid * gate_in * jax.nn.sigmoid(gate_val)
        saved.append((centred, inv_std, mixer_back, kept, gate_in, gate_val))
    back_stream = cotangent.astype(jnp.float32)
    lin_grads = [None] * LAYERS
    vec_grads = [None] * LAYERS
    state_grads = [None] * LAYERS
    for layer_idx in reversed(range(LAYERS)):
        centred, inv_std, mixer_back, kept, gate_in, gate_val = saved[layer_idx]
        sigma = jax.nn.sigmoid(gate_val)
        gated_back = back_stream * valid
        grad_mixed = jnp.stack(
            [gated_back * sigma, gated_back * gate_in * sigma * (1.0 - sigma)], 1
        ).astype(jnp.bfloat16)
        bias_grad = jnp.sum(grad_mixed.astype(jnp.float32), 2).T
        weight_grad = jnp.einsum(
            "ht,cjt->cjh", kept, grad_mixed, preferred_element_type=jnp.float32
        )
        act_part = jnp.einsum(
            "cjt,cjh->ht", grad_mixed, weights_low[layer_idx], preferred_element_type=jnp.float32
        )
        act_grad = lax.psum_scatter(act_part, "chan", scatter_dimension=0, tiled=True)
        normed_grad, decay_grad, freq_grad, re_grad, im_grad, step_grad, skip_grad = mixer_back(
            act_grad
        )
        gain_grad = jnp.sum(normed_grad * centred, 1)
        shift_grad = jnp.sum(normed_grad, 1)
        centred_grad = normed_grad * ln_gain[layer_idx][:, None]
        back_sums = lax.psum((jnp.sum(centred_grad, 0), jnp.sum(centred_grad * centred, 0)), "chan")
        back_stream = back_stream + inv_std * (
            centred_grad
            - back_sums[0][None, :] / chan_total
            - centred * back_sums[1][None, :] / chan_total
        )
        lin_grads[layer_idx] = weight_grad
        vec_grads[layer_idx] = jnp.stack(
            [gain_grad, shift_grad, step_grad, skip_grad, bias_grad[0], bias_grad[1]]
        )
        state_grads[layer_idx] = jnp.stack([decay_grad, freq_grad, re_grad, im_grad])
    lin_total, vec_total, state_total = lax.psum(
        (jnp.stack(lin_grads), jnp.stack(vec_grads), jnp.stack(state_grads)), "batch"
    )
    vec_old = jnp.stack([ln_gain, ln_bias, log_step, skip_gain, lin_bias[:, 0], lin_bias[:, 1]], 1)
    state_old = jnp.stack([log_decay, frequency, w_re, w_im], 1)
    lin_first, lin_second, lin_new = adam(lin_weight, lin_total, lin_moment, lin_square, 0.05)
    vec_first, vec_second, vec_new = adam(vec_old, vec_total, vec_moment, vec_square, 0.2)
    state_first, state_second, state_new = adam(
        state_old, state_total, state_moment, state_square, 0.2
    )
    return (
        stream,
        back_stream,
        lin_first,
        lin_second,
        lin_new,
        vec_first,
        vec_second,
        vec_new,
        state_first,
        state_second,
        state_new,
    )


def solution(mesh):
    in_specs = (
        P("chan", "batch"),
        P("batch"),
        P("chan", "batch"),
        P(None, "chan"),
        P(None, "chan"),
        P(None, "chan"),
        P(None, "chan"),
        P(None, None, "chan"),
        P(None, "chan", None),
        P(None, "chan", None),
        P(None, "chan", None),
        P(None, "chan", None),
        P(None, "chan", None, None),
        P(None, "chan", None, None),
        P(None, "chan", None, None),
        P(None, None, "chan"),
        P(None, None, "chan"),
        P(None, None, "chan", None),
        P(None, None, "chan", None),
    )
    out_specs = (
        P("chan", "batch"),
        P("chan", "batch"),
        P(None, "chan", None, None),
        P(None, "chan", None, None),
        P(None, "chan", None, None),
        P(None, None, "chan"),
        P(None, None, "chan"),
        P(None, None, "chan"),
        P(None, None, "chan", None),
        P(None, None, "chan", None),
        P(None, None, "chan", None),
    )
    n_chan = mesh.shape["chan"]

    def run(*args):
        own_seqs = args[1].shape[0] // mesh.shape["batch"]
        fits = own_seqs % n_chan == 0 and args[3].shape[1] // n_chan % mesh.shape["batch"] == 0
        body = local if fits else wide_local
        return jax.shard_map(body, mesh=mesh, in_specs=in_specs, out_specs=out_specs, check_vma=False)(*args)

    return run
```

```python
import functools
import math

import jax
import jax.numpy as jnp
import numpy as np
from jax import lax
from jax.experimental import pallas as pl
from jax.experimental.pallas import tpu as pltpu
from jax.sharding import PartitionSpec as P

LAYERS = 2
BUCKET = 1024
STEP = 10


QUARTER = BUCKET // 4
HALF_ROOT = math.sqrt(0.5)
STEP_ROWS = 16
UNROLL = 4
CONV_ROWS = 512
CHUNK_ROWS = 256
MAT_ROWS = 512
LIN_ROWS = 256
ROOM = 59 * 2**20
GROUPS = ((0, 256), (256, 256), (512, 512), (1024, 512), (1536, 512))
GELU_A = math.sqrt(2.0 / math.pi)
GELU_B = GELU_A * 0.044715


def transform_tables():
    place = np.arange(QUARTER)[:, None]
    to_spec, to_time = [], []
    for residue in (0, 4):
        bins = np.arange(QUARTER // 2)[None, :]
        turn = (8 * bins + residue) * place % (2 * BUCKET) * (math.pi / BUCKET)
        cosine, sine = np.cos(turn), -np.sin(turn)
        weights = np.full_like(cosine, 2.0)
        if residue == 0:
            sine[:, 0] = 1 - 2 * (place[:, 0] % 2)
            weights[:, 0] = 1.0
        to_spec.append(np.concatenate([cosine, sine], 1))
        to_time.append(np.concatenate([cosine * weights, sine * weights], 1).T / (2 * BUCKET))
    for residue in (1, 2, 3):
        bins = np.arange(QUARTER)[None, :]
        turn = (8 * bins + residue) * place % (2 * BUCKET) * (math.pi / BUCKET)
        cosine, sine = np.cos(turn), np.sin(turn)
        sign = 1.0 if residue == 3 else -1.0
        to_spec.append(np.block([[cosine, -sine], [sign * sine, sign * cosine]]))
        to_time.append(np.block([[cosine.T, sine.T], [-sine.T, cosine.T]]) / BUCKET)
    small = [np.stack(side[:2]).astype(jnp.bfloat16) for side in (to_spec, to_time)]
    large = [np.stack(side[2:]).astype(jnp.bfloat16) for side in (to_spec, to_time)]
    return small[0], large[0], small[1], large[1]


def quarters(x):
    return [x[:, q * QUARTER : (q + 1) * QUARTER] for q in range(4)]


def fold(x0, x1, x2, x3):
    even, odd = x0 + x2, x1 + x3
    diff = x1 - x3
    turned, tilted = diff * HALF_ROOT, odd * HALF_ROOT
    return even + odd, even - odd, x0 + turned, x2 + tilted, x0 - x2, diff, x0 - turned, x2 - tilted


def unfold(y0, y4, r1, i1, r2, i2, r3, i3):
    even, odd = y0 + y4, y0 - y4
    r_sum, r_diff, i_sum, i_diff = r1 + r3, r1 - r3, i1 + i3, i1 - i3
    return (
        even + (r2 + r_sum),
        odd - i2 + (r_diff - i_sum) * HALF_ROOT,
        even - (r2 + i_diff),
        odd + i2 - (r_diff + i_sum) * HALF_ROOT,
    )


def dot(a, b):
    return jnp.dot(a, b, preferred_element_type=jnp.float32)


def product(a, b, first, conj):
    half = a.shape[1] // 2
    ar, ai, br, bi = a[:, :half], a[:, half:], b[:, :half], b[:, half:]
    cross = ai * bi
    if conj:
        imag = ar * bi - ai * br
    else:
        imag = ar * bi + ai * br
    if first:
        lone = lax.broadcasted_iota(jnp.int32, cross.shape, 1) == 0
        imag = jnp.where(lone, cross, imag)
        cross = jnp.where(lone, 0.0, cross)
    real = ar * br + cross if conj else ar * br - cross
    return jnp.concatenate([real, imag], 1)


def table_of(small, large, group):
    return small[group] if group < 2 else large[group - 2]


def put_folded(dest, rows, parts):
    lower = pl.ds(rows.start + dest.shape[0] // 2, rows.size)
    for k, part in enumerate(parts):
        dest[rows if k < 4 else lower, k % 4 * QUARTER : (k % 4 + 1) * QUARTER] = part.astype(dest.dtype)


def get_folded(src, rows, at, width):
    if at >= BUCKET:
        rows, at = pl.ds(rows.start + src.shape[0] // 2, rows.size), at - BUCKET
    return src[rows, at : at + width]


def get_unfolded(src, rows):
    return unfold(*[src[rows, k * QUARTER : (k + 1) * QUARTER] for k in range(8)])


def steps(total, size, body):
    def one(k, carry):
        body(pl.ds(pl.multiple_of(k * size, size), size), k)
        return carry

    lax.fori_loop(0, total // size, one, 0, unroll=UNROLL if size == STEP_ROWS else 1)


def kernel_spectrum(ker, folded, spec, small, large, chunk):
    chans = ker.shape[0]

    def fold_rows(rows, _):
        put_folded(folded, rows, fold(*quarters(ker[rows, :].astype(jnp.float32))))

    steps(chans, STEP_ROWS, fold_rows)

    def transform_rows(rows, _):
        for g, (at, width) in enumerate(GROUPS):
            spec[rows, at : at + width] = dot(get_folded(folded, rows, at, width), table_of(small, large, g))

    steps(chans, chunk, transform_rows)


def token_stats(stream, chans):
    def add(k, carry):
        v = stream[pl.ds(pl.multiple_of(k * STEP_ROWS, STEP_ROWS), STEP_ROWS), :].astype(jnp.float32)
        return carry + v[:8] + v[8:]

    total = lax.fori_loop(0, chans // STEP_ROWS, add, jnp.zeros((8, BUCKET), jnp.float32), unroll=UNROLL)
    mean_val = jnp.sum(total, 0, keepdims=True) / chans

    def add_square(k, carry):
        v = stream[pl.ds(pl.multiple_of(k * STEP_ROWS, STEP_ROWS), STEP_ROWS), :].astype(jnp.float32) - mean_val
        v = v * v
        return carry + v[:8] + v[8:]

    total = lax.fori_loop(0, chans // STEP_ROWS, add_square, jnp.zeros((8, BUCKET), jnp.float32), unroll=UNROLL)
    return mean_val, lax.rsqrt(jnp.sum(total, 0, keepdims=True) / chans + 1e-05)


def lanes(x):
    total = x[:, :128]
    for k in range(1, x.shape[1] // 128):
        total = total + x[:, k * 128 : (k + 1) * 128]
    return total


GAIN, SHIFT, SKIP, BIAS_IN, BIAS_VAL = range(5)
MESH = pl.DeviceIdType.MESH


def bit_of(index, place):
    return lax.rem(lax.div(index, 1 << place), 2)


def flip(index, place):
    return index + (1 - 2 * bit_of(index, place)) * (1 << place)


def peers_of(n_chan):
    me, row = lax.axis_index("chan"), lax.axis_index("batch")
    others = []
    for k in range(1, n_chan):
        other = me
        for place in range(n_chan.bit_length() - 1):
            other = flip(other, place) if k >> place & 1 else other
        others.append(other)
    return me, row, others


def greet(targets):
    barrier = pltpu.get_barrier_semaphore()
    for target in targets:
        pl.semaphore_signal(barrier, inc=1, device_id=target, device_id_type=MESH)
    pl.semaphore_wait(barrier, len(targets))


LANES = 128
POWERS = 8
LOW_STAGE = 1


def halving(n_chan, n_batch):
    me, row = lax.axis_index("chan"), lax.axis_index("batch")
    chan_bits, batch_bits = n_chan.bit_length() - 1, n_batch.bit_length() - 1
    out = [(bit_of(me, k), (row, flip(me, k))) for k in reversed(range(chan_bits))]
    return out + [(bit_of(row, k), (flip(row, k), me)) for k in reversed(range(batch_bits))]


def doubled_powers(decay_rate, turn_rate):
    spans = [2.0**k for k in range(BUCKET.bit_length() - 1)]
    sizes = [jnp.exp(-span * decay_rate) for span in spans]
    total, moment = jnp.ones_like(decay_rate), jnp.zeros_like(decay_rate)
    for span, size in zip(spans, sizes):
        moment = moment * (1.0 + size) + span * size * total
        total = total * (1.0 + size)
    powers = []
    for span, size in list(zip(spans, sizes))[:POWERS]:
        powers += [size * jnp.cos(span * turn_rate), size * jnp.sin(span * turn_rate)]
    return powers, total, moment


def times(a, b):
    return a[0] * b[0] - a[1] * b[1], a[0] * b[1] + a[1] * b[0]


def columns_of(rows):
    pad = jnp.zeros((LANES - rows.shape[0], LANES), jnp.float32)
    return jnp.transpose(jnp.concatenate([rows, pad], 0))


def near_powers(params):
    lane = lax.broadcasted_iota(jnp.int32, (params.shape[0], LANES), 1)
    value = None
    for k in range(POWERS - 1):
        power = params[:, 2 * k : 2 * k + 1], params[:, 2 * k + 1 : 2 * k + 2]
        here = (lane & (1 << k)) != 0
        if value is None:
            value = jnp.where(here, power[0], 1.0), jnp.where(here, power[1], 0.0)
        else:
            moved = times(value, power)
            value = jnp.where(here, moved[0], value[0]), jnp.where(here, moved[1], value[1])
    far = params[:, 2 * POWERS - 2 : 2 * POWERS - 1], params[:, 2 * POWERS - 1 : 2 * POWERS]
    return value, tuple(jnp.broadcast_to(f, lane.shape) for f in far)


def halves(x):
    half = x.shape[0] // 2
    return [jnp.sum(x[:half], 0, keepdims=True), jnp.sum(x[half:], 0, keepdims=True)]


def kernel_rows(params):
    value, far = near_powers(params)
    value = times(value, (params[:, 2 * POWERS : 2 * POWERS + 1], params[:, 2 * POWERS + 1 : 2 * POWERS + 2]))
    out = [halves(value[0])]
    for _ in range(1, BUCKET // LANES):
        value = times(value, far)
        out.append(halves(value[0]))
    return [jnp.concatenate([row[c] for row in out], 0) for c in range(2)]


def state_rows(params, grads):
    value, far = near_powers(params)
    half = params.shape[0] // 2
    place = lax.broadcasted_iota(jnp.int32, (1, LANES), 1).astype(jnp.float32)
    plain = weighted = None
    for k in reversed(range(BUCKET // LANES)):
        rows = [g[:, k * LANES : (k + 1) * LANES] for g in grads]
        g = jnp.concatenate([jnp.broadcast_to(r, (half, LANES)) for r in rows], 0)
        w = jnp.concatenate([jnp.broadcast_to(r * (place + float(k * LANES)), (half, LANES)) for r in rows], 0)
        if plain is None:
            plain, weighted = (g, jnp.zeros_like(g)), (w, jnp.zeros_like(g))
        else:
            plain, weighted = times(plain, far), times(weighted, far)
            plain, weighted = (plain[0] + g, plain[1]), (weighted[0] + w, weighted[1])
    cols = times(plain, value) + times(weighted, value)
    lane = lax.broadcasted_iota(jnp.int32, value[0].shape, 1)
    out = jnp.zeros_like(value[0])
    for k, col in enumerate(cols):
        out = jnp.where(lane == k, jnp.sum(col, 1, keepdims=True), out)
    return jnp.transpose(out)[:8]


def remote(src, dst, send, recv, target):
    return pltpu.make_async_remote_copy(
        src_ref=src, dst_ref=dst, send_sem=send, recv_sem=recv, device_id=target, device_id_type=MESH
    )


def halving_bits(n_chan, n_batch):
    return n_chan.bit_length() + n_batch.bit_length() - 2


def to_tokens(src, dst, send, recv, own_sem):
    own, toks = src.shape[0], dst.shape[1]
    n_chan = dst.shape[0] // own
    me, row, others = peers_of(n_chan)
    rows = pl.ds(pl.multiple_of(me * own, own), own)
    copies = [pltpu.make_async_copy(src.at[:, pl.ds(pl.multiple_of(me * toks, toks), toks)], dst.at[rows], own_sem)]
    for k, other in enumerate(others):
        copies.append(
            pltpu.make_async_remote_copy(
                src_ref=src.at[:, pl.ds(pl.multiple_of(other * toks, toks), toks)],
                dst_ref=dst.at[rows],
                send_sem=send.at[k],
                recv_sem=recv.at[k],
                device_id=(row, other),
                device_id_type=MESH,
            )
        )
    return copies


def to_channels(src, dst, send, recv, own_sem):
    own, toks = dst.shape[0], src.shape[1]
    n_chan = src.shape[0] // own
    me, row, others = peers_of(n_chan)
    cols = pl.ds(pl.multiple_of(me * toks, toks), toks)
    copies = [pltpu.make_async_copy(src.at[pl.ds(pl.multiple_of(me * own, own), own)], dst.at[:, cols], own_sem)]
    for k, other in enumerate(others):
        copies.append(
            pltpu.make_async_remote_copy(
                src_ref=src.at[pl.ds(pl.multiple_of(other * own, own), own)],
                dst_ref=dst.at[:, cols],
                send_sem=send.at[k],
                recv_sem=recv.at[k],
                device_id=(row, other),
                device_id_type=MESH,
            )
        )
    return copies


def forward_kernel(
    n_chan, first, mask, ker, weight, vec, fs, fl, ts, tl, cot_own,
    cot, delta_out, stat, hat_out, pre_out, act_out, sigma_out, slope_out, spec_out,
    stream, hat, ker_spec, folded, mixed, send, recv, own_sem,
):
    layer, seq = pl.program_id(0), pl.program_id(1)
    chans = first.shape[0]
    stream = stream.at[seq]

    @pl.when((layer == 0) & (seq == 0))
    def _():
        me, row, others = peers_of(n_chan)
        greet([(row, other) for other in others])
        for copy in to_tokens(cot_own, cot, send, recv, own_sem):
            copy.start()

    @pl.when(layer == 0)
    def _():
        def widen(rows, _):
            stream[rows, :] = first[rows, :].astype(jnp.float32)

        steps(chans, STEP_ROWS, widen)

    @pl.when(seq == 0)
    def _():
        kernel_spectrum(ker.at[0], folded, ker_spec, fs, fl, CONV_ROWS)

    mean_val, inv_std = token_stats(stream, chans)
    stat[0, 0, 0:1, :] = mean_val
    stat[0, 0, 1:2, :] = inv_std

    def normalise(rows, _):
        v = (stream[rows, :] - stat[0, 0, 0:1, :]) * stat[0, 0, 1:2, :]
        hat[rows, :] = v
        hat_out[0, rows, :] = v.astype(hat_out.dtype)
        v = v * vec[0, rows, GAIN : GAIN + 1] + vec[0, rows, SHIFT : SHIFT + 1]
        put_folded(folded, rows, fold(*quarters(v)))

    steps(chans, STEP_ROWS, normalise)

    def convolve(rows, _):
        for g, (at, width) in enumerate(GROUPS):
            spec = dot(get_folded(folded, rows, at, width), table_of(fs, fl, g))
            spec_out[0, rows, at : at + width] = spec.astype(jnp.bfloat16)
            both = product(ker_spec[rows, at : at + width], spec, g == 0, False)
            mixed[rows, at : at + width] = dot(both.astype(jnp.bfloat16), table_of(ts, tl, g))

    steps(chans, CONV_ROWS, convolve)

    def activate(rows, _):
        gain, shift, skip = [vec[0, rows, k : k + 1] for k in (GAIN, SHIFT, SKIP)]
        gain, shift = gain * skip, shift * skip
        for q, part in enumerate(get_unfolded(mixed, rows)):
            cols = slice(q * QUARTER, (q + 1) * QUARTER)
            pre = part + (gain * hat[rows, cols] + shift)
            pre_out[0, rows, cols] = pre.astype(pre_out.dtype)
            soft = jnp.tanh(pre * (GELU_A + GELU_B * (pre * pre)))
            act_out[0, rows, cols] = (0.5 * pre * (1.0 + soft)).astype(jnp.bfloat16)

    steps(chans, STEP_ROWS, activate)

    block = 2 * LIN_ROWS
    for t in range(4):
        cols = slice(t * QUARTER, (t + 1) * QUARTER)

        def linear(rows, k, cols=cols):
            mixed[:block, :QUARTER] = dot(weight[0, rows, :], act_out[0, :, cols])
            for o in range(LIN_ROWS // 16):
                at = pl.ds(pl.multiple_of(k * LIN_ROWS + o * 16, 16), 16)
                gate = mixed[o * 32 : o * 32 + 16, :QUARTER] + vec[0, at, BIAS_IN : BIAS_IN + 1]
                value = mixed[o * 32 + 16 : o * 32 + 32, :QUARTER] + vec[0, at, BIAS_VAL : BIAS_VAL + 1]
                sigma = 0.5 * jnp.tanh(0.5 * value) + 0.5
                gated = gate * sigma
                sigma_out[0, at, cols] = sigma.astype(sigma_out.dtype)
                slope_out[0, at, cols] = (gated - gated * sigma).astype(slope_out.dtype)
                moved = stream[at, cols] + mask[0, :, cols] * gated
                stream[at, cols] = moved
                delta_out[at, cols] = (moved - first[at, cols].astype(jnp.float32)).astype(jnp.bfloat16)

        steps(2 * chans, block, linear)

    @pl.when((layer == pl.num_programs(0) - 1) & (seq == pl.num_programs(1) - 1))
    def _():
        for copy in to_tokens(cot_own, cot, send, recv, own_sem):
            copy.wait()


def whole(a):
    return pl.BlockSpec(a.shape, lambda i, s, n=a.ndim: (0,) * n, pipeline_mode=pl.Buffered(1))


ANYWHERE = pl.BlockSpec(memory_space=pl.ANY)


def forward_pass(first, mask, kers, weights, vecs, tables, cot_own, n_chan):
    chans, toks = first.shape
    seqs, layers = toks // BUCKET, kers.shape[0]
    shape, low = jax.ShapeDtypeStruct, jnp.bfloat16
    layered = lambda a: pl.BlockSpec((1,) + a.shape[1:], lambda i, s: (i, 0, 0))
    saved = pl.BlockSpec((1, chans, BUCKET), lambda i, s: (i, 0, s))
    return pl.pallas_call(
        functools.partial(forward_kernel, n_chan),
        grid=(layers, seqs),
        in_specs=[
            pl.BlockSpec((chans, BUCKET), lambda i, s: (0, s)),
            pl.BlockSpec((1, 1, BUCKET), lambda i, s: (s, 0, 0)),
            layered(kers), layered(weights), layered(vecs),
            *[whole(t) for t in tables],
            ANYWHERE,
        ],
        out_specs=[
            ANYWHERE,
            pl.BlockSpec((chans, BUCKET), lambda i, s: (0, lax.select(i == layers - 1, s, 0))),
            pl.BlockSpec((1, 1, 8, BUCKET), lambda i, s: (i, s, 0, 0)),
            saved, saved, saved, saved, saved,
            pl.BlockSpec((1, chans, 2 * BUCKET), lambda i, s: (i, 0, s)),
        ],
        out_shape=[
            shape((chans, toks), low),
            shape((chans, toks), low),
            shape((layers, seqs, 8, BUCKET), jnp.float32),
            shape((layers, chans, toks), low),
            shape((layers, chans, toks), low),
            shape((layers, chans, toks), low),
            shape((layers, chans, toks), low),
            shape((layers, chans, toks), low),
            shape((layers, chans, 2 * toks), low),
        ],
        scratch_shapes=[
            pltpu.VMEM((seqs, chans, BUCKET), jnp.float32),
            pltpu.VMEM((chans, BUCKET), jnp.float32),
            pltpu.VMEM((chans, 2 * BUCKET), jnp.float32),
            pltpu.VMEM((2 * chans, BUCKET), low),
            pltpu.VMEM((chans, 2 * BUCKET), jnp.float32),
            pltpu.SemaphoreType.DMA((n_chan - 1,)),
            pltpu.SemaphoreType.DMA((n_chan - 1,)),
            pltpu.SemaphoreType.DMA,
        ],
        compiler_params=pltpu.CompilerParams(vmem_limit_bytes=ROOM, collective_id=2, has_side_effects=True),
        cost_estimate=pl.CostEstimate(flops=24 * 10**9, bytes_accessed=40 * 2**20, transcendentals=0),
        name="forward_pass",
    )(first, mask, kers, weights, vecs, *tables, cot_own)


def backward_kernel(
    n_chan, n_batch, first, mask, stat, hat, pre, act, sigma_in, slope_in, spec, ker, weight_t, vec, fs, fl, ts, tl, params,
    delta_own,
    delta, back_all, state_all, lin_all, vec_all,
    back, ker_spec, spec_grad, folded, mixed, sums, pre_grad, back_low, lin_grad, vec_grad, vec_cols, vec_rows, vec_got, vec_own,
    ker_kept, ker_sums, ker_sent, ker_got, lin_sums, lin_sent, lin_got, low_sent, low_got, ker_final, lin_final, state_own,
    send, recv, own_sem, back_send, back_recv, back_own, part_send, part_recv, ready, vec_send, vec_recv, vec_sem,
    all_send, all_recv, all_own,
):
    step, seq = pl.program_id(0), pl.program_id(1)
    layers, seqs = lin_grad.shape[0], back_low.shape[0]
    chans = first.shape[0]
    own = chans // n_chan
    everything = back
    back = back.at[seq]
    part = ker_final.shape[1]
    me, row, others = peers_of(n_chan)
    rows_of = [lax.rem(row + k, n_batch) for k in range(1, n_batch)]
    path = list(reversed(halving(n_chan, n_batch)))
    bits, batch_bits = len(path), n_batch.bit_length() - 1
    total = 1 << bits
    core_bit = path[0][0]
    moves = to_channels(delta_own, delta, send, recv, own_sem)

    def back_moves(k):
        cols = pl.ds(pl.multiple_of((me * seqs + k) * BUCKET, BUCKET), BUCKET)
        mine = back_low.at[k, pl.ds(pl.multiple_of(me * own, own), own)]
        copies = [pltpu.make_async_copy(mine, back_all.at[:, cols], back_own.at[k])]
        for j, other in enumerate(others):
            source = back_low.at[k, pl.ds(pl.multiple_of(other * own, own), own)]
            copies.append(remote(source, back_all.at[:, cols], back_send.at[k, j], back_recv.at[k, j], (row, other)))
        return copies

    groups = [[0], [1], [2, 3], [4]]
    count, at, gone = [], [0], 0
    for group in groups:
        gone += len(group)
        count.append(total >> gone)
        at.append(at[-1] + count[-1] * ((1 << len(group)) - 1))
    last_stage = len(groups) - 1

    def side(s, mask):
        chan, batch, index = me, row, 0
        for t, dim in enumerate(groups[s]):
            bit = path[dim][0]
            across = mask >> t & 1
            index = index + (1 - bit if across else bit) * (1 << t)
            if across and dim < batch_bits:
                batch = flip(batch, dim)
            elif across:
                chan = flip(chan, dim - batch_bits)
        return (batch, chan), index

    def masks(s):
        return range(1, 1 << len(groups[s]))

    def sums_at(s):
        return sum(count[1 : s + 1])

    def slot(kind, s, mask, sent):
        first = (mask - 1) * count[s]
        if kind == 0 or s == 0:
            return at[s] + first
        if s == LOW_STAGE:
            return first
        return first + at[s] - at[LOW_STAGE + 1] + (0 if sent else at[LOW_STAGE])

    def stage(kind, layer, s, mask):
        to, got = pl.ds(slot(kind, s, mask, True), count[s]), pl.ds(slot(kind, s, mask, False), count[s])
        if kind == 0:
            src, dst = ker_sent.at[to], ker_got.at[got]
        elif s == 0:
            src, dst = lin_grad.at[layer, :, 1 - core_bit], lin_got.at[got]
        elif s == LOW_STAGE:
            src, dst = low_sent.at[to], low_got.at[got]
        else:
            src, dst = lin_sent.at[to], lin_got.at[got]
        k = at_peer[s] + mask - 1
        return remote(src, dst, part_send.at[kind, k], part_recv.at[kind, k], side(s, mask)[0])

    at_peer = [0]
    for s in range(len(groups)):
        at_peer.append(at_peer[-1] + (1 << len(groups[s])) - 1)

    def begin(kind, layer, s):
        for mask in masks(s):
            if layer != layers - 1:
                pl.semaphore_wait(ready.at[kind, at_peer[s] + mask - 1], 1)
            stage(kind, layer, s, mask).start()

    def advance(kind, layer, s):
        for mask in masks(s):
            stage(kind, layer, s, mask).wait()

        def value(b):
            if kind == 0:
                result = ker_kept[b] if s == 0 else ker_sums[sums_at(s - 1) + b]
            else:
                result = lin_grad[layer, b, core_bit] if s == 0 else lin_sums[sums_at(s - 1) + b]
            for mask in masks(s):
                got = ker_got if kind == 0 else low_got if s == LOW_STAGE else lin_got
                result = result + got[slot(kind, s, mask, False) + b].astype(jnp.float32)
            return result

        if s == last_stage:
            final = ker_final if kind == 0 else lin_final
            final[layer] = value(0)
        else:
            wide = 1 << len(groups[s + 1])

            def one(b, carry):
                sums = ker_sums if kind == 0 else lin_sums
                sums[sums_at(s) + b] = value(wide * b + side(s + 1, 0)[1])
                for mask in masks(s + 1):
                    moved = value(wide * b + side(s + 1, mask)[1])
                    to = slot(kind, s + 1, mask, True) + b
                    if kind == 0:
                        ker_sent[to] = moved.astype(jnp.bfloat16)
                    elif s + 1 == LOW_STAGE:
                        low_sent[to] = moved.astype(jnp.bfloat16)
                    else:
                        lin_sent[to] = moved
                return carry

            lax.fori_loop(0, count[s + 1], one, 0)
        if layer == layers - 1:
            for mask in masks(s):
                there = side(s, mask)[0]
                pl.semaphore_signal(ready.at[kind, at_peer[s] + mask - 1], inc=1, device_id=there, device_id_type=MESH)
        if s < last_stage:
            begin(kind, layer, s + 1)

    def spread(own_ref, everyone, k):
        copies = [pltpu.make_async_copy(own_ref, everyone.at[row], all_own.at[k])]
        for j, other in enumerate(rows_of):
            copies.append(remote(own_ref, everyone.at[row], all_send.at[k, j], all_recv.at[k, j], (other, me)))
        return copies

    def spreads(kind, layer):
        if kind == 0:
            half = pl.ds(layer * part // 2, part // 2)
            return spread(state_own.at[half], state_all.at[:, half], layer)
        return spread(lin_final.at[layer], lin_all.at[:, layer], layers + layer)

    def vec_moves():
        copies = [pltpu.make_async_copy(vec_rows.at[me], vec_got.at[me], vec_sem)]
        for k, other in enumerate(others):
            copies.append(remote(vec_rows.at[other], vec_got.at[me], vec_send.at[k], vec_recv.at[k], (row, other)))
        return copies

    def run(copies):
        for copy in copies:
            copy.start()

    def states(layer):
        def one(h, carry):
            at = layer * part // 2 + h
            state_own[at] = state_rows(columns_of(params[at]), [ker_final[layer, pl.ds(2 * h + c, 1), :] for c in range(2)])
            return carry

        lax.fori_loop(0, part // 2, one, 0, unroll=4)

    begins = (step == 0) & (seq == 0)
    next_layer = (step == 1) & (seq == 0)
    ends = (step == layers - 1) & (seq == seqs - 1)
    top, bottom = layers - 1, 0

    @pl.when(begins)
    def _():
        greet([(row, other) for other in others] + [(other, me) for other in rows_of])
        run(moves)
        vec_cols[...] = jnp.zeros_like(vec_cols)

    @pl.when(step == 0)
    def _():
        def widen(rows, _):
            back[rows, :] = first[rows, :].astype(jnp.float32)

        steps(chans, STEP_ROWS, widen)

    @pl.when(seq == 0)
    def _():
        kernel_spectrum(ker.at[0], folded, ker_spec, fs, fl, CONV_ROWS)
        vec_grad[...] = jnp.zeros_like(vec_grad)
        spec_grad[...] = jnp.zeros_like(spec_grad)

    def gates(rows, k):
        gated = back[rows, :] * mask[0]
        left = (gated * sigma_in[0, rows, :].astype(jnp.float32)).astype(jnp.bfloat16)
        right = (gated * slope_in[0, rows, :].astype(jnp.float32)).astype(jnp.bfloat16)
        at = pl.multiple_of(k * 32, 32)
        folded[pl.ds(at, 16), :] = left
        folded[pl.ds(at + 16, 16), :] = right
        vec_grad[3, rows, :] += lanes(left.astype(jnp.float32))
        vec_grad[4, rows, :] += lanes(right.astype(jnp.float32))

    steps(chans, STEP_ROWS, gates)

    layer = layers - 1 - step
    width = 2 * chans // total
    blocks = MAT_ROWS // (2 * width)

    def lin_back(rows, k):
        value = lax.dot_general(
            folded[rows, :], act[0], (((1,), (1,)), ((), ())), preferred_element_type=jnp.float32
        ).reshape(blocks, 2, width, chans)
        at = pl.ds(k * blocks, blocks)

        @pl.when(seq == 0)
        def _():
            lin_grad[layer, at] = value

        @pl.when(seq > 0)
        def _():
            lin_grad[layer, at] += value

    steps(2 * chans, MAT_ROWS, lin_back)

    @pl.when(next_layer)
    def _():
        for kind in (0, 1):
            advance(kind, top, 0)

    @pl.when(ends)
    def _():
        begin(1, bottom, 0)

    def act_back(rows, _):
        for t in range(4):
            cols = slice(t * QUARTER, (t + 1) * QUARTER)
            pre_grad[rows, cols] = dot(weight_t[0, rows, :], folded[:, cols])

    steps(chans, MAT_ROWS, act_back)

    def gelu_back(rows, _):
        skip_sum = jnp.zeros((STEP_ROWS, 128), jnp.float32)
        outs = []
        for q in range(4):
            cols = slice(q * QUARTER, (q + 1) * QUARTER)
            p = pre[0, rows, cols].astype(jnp.float32)
            square = p * p
            soft = jnp.tanh(p * (GELU_A + GELU_B * square))
            slope = 0.5 * (1.0 + soft) + (0.5 * p) * (1.0 - soft * soft) * (GELU_A + (3.0 * GELU_B) * square)
            grad = pre_grad[rows, cols] * slope
            pre_grad[rows, cols] = grad
            norm = hat[0, rows, cols].astype(jnp.float32) * vec[0, rows, GAIN : GAIN + 1] + vec[0, rows, SHIFT : SHIFT + 1]
            skip_sum = skip_sum + lanes(grad * norm)
            outs.append(grad)
        vec_grad[2, rows, :] += skip_sum
        put_folded(folded, rows, fold(*outs))

    steps(chans, STEP_ROWS, gelu_back)

    @pl.when(ends)
    def _():
        for kind in (0, 1):
            advance(kind, top, 2)
        advance(1, bottom, 0)

    sums[...] = jnp.zeros_like(sums)

    def correlate(rows, chunk):
        for g, (at, width) in enumerate(GROUPS):
            grad = dot(get_folded(folded, rows, at, width), table_of(fs, fl, g))
            spec_grad[rows, at : at + width] += product(
                spec[0, rows, at : at + width].astype(jnp.float32), grad, g == 0, True
            )
            both = product(ker_spec[rows, at : at + width], grad, g == 0, True)
            mixed[:, at : at + width] = dot(both.astype(jnp.bfloat16), table_of(ts, tl, g))

        def norm_back(k, carry):
            here = pl.ds(pl.multiple_of(k * STEP_ROWS, STEP_ROWS), STEP_ROWS)
            rows = pl.ds(pl.multiple_of(chunk * CHUNK_ROWS + k * STEP_ROWS, STEP_ROWS), STEP_ROWS)
            skip = vec[0, rows, SKIP : SKIP + 1]
            gain = vec[0, rows, GAIN : GAIN + 1]
            gain_sum = jnp.zeros((STEP_ROWS, 128), jnp.float32)
            shift_sum = jnp.zeros((STEP_ROWS, 128), jnp.float32)
            plain, weighted = [], []
            for q, part in enumerate(get_unfolded(mixed, here)):
                cols = slice(q * QUARTER, (q + 1) * QUARTER)
                grad = part + skip * pre_grad[rows, cols]
                both = grad * hat[0, rows, cols].astype(jnp.float32)
                gain_sum = gain_sum + lanes(both)
                shift_sum = shift_sum + lanes(grad)
                cent = grad * gain
                pre_grad[rows, cols] = cent
                both = both * gain
                plain.append(cent[:8] + cent[8:])
                weighted.append(both[:8] + both[8:])
            vec_grad[0, rows, :] += gain_sum
            vec_grad[1, rows, :] += shift_sum
            return carry[0] + jnp.concatenate(plain, 1), carry[1] + jnp.concatenate(weighted, 1)

        zero = jnp.zeros((8, BUCKET), jnp.float32)
        plain, weighted = lax.fori_loop(0, CHUNK_ROWS // STEP_ROWS, norm_back, (zero, zero), unroll=2)
        sums[0:8, :] += plain
        sums[8:16, :] += weighted

    steps(chans, CHUNK_ROWS, correlate)

    @pl.when(seq == seqs - 1)
    def _():
        def to_time(rows, _):
            for g, (at, width) in enumerate(GROUPS):
                low = spec_grad[rows, at : at + width].astype(jnp.bfloat16)
                ker_spec[rows, at : at + width] = dot(low, table_of(ts, tl, g))

        steps(chans, CONV_ROWS, to_time)

        def block_rows(b):
            return pl.ds(pl.multiple_of(b * part, part), part)

        def write(b, carry):
            for q, value in enumerate(get_unfolded(ker_spec, block_rows(2 * b + core_bit))):
                ker_kept[b, :, q * QUARTER : (q + 1) * QUARTER] = value
            for q, value in enumerate(get_unfolded(ker_spec, block_rows(2 * b + 1 - core_bit))):
                ker_sent[b, :, q * QUARTER : (q + 1) * QUARTER] = value.astype(jnp.bfloat16)
            return carry

        lax.fori_loop(0, total // 2, write, 0)

    for i in range(layers):

        @pl.when((step == i) & (seq == seqs - 1))
        def _(i=i):
            layer = layers - 1 - i
            begin(0, layer, 0)
            if layer == layers - 1:
                begin(1, layer, 0)
            else:
                advance(1, layer, 1)

    mean_plain = jnp.sum(sums[0:8, :], 0, keepdims=True) / chans
    mean_weighted = jnp.sum(sums[8:16, :], 0, keepdims=True) / chans
    sums[0:1, :] = mean_plain
    sums[8:9, :] = mean_weighted

    @pl.when(next_layer)
    def _():
        for kind in (0, 1):
            advance(kind, top, 1)

    def finish(rows, _):
        scaled = hat[0, rows, :].astype(jnp.float32) * sums[8:9, :]
        moved = back[rows, :] + stat[0, 0, 1:2, :] * (pre_grad[rows, :] - sums[0:1, :] - scaled)
        back[rows, :] = moved
        back_low[seq, rows, :] = (moved - first[rows, :].astype(jnp.float32)).astype(jnp.bfloat16)

    steps(chans, STEP_ROWS, finish)

    for k in range(seqs):

        @pl.when((step == layers - 1) & (seq == k))
        def _(k=k):
            run(back_moves(k))

    @pl.when(ends)
    def _():
        for kind in (0, 1):
            advance(kind, top, 3)

    for i in range(layers):

        @pl.when((step == i) & (seq == seqs - 1))
        def _(i=i):
            layer = layers - 1 - i

            def columns(rows, _):
                lane = lax.broadcasted_iota(jnp.int32, (STEP_ROWS, LANES), 1)
                out = vec_cols[rows, :]
                for kind in range(5):
                    out = jnp.where(lane == layer * 5 + kind, jnp.sum(vec_grad[kind, rows, :], 1, keepdims=True), out)
                vec_cols[rows, :] = out

            steps(chans, STEP_ROWS, columns)

    @pl.when(ends)
    def _():
        for c in range(n_chan):
            vec_rows[c] = columns_of(vec_cols[c * own : (c + 1) * own, :])[:16]
        run(vec_moves())
        states(top)
        run(spreads(0, top) + spreads(1, top))
        for s in range(last_stage + 1):
            advance(0, bottom, s)
            if s + 2 <= last_stage:
                advance(1, bottom, s + 2)
                if s + 2 == last_stage:
                    run(spreads(1, bottom))
            if s == 1:
                for copy in vec_moves():
                    copy.wait()
                vec_own[...] = jnp.sum(vec_got[...], 0)
                run(spread(vec_own, vec_all, 2 * layers))
        states(bottom)
        run(spreads(0, bottom))
        for copy in moves:
            copy.wait()
        for k in range(seqs):
            for copy in back_moves(k):
                copy.wait()
        for i in range(layers):
            for copy in spreads(0, i) + spreads(1, i):
                copy.wait()
        for copy in spread(vec_own, vec_all, 2 * layers):
            copy.wait()


def backward_pass(cot, mask, saved, kers, weights_t, vecs, tables, params, delta_own, n_chan, n_batch):
    chans, toks = cot.shape
    seqs, layers = toks // BUCKET, kers.shape[0]
    own, group = chans // n_chan, toks * n_chan
    bits = halving_bits(n_chan, n_batch)
    total = 1 << bits
    part = chans // total
    low_count, peers = total >> (LOW_STAGE + 1), bits + 1
    shape, low, full = jax.ShapeDtypeStruct, jnp.bfloat16, jnp.float32
    top = layers - 1
    layered = lambda a: pl.BlockSpec((1,) + a.shape[1:], lambda i, s: (top - i, 0, 0), pipeline_mode=pl.Buffered(1))
    block = pl.BlockSpec((1, chans, BUCKET), lambda i, s: (top - i, 0, s))
    vmem, dma = pltpu.VMEM, pltpu.SemaphoreType.DMA
    return pl.pallas_call(
        functools.partial(backward_kernel, n_chan, n_batch),
        grid=(layers, seqs),
        in_specs=[
            pl.BlockSpec((chans, BUCKET), lambda i, s: (0, s)),
            pl.BlockSpec((1, 1, BUCKET), lambda i, s: (s, 0, 0)),
            pl.BlockSpec((1, 1, 8, BUCKET), lambda i, s: (top - i, s, 0, 0)),
            block, block, block, block, block,
            pl.BlockSpec((1, chans, 2 * BUCKET), lambda i, s: (top - i, 0, s)),
            layered(kers), layered(weights_t), layered(vecs),
            *[whole(t) for t in tables],
            whole(params),
            ANYWHERE,
        ],
        out_specs=[ANYWHERE] * 5,
        out_shape=[
            shape((own, group), low),
            shape((own, group), low),
            shape((n_batch, layers * part // 2, 8, LANES), full),
            shape((n_batch, layers, 2 * part, chans), full),
            shape((n_batch, 16, LANES), full),
        ],
        scratch_shapes=[
            vmem((seqs, chans, BUCKET), full),
            vmem((chans, 2 * BUCKET), full),
            vmem((chans, 2 * BUCKET), full),
            vmem((2 * chans, BUCKET), low),
            vmem((CHUNK_ROWS, 2 * BUCKET), full),
            vmem((16, BUCKET), full),
            vmem((chans, BUCKET), full),
            vmem((seqs, chans, BUCKET), low),
            vmem((layers, total // 2, 2, 2 * part, chans), full),
            vmem((5, chans, LANES), full),
            vmem((chans, LANES), full),
            vmem((n_chan, 16, LANES), full),
            vmem((n_chan, 16, LANES), full),
            vmem((16, LANES), full),
            vmem((total // 2, part, BUCKET), full),
            vmem((total // 2, part, BUCKET), full),
            vmem((total, part, BUCKET), low),
            vmem((total, part, BUCKET), low),
            vmem((total // 2, 2 * part, chans), full),
            vmem((low_count, 2 * part, chans), full),
            vmem((total - low_count, 2 * part, chans), full),
            vmem((low_count, 2 * part, chans), low),
            vmem((low_count, 2 * part, chans), low),
            vmem((layers, part, BUCKET), full),
            vmem((layers, 2 * part, chans), full),
            vmem((layers * part // 2, 8, LANES), full),
            dma((n_chan - 1,)), dma((n_chan - 1,)), dma,
            dma((seqs, n_chan - 1)), dma((seqs, n_chan - 1)), dma((seqs,)),
            dma((2, peers)), dma((2, peers)), pltpu.SemaphoreType.REGULAR((2, peers)),
            dma((n_chan - 1,)), dma((n_chan - 1,)), dma,
            dma((2 * layers + 1, n_batch - 1)), dma((2 * layers + 1, n_batch - 1)), dma((2 * layers + 1,)),
        ],
        compiler_params=pltpu.CompilerParams(vmem_limit_bytes=ROOM, collective_id=3, has_side_effects=True),
        cost_estimate=pl.CostEstimate(flops=40 * 10**9, bytes_accessed=60 * 2**20, transcendentals=0),
        name="backward_pass",
    )(cot, mask, *saved, kers, weights_t, vecs, *tables, params, delta_own)


def gather_kernel(
    n_chan, n_batch, params, x_own, w_own, vec_own,
    x_all, ker_all, w_all, vec_all,
    ker_rows, ker_low, send, recv, own_sem, vec_send, vec_recv, own_sems, part_send, part_recv,
):
    layers, part = ker_low.shape[:2]
    path = halving(n_chan, n_batch)
    bits = len(path)
    me, row, others = peers_of(n_chan)
    greet([(row, other) for other in others] + [target for _, target in path if True][n_chan.bit_length() - 1 :])
    place = tuple(bit for bit, _ in path)
    own = [pltpu.make_async_copy(w_own.at[i], w_all.at[(i,) + place], own_sems.at[i]) for i in range(layers)]
    for copy in own:
        copy.start()
    vec_copies = [pltpu.make_async_copy(vec_own, vec_all.at[me], own_sems.at[2 * layers])]
    for k, other in enumerate(others):
        vec_copies.append(remote(vec_own, vec_all.at[me], vec_send.at[k], vec_recv.at[k], (row, other)))
    for copy in vec_copies:
        copy.start()

    orders = [(0, 1, 3, 2, 4)] * layers + [(0, 1, 2, 3, 4)] * layers

    def stage(p, s):
        ref = w_all.at[p] if p < layers else ker_all.at[p - layers]
        done, dim = orders[p][:s], orders[p][s]
        at = ref.at[tuple(slice(None) if d in done else place[d] for d in range(bits))]
        return remote(at, at, part_send.at[p, s], part_recv.at[p, s], path[dim][1])

    moves = to_tokens(x_own, x_all, send, recv, own_sem)
    plan = [[0], [4], [5, 6], [7, 2], [1, 3], [], []]

    def issue(k):
        for m in plan[k]:
            moves[m].start()

    for copy in own:
        copy.wait()
    for p in range(layers):
        stage(p, 0).start()
    issue(0)

    def make(h, carry):
        first_row, second_row = kernel_rows(columns_of(params[h]))
        ker_rows[2 * h] = first_row
        ker_rows[2 * h + 1] = second_row
        return carry

    lax.fori_loop(0, layers * part // 2, make, 0, unroll=4)
    for i in range(layers):
        for k in range(BUCKET // LANES):
            value = ker_rows[i * part : (i + 1) * part, k, :]
            ker_low[i, :, k * LANES : (k + 1) * LANES] = value.astype(jnp.bfloat16)
    own = [pltpu.make_async_copy(ker_low.at[i], ker_all.at[(i,) + place], own_sems.at[layers + i]) for i in range(layers)]
    for copy in own:
        copy.start()
    for copy in own:
        copy.wait()
    for p in range(layers, 2 * layers):
        stage(p, 0).start()
    issue(1)
    for s in range(1, bits + 1):
        for p in range(2 * layers):
            stage(p, s - 1).wait()
            if s < bits:
                stage(p, s).start()
        issue(s + 1)
    for copy in vec_copies + moves:
        copy.wait()


def gather_params(params, x_own, w_own, vec_own, n_chan, n_batch):
    own, group = x_own.shape
    chans, toks = own * n_chan, group // n_chan
    layers, wide, _ = w_own.shape
    part = wide // 2
    bits = halving_bits(n_chan, n_batch)
    shape, low = jax.ShapeDtypeStruct, jnp.bfloat16
    vmem = pl.BlockSpec(memory_space=pltpu.VMEM)
    return pl.pallas_call(
        functools.partial(gather_kernel, n_chan, n_batch),
        in_specs=[vmem, ANYWHERE, ANYWHERE, vmem],
        out_specs=[ANYWHERE, ANYWHERE, ANYWHERE, vmem],
        out_shape=[
            shape((chans, toks), low),
            shape((layers,) + (2,) * bits + (part, BUCKET), low),
            shape((layers,) + (2,) * bits + (wide, chans), low),
            shape((n_chan,) + vec_own.shape, jnp.float32),
        ],
        scratch_shapes=[
            pltpu.VMEM((layers * part, BUCKET // LANES, LANES), jnp.float32),
            pltpu.VMEM((layers, part, BUCKET), low),
            pltpu.SemaphoreType.DMA((n_chan - 1,)),
            pltpu.SemaphoreType.DMA((n_chan - 1,)),
            pltpu.SemaphoreType.DMA,
            pltpu.SemaphoreType.DMA((n_chan - 1,)),
            pltpu.SemaphoreType.DMA((n_chan - 1,)),
            pltpu.SemaphoreType.DMA((2 * layers + 1,)),
            pltpu.SemaphoreType.DMA((2 * layers, bits)),
            pltpu.SemaphoreType.DMA((2 * layers, bits)),
        ],
        compiler_params=pltpu.CompilerParams(vmem_limit_bytes=ROOM, collective_id=1, has_side_effects=True),
        cost_estimate=pl.CostEstimate(flops=10**8, bytes_accessed=10 * 2**20, transcendentals=0),
        name="gather_params",
    )(params, x_own, w_own, vec_own)


def adam(weight, grad, first, second, rate):
    first_new = 0.9 * first + 0.1 * grad
    second_new = 0.999 * second + 0.001 * grad * grad
    fixed_first = first_new / (1.0 - 0.9**STEP)
    fixed_second = second_new / (1.0 - 0.999**STEP)
    new_weight = weight - rate * (fixed_first / (jnp.sqrt(fixed_second) + 1e-08) + 0.01 * weight)
    return (first_new, second_new, new_weight)


def local(
    inputs, lengths, cotangent, ln_gain, ln_bias, log_step, skip_gain, lin_bias, log_decay, frequency,
    w_re, w_im, lin_weight, lin_moment, lin_square, vec_moment, vec_square, state_moment, state_square,
):
    n_chan = lax.axis_size("chan")
    n_batch = lax.axis_size("batch")
    own = inputs.shape[0]
    chans = own * n_chan
    toks = inputs.shape[1] // n_chan
    seqs = toks // BUCKET
    part = own // n_batch
    me = lax.axis_index("chan")
    row = lax.axis_index("batch")
    lens = lax.dynamic_slice_in_dim(lengths, me * seqs, seqs)
    places = lax.iota(jnp.int32, BUCKET)
    valid = (places[None, :] < lens[:, None]).astype(jnp.float32).reshape(seqs, 1, BUCKET)
    tables = tuple(jnp.asarray(t) for t in transform_tables())

    def mine(a):
        return lax.dynamic_slice_in_dim(a, row * part, part, 1)

    step_size = jnp.exp(log_step)[..., None]
    decay_rate = step_size * jnp.exp(log_decay)
    turn_rate = step_size * frequency
    powers, total, moment = doubled_powers(decay_rate, turn_rate)
    params = jnp.stack([mine(a).reshape(LAYERS * part // 2, -1) for a in powers + [w_re / total, w_im / total]], 1)
    params = jnp.pad(params, ((0, 0), (0, -params.shape[1] % 8), (0, 0)))
    w_own = mine(lin_weight).transpose(0, 2, 1, 3).reshape(LAYERS, 2 * part, chans).astype(jnp.bfloat16)
    vec_own = jnp.stack([ln_gain, ln_bias, skip_gain, lin_bias[:, 0], lin_bias[:, 1]], 1).reshape(5 * LAYERS, own)
    vec_own = jnp.pad(vec_own, ((0, 16 - 5 * LAYERS), (0, LANES - own)))
    first, kers, weights, vec_all = gather_params(params, inputs, w_own, vec_own, n_chan, n_batch)
    kers = kers.reshape(LAYERS, chans, BUCKET)
    weights = weights.reshape(LAYERS, 2 * chans, chans)
    vecs = vec_all[:, : 5 * LAYERS, :own].reshape(n_chan, LAYERS, 5, own).transpose(1, 0, 3, 2).reshape(LAYERS, chans, 5)

    cot, out_delta, *saved = forward_pass(first, valid, kers, weights, vecs, tables, cotangent, n_chan)
    out_delta, in_delta, state_all, lin_all, vec_all = backward_pass(
        cot, valid, saved, kers, weights.transpose(0, 2, 1), vecs, tables, params, out_delta, n_chan, n_batch
    )
    output = inputs.astype(jnp.float32) + out_delta.astype(jnp.float32)
    input_grad = cotangent.astype(jnp.float32) + in_delta.astype(jnp.float32)

    state_all = state_all.reshape(n_batch, LAYERS, part // 2, 8, 2, LANES // 2)
    state_all = state_all.transpose(3, 1, 0, 2, 4, 5).reshape(8, LAYERS, own, -1) / total
    c_re, c_im, d_re, d_im = [state_all[k] for k in range(4)]
    turn_grad = -(w_re * d_im + w_im * d_re)
    decay_grad = ((w_re * c_re - w_im * c_im) * (moment / total) - (w_re * d_re - w_im * d_im)) * decay_rate
    state_total = jnp.stack([decay_grad, turn_grad * step_size, c_re, -c_im], 1)
    step_total = jnp.sum(decay_grad + turn_grad * turn_rate, -1)
    lin_total = lin_all.reshape(n_batch, LAYERS, 2, part, chans).transpose(1, 0, 3, 2, 4).reshape(LAYERS, own, 2, chans)
    vec_sum = jnp.sum(vec_all, 0)[: 5 * LAYERS, :own].reshape(LAYERS, 5, own)
    vec_total = jnp.stack([vec_sum[:, 0], vec_sum[:, 1], step_total, vec_sum[:, 2], vec_sum[:, 3], vec_sum[:, 4]], 1)

    vec_old = jnp.stack([ln_gain, ln_bias, log_step, skip_gain, lin_bias[:, 0], lin_bias[:, 1]], 1)
    state_old = jnp.stack([log_decay, frequency, w_re, w_im], 1)
    lin_first, lin_second, lin_new = adam(lin_weight, lin_total, lin_moment, lin_square, 0.05)
    vec_first, vec_second, vec_new = adam(vec_old, vec_total, vec_moment, vec_square, 0.2)
    state_first, state_second, state_new = adam(state_old, state_total, state_moment, state_square, 0.2)
    return (
        output, input_grad, lin_first, lin_second, lin_new, vec_first, vec_second, vec_new,
        state_first, state_second, state_new,
    )


def tables(length):
    full_width = 2 * length
    row_ids = lax.iota(jnp.int32, length)[:, None]
    col_ids = lax.iota(jnp.int32, length)[None, :]
    turn_all = (row_ids * col_ids % full_width).astype(jnp.float32) * (2.0 * math.pi / full_width)
    cosine = jnp.cos(turn_all)
    sine_table = jnp.sin(turn_all)
    weights = jnp.where(lax.iota(jnp.int32, length) == 0, 1.0, 2.0).astype(jnp.float32)[None, :]
    alternate = (1 - 2 * (lax.iota(jnp.int32, length) % 2)).astype(jnp.float32)
    return (cosine, sine_table, cosine * weights, sine_table * weights, alternate)


def mixer(normed, log_decay, frequency, w_re, w_im, log_step, skip_gain):
    top_prec = lax.Precision.HIGHEST
    chan_count = normed.shape[0]
    seq_count = normed.shape[1] // BUCKET
    step_size = jnp.exp(log_step)[:, None]
    decay_rate = step_size * jnp.exp(log_decay)
    turn_rate = step_size * frequency
    places = lax.iota(jnp.float32, BUCKET)
    decay_all = jnp.exp(-decay_rate[..., None] * places)
    soft = decay_all / jnp.sum(decay_all, -1, keepdims=True)
    phase_all = turn_rate[..., None] * places
    kernel = jnp.sum(
        (w_re[..., None] * jnp.cos(phase_all) - w_im[..., None] * jnp.sin(phase_all)) * soft, 1
    )
    cosine, sine_table, cos_back, sin_back, alternate = tables(BUCKET)
    signal = normed.reshape(chan_count, seq_count, BUCKET)
    sig_re = jnp.einsum("csl,lk->csk", signal, cosine, precision=top_prec)
    sig_im = -jnp.einsum("csl,lk->csk", signal, sine_table, precision=top_prec)
    sig_top = jnp.sum(signal * alternate, -1)
    ker_re = jnp.dot(kernel, cosine, precision=top_prec)[:, None, :]
    ker_im = -jnp.dot(kernel, sine_table, precision=top_prec)[:, None, :]
    ker_top = jnp.sum(kernel * alternate, -1)[:, None]
    prod_re = sig_re * ker_re - sig_im * ker_im
    prod_im = sig_re * ker_im + sig_im * ker_re
    prod_top = sig_top * ker_top
    conv_out = jnp.einsum("csk,lk->csl", prod_re, cos_back, precision=top_prec)
    conv_out = conv_out - jnp.einsum("csk,lk->csl", prod_im, sin_back, precision=top_prec)
    conv_out = conv_out + prod_top[..., None] * alternate
    conv_out = conv_out / (2.0 * BUCKET)
    pre_act = conv_out.reshape(normed.shape) + skip_gain[:, None] * normed
    return jax.nn.gelu(pre_act)


def wide_local(
    inputs,
    lengths,
    cotangent,
    ln_gain,
    ln_bias,
    log_step,
    skip_gain,
    lin_bias,
    log_decay,
    frequency,
    w_re,
    w_im,
    lin_weight,
    lin_moment,
    lin_square,
    vec_moment,
    vec_square,
    state_moment,
    state_square,
):
    chan_total = inputs.shape[0] * lax.axis_size("chan")
    tok_count = inputs.shape[1]
    places = lax.iota(jnp.int32, BUCKET)
    valid = (places[None, :] < lengths[:, None]).astype(jnp.float32).reshape(1, tok_count)
    weights_low = lin_weight.astype(jnp.bfloat16)
    stream = inputs.astype(jnp.float32)
    saved = []
    for layer_idx in range(LAYERS):
        sums = lax.psum((jnp.sum(stream, 0), jnp.sum(stream * stream, 0)), "chan")
        mean_val = sums[0] / chan_total
        variance = sums[1] / chan_total - mean_val * mean_val
        inv_std = lax.rsqrt(variance + 1e-05)[None, :]
        centred = (stream - mean_val[None, :]) * inv_std
        normed = centred * ln_gain[layer_idx][:, None] + ln_bias[layer_idx][:, None]
        activated, mixer_back = jax.vjp(
            mixer,
            normed,
            log_decay[layer_idx],
            frequency[layer_idx],
            w_re[layer_idx],
            w_im[layer_idx],
            log_step[layer_idx],
            skip_gain[layer_idx],
        )
        act_low = activated.astype(jnp.bfloat16)
        act_all = lax.all_gather(act_low, "chan", axis=0, tiled=True)
        mixed = jnp.einsum(
            "ht,cjh->cjt", act_all, weights_low[layer_idx], preferred_element_type=jnp.float32
        )
        kept = act_all
        mixed = mixed + lin_bias[layer_idx].T[:, :, None]
        gate_in = mixed[:, 0]
        gate_val = mixed[:, 1]
        stream = stream + valid * gate_in * jax.nn.sigmoid(gate_val)
        saved.append((centred, inv_std, mixer_back, kept, gate_in, gate_val))
    back_stream = cotangent.astype(jnp.float32)
    lin_grads = [None] * LAYERS
    vec_grads = [None] * LAYERS
    state_grads = [None] * LAYERS
    for layer_idx in reversed(range(LAYERS)):
        centred, inv_std, mixer_back, kept, gate_in, gate_val = saved[layer_idx]
        sigma = jax.nn.sigmoid(gate_val)
        gated_back = back_stream * valid
        grad_mixed = jnp.stack(
            [gated_back * sigma, gated_back * gate_in * sigma * (1.0 - sigma)], 1
        ).astype(jnp.bfloat16)
        bias_grad = jnp.sum(grad_mixed.astype(jnp.float32), 2).T
        weight_grad = jnp.einsum(
            "ht,cjt->cjh", kept, grad_mixed, preferred_element_type=jnp.float32
        )
        act_part = jnp.einsum(
            "cjt,cjh->ht", grad_mixed, weights_low[layer_idx], preferred_element_type=jnp.float32
        )
        act_grad = lax.psum_scatter(act_part, "chan", scatter_dimension=0, tiled=True)
        normed_grad, decay_grad, freq_grad, re_grad, im_grad, step_grad, skip_grad = mixer_back(
            act_grad
        )
        gain_grad = jnp.sum(normed_grad * centred, 1)
        shift_grad = jnp.sum(normed_grad, 1)
        centred_grad = normed_grad * ln_gain[layer_idx][:, None]
        back_sums = lax.psum((jnp.sum(centred_grad, 0), jnp.sum(centred_grad * centred, 0)), "chan")
        back_stream = back_stream + inv_std * (
            centred_grad
            - back_sums[0][None, :] / chan_total
            - centred * back_sums[1][None, :] / chan_total
        )
        lin_grads[layer_idx] = weight_grad
        vec_grads[layer_idx] = jnp.stack(
            [gain_grad, shift_grad, step_grad, skip_grad, bias_grad[0], bias_grad[1]]
        )
        state_grads[layer_idx] = jnp.stack([decay_grad, freq_grad, re_grad, im_grad])
    lin_total, vec_total, state_total = lax.psum(
        (jnp.stack(lin_grads), jnp.stack(vec_grads), jnp.stack(state_grads)), "batch"
    )
    vec_old = jnp.stack([ln_gain, ln_bias, log_step, skip_gain, lin_bias[:, 0], lin_bias[:, 1]], 1)
    state_old = jnp.stack([log_decay, frequency, w_re, w_im], 1)
    lin_first, lin_second, lin_new = adam(lin_weight, lin_total, lin_moment, lin_square, 0.05)
    vec_first, vec_second, vec_new = adam(vec_old, vec_total, vec_moment, vec_square, 0.2)
    state_first, state_second, state_new = adam(
        state_old, state_total, state_moment, state_square, 0.2
    )
    return (
        stream,
        back_stream,
        lin_first,
        lin_second,
        lin_new,
        vec_first,
        vec_second,
        vec_new,
        state_first,
        state_second,
        state_new,
    )


def suits(own_seqs, chans, n_chan, n_batch):
    powers = n_chan & (n_chan - 1) == 0 and n_batch & (n_batch - 1) == 0
    return powers and own_seqs % n_chan == 0 and own_seqs > n_chan and chans == 16 * n_chan * n_batch


def solution(mesh):
    in_specs = (
        P("chan", "batch"),
        P("batch"),
        P("chan", "batch"),
        P(None, "chan"),
        P(None, "chan"),
        P(None, "chan"),
        P(None, "chan"),
        P(None, None, "chan"),
        P(None, "chan", None),
        P(None, "chan", None),
        P(None, "chan", None),
        P(None, "chan", None),
        P(None, "chan", None, None),
        P(None, "chan", None, None),
        P(None, "chan", None, None),
        P(None, None, "chan"),
        P(None, None, "chan"),
        P(None, None, "chan", None),
        P(None, None, "chan", None),
    )
    out_specs = (
        P("chan", "batch"),
        P("chan", "batch"),
        P(None, "chan", None, None),
        P(None, "chan", None, None),
        P(None, "chan", None, None),
        P(None, None, "chan"),
        P(None, None, "chan"),
        P(None, None, "chan"),
        P(None, None, "chan", None),
        P(None, None, "chan", None),
        P(None, None, "chan", None),
    )
    n_chan = mesh.shape["chan"]

    def run(*args):
        own_seqs = args[1].shape[0] // mesh.shape["batch"]
        fits = suits(own_seqs, args[3].shape[1], n_chan, mesh.shape["batch"])
        body = local if fits else wide_local
        return jax.shard_map(body, mesh=mesh, in_specs=in_specs, out_specs=out_specs, check_vma=False)(*args)

    return run
```

```python
import functools
import math

import jax
import jax.numpy as jnp
import numpy as np
from jax import lax
from jax.experimental import pallas as pl
from jax.experimental.pallas import tpu as pltpu
from jax.sharding import PartitionSpec as P

LAYERS = 2
BUCKET = 1024
STEP = 10


QUARTER = BUCKET // 4
HALF_ROOT = math.sqrt(0.5)
STEP_ROWS = 16
UNROLL = 4
CONV_ROWS = 256
CHUNK_ROWS = 256
MAT_ROWS = 256
LIN_ROWS = 256
ROOM = 59 * 2**20
GROUPS = ((0, 256), (256, 256), (512, 512), (1024, 512), (1536, 512))
GELU_A = math.sqrt(2.0 / math.pi)
GELU_B = GELU_A * 0.044715


def transform_tables():
    place = np.arange(QUARTER)[:, None]
    to_spec, to_time = [], []
    for residue in (0, 4):
        bins = np.arange(QUARTER // 2)[None, :]
        turn = (8 * bins + residue) * place % (2 * BUCKET) * (math.pi / BUCKET)
        cosine, sine = np.cos(turn), -np.sin(turn)
        weights = np.full_like(cosine, 2.0)
        if residue == 0:
            sine[:, 0] = 1 - 2 * (place[:, 0] % 2)
            weights[:, 0] = 1.0
        to_spec.append(np.concatenate([cosine, sine], 1))
        to_time.append(np.concatenate([cosine * weights, sine * weights], 1).T / (2 * BUCKET))
    for residue in (1, 2, 3):
        bins = np.arange(QUARTER)[None, :]
        turn = (8 * bins + residue) * place % (2 * BUCKET) * (math.pi / BUCKET)
        cosine, sine = np.cos(turn), np.sin(turn)
        sign = 1.0 if residue == 3 else -1.0
        to_spec.append(np.block([[cosine, -sine], [sign * sine, sign * cosine]]))
        to_time.append(np.block([[cosine.T, sine.T], [-sine.T, cosine.T]]) / BUCKET)
    small = [np.stack(side[:2]).astype(jnp.bfloat16) for side in (to_spec, to_time)]
    large = [np.stack(side[2:]).astype(jnp.bfloat16) for side in (to_spec, to_time)]
    return small[0], large[0], small[1], large[1]


def quarters(x):
    return [x[:, q * QUARTER : (q + 1) * QUARTER] for q in range(4)]


def fold(x0, x1, x2, x3):
    even, odd = x0 + x2, x1 + x3
    diff = x1 - x3
    turned, tilted = diff * HALF_ROOT, odd * HALF_ROOT
    return even + odd, even - odd, x0 + turned, x2 + tilted, x0 - x2, diff, x0 - turned, x2 - tilted


def unfold(y0, y4, r1, i1, r2, i2, r3, i3):
    even, odd = y0 + y4, y0 - y4
    r_sum, r_diff, i_sum, i_diff = r1 + r3, r1 - r3, i1 + i3, i1 - i3
    return (
        even + (r2 + r_sum),
        odd - i2 + (r_diff - i_sum) * HALF_ROOT,
        even - (r2 + i_diff),
        odd + i2 - (r_diff + i_sum) * HALF_ROOT,
    )


def dot(a, b):
    return jnp.dot(a, b, preferred_element_type=jnp.float32)


def product(a, b, first, conj):
    half = a.shape[1] // 2
    ar, ai, br, bi = a[:, :half], a[:, half:], b[:, :half], b[:, half:]
    cross = ai * bi
    if conj:
        imag = ar * bi - ai * br
    else:
        imag = ar * bi + ai * br
    if first:
        lone = lax.broadcasted_iota(jnp.int32, cross.shape, 1) == 0
        imag = jnp.where(lone, cross, imag)
        cross = jnp.where(lone, 0.0, cross)
    real = ar * br + cross if conj else ar * br - cross
    return jnp.concatenate([real, imag], 1)


def table_of(small, large, group):
    return small[group] if group < 2 else large[group - 2]


def put_folded(dest, rows, parts):
    lower = pl.ds(rows.start + dest.shape[0] // 2, rows.size)
    for k, part in enumerate(parts):
        dest[rows if k < 4 else lower, k % 4 * QUARTER : (k % 4 + 1) * QUARTER] = part.astype(dest.dtype)


def get_folded(src, rows, at, width):
    if at >= BUCKET:
        rows, at = pl.ds(rows.start + src.shape[0] // 2, rows.size), at - BUCKET
    return src[rows, at : at + width]


def get_unfolded(src, rows):
    return unfold(*[src[rows, k * QUARTER : (k + 1) * QUARTER] for k in range(8)])


def steps(total, size, body):
    def one(k, carry):
        body(pl.ds(pl.multiple_of(k * size, size), size), k)
        return carry

    lax.fori_loop(0, total // size, one, 0, unroll=UNROLL if size == STEP_ROWS else 1)


def kernel_spectrum(ker, folded, spec, small, large, chunk):
    chans = ker.shape[0]

    def fold_rows(rows, _):
        put_folded(folded, rows, fold(*quarters(ker[rows, :].astype(jnp.float32))))

    steps(chans, STEP_ROWS, fold_rows)

    def transform_rows(rows, _):
        for g, (at, width) in enumerate(GROUPS):
            spec[rows, at : at + width] = dot(get_folded(folded, rows, at, width), table_of(small, large, g))

    steps(chans, chunk, transform_rows)


def token_stats(stream, chans):
    def add(k, carry):
        v = stream[pl.ds(pl.multiple_of(k * STEP_ROWS, STEP_ROWS), STEP_ROWS), :].astype(jnp.float32)
        return carry + v[:8] + v[8:]

    total = lax.fori_loop(0, chans // STEP_ROWS, add, jnp.zeros((8, BUCKET), jnp.float32), unroll=UNROLL)
    mean_val = jnp.sum(total, 0, keepdims=True) / chans

    def add_square(k, carry):
        v = stream[pl.ds(pl.multiple_of(k * STEP_ROWS, STEP_ROWS), STEP_ROWS), :].astype(jnp.float32) - mean_val
        v = v * v
        return carry + v[:8] + v[8:]

    total = lax.fori_loop(0, chans // STEP_ROWS, add_square, jnp.zeros((8, BUCKET), jnp.float32), unroll=UNROLL)
    return mean_val, lax.rsqrt(jnp.sum(total, 0, keepdims=True) / chans + 1e-05)


def lanes(x):
    total = x[:, :128]
    for k in range(1, x.shape[1] // 128):
        total = total + x[:, k * 128 : (k + 1) * 128]
    return total


GAIN, SHIFT, SKIP, BIAS_IN, BIAS_VAL = range(5)
MESH = pl.DeviceIdType.MESH


def bit_of(index, place):
    return lax.rem(lax.div(index, 1 << place), 2)


def flip(index, place):
    return index + (1 - 2 * bit_of(index, place)) * (1 << place)


def peers_of(n_chan):
    me, row = lax.axis_index("chan"), lax.axis_index("batch")
    others = []
    for k in range(1, n_chan):
        other = me
        for place in range(n_chan.bit_length() - 1):
            other = flip(other, place) if k >> place & 1 else other
        others.append(other)
    return me, row, others


def greet(targets):
    barrier = pltpu.get_barrier_semaphore()
    for target in targets:
        pl.semaphore_signal(barrier, inc=1, device_id=target, device_id_type=MESH)
    pl.semaphore_wait(barrier, len(targets))


LANES = 128
POWERS = 8
LOW_STAGE = 1


def halving(n_chan, n_batch):
    me, row = lax.axis_index("chan"), lax.axis_index("batch")
    chan_bits, batch_bits = n_chan.bit_length() - 1, n_batch.bit_length() - 1
    out = [(bit_of(me, k), (row, flip(me, k))) for k in reversed(range(chan_bits))]
    return out + [(bit_of(row, k), (flip(row, k), me)) for k in reversed(range(batch_bits))]


def doubled_powers(decay_rate, turn_rate):
    spans = [2.0**k for k in range(BUCKET.bit_length() - 1)]
    sizes = [jnp.exp(-span * decay_rate) for span in spans]
    total, moment = jnp.ones_like(decay_rate), jnp.zeros_like(decay_rate)
    for span, size in zip(spans, sizes):
        moment = moment * (1.0 + size) + span * size * total
        total = total * (1.0 + size)
    powers = []
    for span, size in list(zip(spans, sizes))[:POWERS]:
        powers += [size * jnp.cos(span * turn_rate), size * jnp.sin(span * turn_rate)]
    return powers, total, moment


def times(a, b):
    return a[0] * b[0] - a[1] * b[1], a[0] * b[1] + a[1] * b[0]


def columns_of(rows):
    pad = jnp.zeros((LANES - rows.shape[0], LANES), jnp.float32)
    return jnp.transpose(jnp.concatenate([rows, pad], 0))


def near_powers(params):
    lane = lax.broadcasted_iota(jnp.int32, (params.shape[0], LANES), 1)
    value = None
    for k in range(POWERS - 1):
        power = params[:, 2 * k : 2 * k + 1], params[:, 2 * k + 1 : 2 * k + 2]
        here = (lane & (1 << k)) != 0
        if value is None:
            value = jnp.where(here, power[0], 1.0), jnp.where(here, power[1], 0.0)
        else:
            moved = times(value, power)
            value = jnp.where(here, moved[0], value[0]), jnp.where(here, moved[1], value[1])
    far = params[:, 2 * POWERS - 2 : 2 * POWERS - 1], params[:, 2 * POWERS - 1 : 2 * POWERS]
    return value, tuple(jnp.broadcast_to(f, lane.shape) for f in far)


def halves(x):
    half = x.shape[0] // 2
    return [jnp.sum(x[:half], 0, keepdims=True), jnp.sum(x[half:], 0, keepdims=True)]


def kernel_rows(params):
    value, far = near_powers(params)
    value = times(value, (params[:, 2 * POWERS : 2 * POWERS + 1], params[:, 2 * POWERS + 1 : 2 * POWERS + 2]))
    out = [halves(value[0])]
    for _ in range(1, BUCKET // LANES):
        value = times(value, far)
        out.append(halves(value[0]))
    return [jnp.concatenate([row[c] for row in out], 0) for c in range(2)]


def state_rows(params, grads):
    value, far = near_powers(params)
    half = params.shape[0] // 2
    place = lax.broadcasted_iota(jnp.int32, (1, LANES), 1).astype(jnp.float32)
    plain = weighted = None
    for k in reversed(range(BUCKET // LANES)):
        rows = [g[:, k * LANES : (k + 1) * LANES] for g in grads]
        g = jnp.concatenate([jnp.broadcast_to(r, (half, LANES)) for r in rows], 0)
        w = jnp.concatenate([jnp.broadcast_to(r * (place + float(k * LANES)), (half, LANES)) for r in rows], 0)
        if plain is None:
            plain, weighted = (g, jnp.zeros_like(g)), (w, jnp.zeros_like(g))
        else:
            plain, weighted = times(plain, far), times(weighted, far)
            plain, weighted = (plain[0] + g, plain[1]), (weighted[0] + w, weighted[1])
    cols = times(plain, value) + times(weighted, value)
    lane = lax.broadcasted_iota(jnp.int32, value[0].shape, 1)
    out = jnp.zeros_like(value[0])
    for k, col in enumerate(cols):
        out = jnp.where(lane == k, jnp.sum(col, 1, keepdims=True), out)
    return jnp.transpose(out)[:8]


def remote(src, dst, send, recv, target):
    return pltpu.make_async_remote_copy(
        src_ref=src, dst_ref=dst, send_sem=send, recv_sem=recv, device_id=target, device_id_type=MESH
    )


def halving_bits(n_chan, n_batch):
    return n_chan.bit_length() + n_batch.bit_length() - 2


def whole(a):
    return pl.BlockSpec(a.shape, lambda t, n=a.ndim: (0,) * n, pipeline_mode=pl.Buffered(1))


ANYWHERE = pl.BlockSpec(memory_space=pl.ANY)
GATHER_ORDER = ((0, 1, 2, 3, 4), (0, 1, 3, 2, 4))


def train_kernel(
    n_chan, n_batch, mask, params, fs, fl, ts, tl, vec_mine, x_own, cot_own, w_own,
    out_all, in_all, state_all, lin_all, vec_all, cot_all, ker_all, w_all,
    hat_far, pre_far, act_far, sigma_far, slope_far, spec_far,
    x_low, hats, pres, acts, sigmas, slopes, specs, stats, streams, ker_spec, spec_grad, mixed, folded, pre_grad, back_low,
    w_near, loaded, sums, vecs, vec_in, ker_rows, ker_low,
    lin_grad, vec_grad, vec_cols, vec_rows, vec_got, vec_own,
    ker_sums, ker_sent, ker_got, lin_sums, lin_sent, lin_got, low_sent, low_got, ker_final, lin_final, state_own,
    move_send, move_recv, move_own, gather_send, gather_recv, gather_own, load_sem, far_sem,
    part_send, part_recv, ready, vec_send, vec_recv, vec_sem, all_send, all_recv, all_own,
):
    step = pl.program_id(0)
    layers, seqs = stats.shape[:2]
    chans = x_low.shape[1]
    own = chans // n_chan
    part = ker_final.shape[1]
    forward_steps = layers * seqs
    me, row, others = peers_of(n_chan)
    rows_of = [lax.rem(row + k, n_batch) for k in range(1, n_batch)]
    above = halving(n_chan, n_batch)
    path = list(reversed(above))
    bits, batch_bits = len(path), n_batch.bit_length() - 1
    total = 1 << bits
    core_bit = path[0][0]
    top, bottom = layers - 1, 0
    mine = pl.ds(pl.multiple_of(me * own, own), own)

    def trade(kind, k, source, dest):
        copies = [pltpu.make_async_copy(source(me), dest, move_own.at[kind, k])]
        for j, other in enumerate(others):
            copies.append(remote(source(other), dest, move_send.at[kind, k, j], move_recv.at[kind, k, j], (row, other)))
        return copies

    def columns(device, k):
        return pl.ds(pl.multiple_of((device * seqs + k) * BUCKET, BUCKET), BUCKET)

    def x_moves(k):
        return trade(0, k, lambda device: x_own.at[:, columns(device, k)], x_low.at[k, mine])

    def cot_moves(k):
        return trade(1, k, lambda device: cot_own.at[:, columns(device, k)], cot_all.at[k, mine])

    def rows_for(device):
        return pl.ds(pl.multiple_of(device * own, own), own)

    def out_moves(k):
        return trade(2, k, lambda device: back_low.at[k, rows_for(device)], out_all.at[:, columns(me, k)])

    def in_moves(k):
        return trade(3, k, lambda device: back_low.at[k, rows_for(device)], in_all.at[:, columns(me, k)])

    def run(copies):
        for copy in copies:
            copy.start()

    def finish_all(copies):
        for copy in copies:
            copy.wait()

    place = tuple(bit for bit, _ in above)

    def held(kind, i, s):
        order = GATHER_ORDER[kind]
        ref = (ker_all if kind == 0 else w_all).at[i]
        ref = ref.at[tuple(slice(None) if d in order[:s] else place[d] for d in range(bits))]
        k = 2 * i + kind
        return remote(ref, ref, gather_send.at[k, s], gather_recv.at[k, s], above[order[s]][1])

    def gather_next(i, s):
        for kind in (1, 0):
            held(kind, i, s).wait()
            if s + 1 < bits:
                held(kind, i, s + 1).start()

    def vec_in_moves():
        copies = [pltpu.make_async_copy(vec_mine, vec_in.at[me], gather_own.at[2 * layers])]
        for k, other in enumerate(others):
            copies.append(remote(vec_mine, vec_in.at[me], vec_send.at[1, k], vec_recv.at[1, k], (row, other)))
        return copies

    def make_kernels(i):
        def make(h, carry):
            first_row, second_row = kernel_rows(columns_of(params[i * part // 2 + h]))
            ker_rows[2 * h] = first_row
            ker_rows[2 * h + 1] = second_row
            return carry

        lax.fori_loop(0, part // 2, make, 0, unroll=4)
        for k in range(BUCKET // LANES):
            ker_low[i, :, k * LANES : (k + 1) * LANES] = ker_rows[:, k, :].astype(jnp.bfloat16)
        return pltpu.make_async_copy(ker_low.at[i], ker_all.at[(i,) + place], gather_own.at[2 * i])

    def load_kernels(layer):
        copy = pltpu.make_async_copy(ker_all.at[layer].reshape(chans, BUCKET), loaded, load_sem)
        copy.start()
        copy.wait()
        kernel_spectrum(loaded, folded, ker_spec, fs, fl, CONV_ROWS)

    def far_copies(k, back):
        pairs = zip((hats, pres, acts, sigmas, slopes, specs), (hat_far, pre_far, act_far, sigma_far, slope_far, spec_far))
        copies = []
        for j, (near, far) in enumerate(pairs):
            ends = (far.at[k], near.at[k]) if back else (near.at[k], far.at[k])
            copies.append(pltpu.make_async_copy(*ends, far_sem.at[j, k]))
        return copies

    groups = [[0], [1], [2, 3], [4]]
    count, at, gone = [], [0], 0
    for group in groups:
        gone += len(group)
        count.append(total >> gone)
        at.append(at[-1] + count[-1] * ((1 << len(group)) - 1))
    last_stage = len(groups) - 1

    def side(s, mask):
        chan, batch, index = me, row, 0
        for t, dim in enumerate(groups[s]):
            bit = path[dim][0]
            across = mask >> t & 1
            index = index + (1 - bit if across else bit) * (1 << t)
            if across and dim < batch_bits:
                batch = flip(batch, dim)
            elif across:
                chan = flip(chan, dim - batch_bits)
        return (batch, chan), index

    def masks(s):
        return range(1, 1 << len(groups[s]))

    def kept_rows(b):
        return spec_grad[pl.ds(pl.multiple_of(b * part, part), part), :BUCKET]

    def sums_at(s):
        return sum(count[1 : s + 1])

    def slot(kind, s, mask, sent):
        first = (mask - 1) * count[s]
        if kind == 0 or s == 0:
            return at[s] + first
        if s == LOW_STAGE:
            return first
        return first + at[s] - at[LOW_STAGE + 1] + (0 if sent else at[LOW_STAGE])

    def stage(kind, layer, s, mask):
        to, got = pl.ds(slot(kind, s, mask, True), count[s]), pl.ds(slot(kind, s, mask, False), count[s])
        if kind == 0:
            src, dst = ker_sent.at[to], ker_got.at[got]
        elif s == 0:
            src, dst = lin_grad.at[layer, :, 1 - core_bit], lin_got.at[got]
        elif s == LOW_STAGE:
            src, dst = low_sent.at[to], low_got.at[got]
        else:
            src, dst = lin_sent.at[to], lin_got.at[got]
        k = at_peer[s] + mask - 1
        return remote(src, dst, part_send.at[kind, k], part_recv.at[kind, k], side(s, mask)[0])

    at_peer = [0]
    for s in range(len(groups)):
        at_peer.append(at_peer[-1] + (1 << len(groups[s])) - 1)

    def begin(kind, layer, s):
        for mask in masks(s):
            if layer != layers - 1:
                pl.semaphore_wait(ready.at[kind, at_peer[s] + mask - 1], 1)
            stage(kind, layer, s, mask).start()

    def advance(kind, layer, s):
        for mask in masks(s):
            stage(kind, layer, s, mask).wait()

        def value(b):
            if kind == 0:
                result = kept_rows(b) if s == 0 else ker_sums[sums_at(s - 1) + b]
            else:
                result = lin_grad[layer, b, core_bit] if s == 0 else lin_sums[sums_at(s - 1) + b]
            for mask in masks(s):
                got = ker_got if kind == 0 else low_got if s == LOW_STAGE else lin_got
                result = result + got[slot(kind, s, mask, False) + b].astype(jnp.float32)
            return result

        if s == last_stage:
            final = ker_final if kind == 0 else lin_final
            final[layer] = value(0)
        else:
            wide = 1 << len(groups[s + 1])

            def one(b, carry):
                sums = ker_sums if kind == 0 else lin_sums
                sums[sums_at(s) + b] = value(wide * b + side(s + 1, 0)[1])
                for mask in masks(s + 1):
                    moved = value(wide * b + side(s + 1, mask)[1])
                    to = slot(kind, s + 1, mask, True) + b
                    if kind == 0:
                        ker_sent[to] = moved.astype(jnp.bfloat16)
                    elif s + 1 == LOW_STAGE:
                        low_sent[to] = moved.astype(jnp.bfloat16)
                    else:
                        lin_sent[to] = moved
                return carry

            lax.fori_loop(0, count[s + 1], one, 0)
        if layer == layers - 1:
            for mask in masks(s):
                there = side(s, mask)[0]
                pl.semaphore_signal(ready.at[kind, at_peer[s] + mask - 1], inc=1, device_id=there, device_id_type=MESH)
        if s < last_stage:
            begin(kind, layer, s + 1)

    def spread(own_ref, everyone, k):
        copies = [pltpu.make_async_copy(own_ref, everyone.at[row], all_own.at[k])]
        for j, other in enumerate(rows_of):
            copies.append(remote(own_ref, everyone.at[row], all_send.at[k, j], all_recv.at[k, j], (other, me)))
        return copies

    def spreads(kind, layer):
        if kind == 0:
            half = pl.ds(layer * part // 2, part // 2)
            return spread(state_own.at[half], state_all.at[:, half], layer)
        return spread(lin_final.at[layer], lin_all.at[:, layer], layers + layer)

    def vec_moves():
        copies = [pltpu.make_async_copy(vec_rows.at[me], vec_got.at[me], vec_sem)]
        for k, other in enumerate(others):
            copies.append(remote(vec_rows.at[other], vec_got.at[me], vec_send.at[0, k], vec_recv.at[0, k], (row, other)))
        return copies

    def states(layer):
        def one(h, carry):
            at = layer * part // 2 + h
            state_own[at] = state_rows(columns_of(params[at]), [ker_final[layer, pl.ds(2 * h + c, 1), :] for c in range(2)])
            return carry

        lax.fori_loop(0, part // 2, one, 0, unroll=4)

    @pl.when(step == 0)
    def _():
        greet([(row, other) for other in others] + [(other, me) for other in rows_of])
        locals_ = [pltpu.make_async_copy(w_own.at[i], w_all.at[(i,) + place], gather_own.at[2 * i + 1]) for i in range(layers)]
        run(locals_)
        run(vec_in_moves())
        finish_all(locals_)
        held(1, 0, 0).start()
        moves = x_moves(0)
        run(moves[:2])
        copy = make_kernels(0)
        copy.start()
        copy.wait()
        held(0, 0, 0).start()
        run(moves[2:])
        for i in range(1, layers):
            copy = make_kernels(i)
            copy.start()
            copy.wait()
            for kind in (1, 0):
                held(kind, i, 0).start()
        for s in range(bits):
            gather_next(0, s)
            if s == 1:
                run(x_moves(1)[:4])
            if s == 2:
                run(x_moves(1)[4:])
        finish_all(vec_in_moves())
        for i in range(layers):
            for c in range(n_chan):
                vecs[i, c * own : (c + 1) * own, :] = columns_of(vec_in[c, 8 * i : 8 * i + 8, :])[:own]
        vec_cols[...] = jnp.zeros_like(vec_cols)
        finish_all(x_moves(0))

    @pl.when(step == 1)
    def _():
        for k in range(1, seqs):
            finish_all(x_moves(k))
        for k in range(seqs):
            run(cot_moves(k))

    @pl.when(step < forward_steps)
    def _():
        layer, seq = lax.div(step, seqs), lax.rem(step, seqs)
        stream, hat_out, pre_out, act_out = streams.at[seq], hats.at[seq], pres.at[seq], acts.at[seq]
        sigma_out, slope_out, spec_out, first = sigmas.at[seq], slopes.at[seq], specs.at[seq], x_low.at[seq]
        stat, vec, weight = stats.at[layer, seq], vecs.at[layer], w_near.at[layer]
        hat, mixed = pre_grad, spec_grad

        @pl.when(layer == 0)
        def _():
            def widen(rows, _):
                stream[rows, :] = first[rows, :].astype(jnp.float32)

            steps(chans, STEP_ROWS, widen)

        @pl.when(seq == 0)
        def _():
            copy = pltpu.make_async_copy(w_all.at[layer].reshape(2 * chans, chans), weight, load_sem)
            copy.start()
            copy.wait()
            load_kernels(layer)

        @pl.when(layer > 0)
        def _():
            finish_all(far_copies(seq, False))

        mean_val, inv_std = token_stats(stream, chans)
        stat[0:1, :] = mean_val
        stat[1:2, :] = inv_std

        def normalise(rows, _):
            v = (stream[rows, :] - stat[0:1, :]) * stat[1:2, :]
            hat[rows, :] = v
            hat_out[rows, :] = v.astype(hat_out.dtype)
            v = v * vec[rows, GAIN : GAIN + 1] + vec[rows, SHIFT : SHIFT + 1]
            put_folded(folded, rows, fold(*quarters(v)))

        steps(chans, STEP_ROWS, normalise)

        @pl.when(step == 0)
        def _():
            gather_next(1, 0)

        def convolve(rows, _):
            for g, (at, width) in enumerate(GROUPS):
                spec = dot(get_folded(folded, rows, at, width), table_of(fs, fl, g))
                spec_out[rows, at : at + width] = spec.astype(jnp.bfloat16)
                both = product(ker_spec[rows, at : at + width], spec, g == 0, False)
                mixed[rows, at : at + width] = dot(both.astype(jnp.bfloat16), table_of(ts, tl, g))

        steps(chans, CONV_ROWS, convolve)

        @pl.when(step == 0)
        def _():
            gather_next(1, 1)

        def activate(rows, _):
            gain, shift, skip = [vec[rows, k : k + 1] for k in (GAIN, SHIFT, SKIP)]
            gain, shift = gain * skip, shift * skip
            for q, value in enumerate(get_unfolded(mixed, rows)):
                cols = slice(q * QUARTER, (q + 1) * QUARTER)
                pre = value + (gain * hat[rows, cols] + shift)
                pre_out[rows, cols] = pre.astype(pre_out.dtype)
                soft = jnp.tanh(pre * (GELU_A + GELU_B * (pre * pre)))
                act_out[rows, cols] = (0.5 * pre * (1.0 + soft)).astype(jnp.bfloat16)

        steps(chans, STEP_ROWS, activate)

        @pl.when(step == 0)
        def _():
            gather_next(1, 2)

        block = 2 * LIN_ROWS
        for t in range(4):
            cols = slice(t * QUARTER, (t + 1) * QUARTER)

            def linear(rows, k, cols=cols):
                mixed[:block, :QUARTER] = dot(weight[rows, :], act_out[:, cols])
                for o in range(LIN_ROWS // 16):
                    at = pl.ds(pl.multiple_of(k * LIN_ROWS + o * 16, 16), 16)
                    gate = mixed[o * 32 : o * 32 + 16, :QUARTER] + vec[at, BIAS_IN : BIAS_IN + 1]
                    value = mixed[o * 32 + 16 : o * 32 + 32, :QUARTER] + vec[at, BIAS_VAL : BIAS_VAL + 1]
                    sigma = 0.5 * jnp.tanh(0.5 * value) + 0.5
                    gated = gate * sigma
                    sigma_out[at, cols] = sigma.astype(sigma_out.dtype)
                    slope_out[at, cols] = (gated - gated * sigma).astype(slope_out.dtype)
                    moved = stream[at, cols] + mask[seq, :, cols] * gated
                    stream[at, cols] = moved
                    back_low[seq, at, cols] = (moved - first[at, cols].astype(jnp.float32)).astype(jnp.bfloat16)

            steps(2 * chans, block, linear)

        @pl.when(step == 0)
        def _():
            gather_next(1, 3)

        @pl.when(step == 1)
        def _():
            gather_next(1, 4)

        @pl.when(layer == 0)
        def _():
            run(far_copies(seq, False))

    @pl.when(step >= forward_steps)
    def _():
        turn, seq = lax.div(step - forward_steps, seqs), lax.rem(step - forward_steps, seqs)
        layer = layers - 1 - turn
        back, hat, pre, act = streams.at[seq], hats.at[seq], pres.at[seq], acts.at[seq]
        sigma_in, slope_in, spec, first = sigmas.at[seq], slopes.at[seq], specs.at[seq], x_low.at[seq]
        stat, vec = stats.at[layer, seq], vecs.at[layer]
        next_layer = (turn == 1) & (seq == 0)
        ends = (turn == layers - 1) & (seq == seqs - 1)

        for k in range(seqs):

            @pl.when((turn == 0) & (seq == k))
            def _(k=k):
                finish_all(cot_moves(k))
                copy = pltpu.make_async_copy(cot_all.at[k], x_low.at[k], load_sem)
                copy.start()
                run(out_moves(k))
                copy.wait()

            @pl.when((turn == 1) & (seq == k))
            def _(k=k):
                finish_all(far_copies(k, True))

        @pl.when((turn == 0) & (seq > 0))
        def _():
            run(far_copies(seq - 1, True))

        @pl.when((turn == 1) & (seq == 0))
        def _():
            run(far_copies(seqs - 1, True))

        @pl.when(turn == 0)
        def _():
            def widen(rows, _):
                back[rows, :] = first[rows, :].astype(jnp.float32)

            steps(chans, STEP_ROWS, widen)

        @pl.when(seq == 0)
        def _():
            load_kernels(layer)
            for k in range(4):
                cols = slice(k * QUARTER, (k + 1) * QUARTER)
                loaded[:, cols] = jnp.transpose(w_near[layer, cols, :])
            vec_grad[...] = jnp.zeros_like(vec_grad)

        def gates(rows, k):
            gated = back[rows, :] * mask[seq]
            left = (gated * sigma_in[rows, :].astype(jnp.float32)).astype(jnp.bfloat16)
            right = (gated * slope_in[rows, :].astype(jnp.float32)).astype(jnp.bfloat16)
            at = pl.multiple_of(k * 32, 32)
            folded[pl.ds(at, 16), :] = left
            folded[pl.ds(at + 16, 16), :] = right
            vec_grad[3, rows, :] += lanes(left.astype(jnp.float32))
            vec_grad[4, rows, :] += lanes(right.astype(jnp.float32))

        steps(chans, STEP_ROWS, gates)

        width = 2 * chans // total
        blocks = MAT_ROWS // (2 * width)

        def lin_back(rows, k):
            value = lax.dot_general(
                folded[rows, :], act[...], (((1,), (1,)), ((), ())), preferred_element_type=jnp.float32
            ).reshape(blocks, 2, width, chans)
            at = pl.ds(k * blocks, blocks)

            @pl.when(seq == 0)
            def _():
                lin_grad[layer, at] = value

            @pl.when(seq > 0)
            def _():
                lin_grad[layer, at] += value

        steps(2 * chans, MAT_ROWS, lin_back)

        @pl.when(next_layer)
        def _():
            for kind in (0, 1):
                advance(kind, top, 0)

        @pl.when(ends)
        def _():
            begin(1, bottom, 0)

        def act_back(rows, _):
            for t in range(4):
                cols = slice(t * QUARTER, (t + 1) * QUARTER)
                pre_grad[rows, cols] = dot(loaded[rows, :], folded[:, cols])

        steps(chans, MAT_ROWS, act_back)

        def gelu_back(rows, _):
            skip_sum = jnp.zeros((STEP_ROWS, 128), jnp.float32)
            outs = []
            for q in range(4):
                cols = slice(q * QUARTER, (q + 1) * QUARTER)
                p = pre[rows, cols].astype(jnp.float32)
                square = p * p
                soft = jnp.tanh(p * (GELU_A + GELU_B * square))
                slope = 0.5 * (1.0 + soft) + (0.5 * p) * (1.0 - soft * soft) * (GELU_A + (3.0 * GELU_B) * square)
                grad = pre_grad[rows, cols] * slope
                pre_grad[rows, cols] = grad
                norm = hat[rows, cols].astype(jnp.float32) * vec[rows, GAIN : GAIN + 1] + vec[rows, SHIFT : SHIFT + 1]
                skip_sum = skip_sum + lanes(grad * norm)
                outs.append(grad)
            vec_grad[2, rows, :] += skip_sum
            put_folded(folded, rows, fold(*outs))

        steps(chans, STEP_ROWS, gelu_back)

        @pl.when(ends)
        def _():
            for kind in (0, 1):
                advance(kind, top, 2)
            advance(1, bottom, 0)

        sums[...] = jnp.zeros_like(sums)

        @pl.when(seq == 0)
        def _():
            spec_grad[...] = jnp.zeros_like(spec_grad)

        def correlate(rows, chunk):
            for g, (at, width) in enumerate(GROUPS):
                grad = dot(get_folded(folded, rows, at, width), table_of(fs, fl, g))
                spec_grad[rows, at : at + width] += product(
                    spec[rows, at : at + width].astype(jnp.float32), grad, g == 0, True
                )
                both = product(ker_spec[rows, at : at + width], grad, g == 0, True)
                mixed[:, at : at + width] = dot(both.astype(jnp.bfloat16), table_of(ts, tl, g))

            def norm_back(k, carry):
                here = pl.ds(pl.multiple_of(k * STEP_ROWS, STEP_ROWS), STEP_ROWS)
                rows = pl.ds(pl.multiple_of(chunk * CHUNK_ROWS + k * STEP_ROWS, STEP_ROWS), STEP_ROWS)
                skip = vec[rows, SKIP : SKIP + 1]
                gain = vec[rows, GAIN : GAIN + 1]
                gain_sum = jnp.zeros((STEP_ROWS, 128), jnp.float32)
                shift_sum = jnp.zeros((STEP_ROWS, 128), jnp.float32)
                plain, weighted = [], []
                for q, part in enumerate(get_unfolded(mixed, here)):
                    cols = slice(q * QUARTER, (q + 1) * QUARTER)
                    grad = part + skip * pre_grad[rows, cols]
                    both = grad * hat[rows, cols].astype(jnp.float32)
                    gain_sum = gain_sum + lanes(both)
                    shift_sum = shift_sum + lanes(grad)
                    cent = grad * gain
                    pre_grad[rows, cols] = cent
                    both = both * gain
                    plain.append(cent[:8] + cent[8:])
                    weighted.append(both[:8] + both[8:])
                vec_grad[0, rows, :] += gain_sum
                vec_grad[1, rows, :] += shift_sum
                return carry[0] + jnp.concatenate(plain, 1), carry[1] + jnp.concatenate(weighted, 1)

            zero = jnp.zeros((8, BUCKET), jnp.float32)
            plain, weighted = lax.fori_loop(0, CHUNK_ROWS // STEP_ROWS, norm_back, (zero, zero), unroll=2)
            sums[0:8, :] += plain
            sums[8:16, :] += weighted

        steps(chans, CHUNK_ROWS, correlate)

        @pl.when(seq == seqs - 1)
        def _():
            def to_time(rows, _):
                for g, (at, width) in enumerate(GROUPS):
                    low = spec_grad[rows, at : at + width].astype(jnp.bfloat16)
                    ker_spec[rows, at : at + width] = dot(low, table_of(ts, tl, g))

            steps(chans, CONV_ROWS, to_time)

            def block_rows(b):
                return pl.ds(pl.multiple_of(b * part, part), part)

            def write(b, carry):
                for q, value in enumerate(get_unfolded(ker_spec, block_rows(2 * b + core_bit))):
                    spec_grad[block_rows(b), q * QUARTER : (q + 1) * QUARTER] = value
                for q, value in enumerate(get_unfolded(ker_spec, block_rows(2 * b + 1 - core_bit))):
                    ker_sent[b, :, q * QUARTER : (q + 1) * QUARTER] = value.astype(jnp.bfloat16)
                return carry

            lax.fori_loop(0, total // 2, write, 0)

        for i in range(layers):

            @pl.when((turn == i) & (seq == seqs - 1))
            def _(i=i):
                layer = layers - 1 - i
                begin(0, layer, 0)
                if layer == layers - 1:
                    begin(1, layer, 0)
                else:
                    advance(1, layer, 1)

        mean_plain = jnp.sum(sums[0:8, :], 0, keepdims=True) / chans
        mean_weighted = jnp.sum(sums[8:16, :], 0, keepdims=True) / chans
        sums[0:1, :] = mean_plain
        sums[8:9, :] = mean_weighted

        @pl.when(next_layer)
        def _():
            for kind in (0, 1):
                advance(kind, top, 1)

        for k in range(seqs):

            @pl.when((turn == layers - 1) & (seq == k))
            def _(k=k):
                finish_all(out_moves(k))

        def finish(rows, _):
            scaled = hat[rows, :].astype(jnp.float32) * sums[8:9, :]
            moved = back[rows, :] + stat[1:2, :] * (pre_grad[rows, :] - sums[0:1, :] - scaled)
            back[rows, :] = moved

        def leave(rows, _):
            scaled = hat[rows, :].astype(jnp.float32) * sums[8:9, :]
            moved = back[rows, :] + stat[1:2, :] * (pre_grad[rows, :] - sums[0:1, :] - scaled)
            back_low[seq, rows, :] = (moved - first[rows, :].astype(jnp.float32)).astype(jnp.bfloat16)

        @pl.when(turn < layers - 1)
        def _():
            steps(chans, STEP_ROWS, finish)

        @pl.when(turn == layers - 1)
        def _():
            steps(chans, STEP_ROWS, leave)

        for k in range(seqs):

            @pl.when((turn == layers - 1) & (seq == k))
            def _(k=k):
                run(in_moves(k))

        @pl.when(ends)
        def _():
            for kind in (0, 1):
                advance(kind, top, 3)

        for i in range(layers):

            @pl.when((turn == i) & (seq == seqs - 1))
            def _(i=i):
                layer = layers - 1 - i

                def vec_columns(rows, _):
                    lane = lax.broadcasted_iota(jnp.int32, (STEP_ROWS, LANES), 1)
                    out = vec_cols[rows, :]
                    for kind in range(5):
                        out = jnp.where(lane == layer * 5 + kind, jnp.sum(vec_grad[kind, rows, :], 1, keepdims=True), out)
                    vec_cols[rows, :] = out

                steps(chans, STEP_ROWS, vec_columns)

        @pl.when(ends)
        def _():
            for c in range(n_chan):
                vec_rows[c] = columns_of(vec_cols[c * own : (c + 1) * own, :])[:16]
            run(vec_moves())
            states(top)
            run(spreads(0, top) + spreads(1, top))
            for s in range(last_stage + 1):
                advance(0, bottom, s)
                if s + 2 <= last_stage:
                    advance(1, bottom, s + 2)
                    if s + 2 == last_stage:
                        run(spreads(1, bottom))
                if s == 1:
                    for copy in vec_moves():
                        copy.wait()
                    vec_own[...] = jnp.sum(vec_got[...], 0)
                    run(spread(vec_own, vec_all, 2 * layers))
            states(bottom)
            run(spreads(0, bottom))
            for k in range(seqs):
                finish_all(in_moves(k))
            for i in range(layers):
                for copy in spreads(0, i) + spreads(1, i):
                    copy.wait()
            for copy in spread(vec_own, vec_all, 2 * layers):
                copy.wait()


def train(mask, params, tables, vec_mine, x_own, cot_own, w_own, n_chan, n_batch):
    own, group = x_own.shape
    chans, toks = own * n_chan, group // n_chan
    seqs, layers = toks // BUCKET, w_own.shape[0]
    bits = halving_bits(n_chan, n_batch)
    total = 1 << bits
    part = chans // total
    low_count, peers = total >> (LOW_STAGE + 1), bits + 1
    shape, low, full = jax.ShapeDtypeStruct, jnp.bfloat16, jnp.float32
    vmem, dma = pltpu.VMEM, pltpu.SemaphoreType.DMA
    there = (2,) * bits
    slots, wide = (seqs, chans, BUCKET), (seqs, chans, 2 * BUCKET)
    return pl.pallas_call(
        functools.partial(train_kernel, n_chan, n_batch),
        grid=(2 * layers * seqs,),
        in_specs=[whole(a) for a in (mask, params, *tables, vec_mine)] + [ANYWHERE] * 3,
        out_specs=[ANYWHERE] * 14,
        out_shape=[
            shape((own, group), low),
            shape((own, group), low),
            shape((n_batch, layers * part // 2, 8, LANES), full),
            shape((n_batch, layers, 2 * part, chans), full),
            shape((n_batch, 16, LANES), full),
            shape(slots, low),
            shape((layers,) + there + (part, BUCKET), low),
            shape((layers,) + there + (2 * part, chans), low),
        ]
        + [shape(slots, low)] * 5
        + [shape(wide, low)],
        scratch_shapes=[vmem(slots, low)] * 6
        + [
            vmem(wide, low),
            vmem((layers, seqs, 8, BUCKET), full),
            vmem(slots, full),
            vmem((chans, 2 * BUCKET), full),
            vmem((chans, 2 * BUCKET), full),
            vmem((CHUNK_ROWS, 2 * BUCKET), full),
            vmem((2 * chans, BUCKET), low),
            vmem((chans, BUCKET), full),
            vmem(slots, low),
            vmem((layers, 2 * chans, chans), low),
            vmem((chans, BUCKET), low),
            vmem((16, BUCKET), full),
            vmem((layers, chans, LANES), full),
            vmem((n_chan, 16, LANES), full),
            vmem((part, BUCKET // LANES, LANES), full),
            vmem((layers, part, BUCKET), low),
            vmem((layers, total // 2, 2, 2 * part, chans), full),
            vmem((5, chans, LANES), full),
            vmem((chans, LANES), full),
            vmem((n_chan, 16, LANES), full),
            vmem((n_chan, 16, LANES), full),
            vmem((16, LANES), full),
            vmem((3 * total // 8, part, BUCKET), full),
            vmem((total, part, BUCKET), low),
            vmem((total, part, BUCKET), low),
            vmem((3 * total // 8, 2 * part, chans), full),
            vmem((low_count, 2 * part, chans), full),
            vmem((total - low_count, 2 * part, chans), full),
            vmem((low_count, 2 * part, chans), low),
            vmem((low_count, 2 * part, chans), low),
            vmem((layers, part, BUCKET), full),
            vmem((layers, 2 * part, chans), full),
            vmem((layers * part // 2, 8, LANES), full),
            dma((4, seqs, n_chan - 1)), dma((4, seqs, n_chan - 1)), dma((4, seqs)),
            dma((2 * layers, bits)), dma((2 * layers, bits)), dma((2 * layers + 1,)),
            dma, dma((6, seqs)),
            dma((2, peers)), dma((2, peers)), pltpu.SemaphoreType.REGULAR((2, peers)),
            dma((2, n_chan - 1)), dma((2, n_chan - 1)), dma,
            dma((2 * layers + 1, n_batch - 1)), dma((2 * layers + 1, n_batch - 1)), dma((2 * layers + 1,)),
        ],
        compiler_params=pltpu.CompilerParams(vmem_limit_bytes=ROOM, collective_id=1, has_side_effects=True),
        cost_estimate=pl.CostEstimate(flops=60 * 10**9, bytes_accessed=60 * 2**20, transcendentals=0),
        name="train",
    )(mask, params, *tables, vec_mine, x_own, cot_own, w_own)


def adam(weight, grad, first, second, rate):
    first_new = 0.9 * first + 0.1 * grad
    second_new = 0.999 * second + 0.001 * grad * grad
    fixed_first = first_new / (1.0 - 0.9**STEP)
    fixed_second = second_new / (1.0 - 0.999**STEP)
    new_weight = weight - rate * (fixed_first / (jnp.sqrt(fixed_second) + 1e-08) + 0.01 * weight)
    return (first_new, second_new, new_weight)


def local(
    inputs, lengths, cotangent, ln_gain, ln_bias, log_step, skip_gain, lin_bias, log_decay, frequency,
    w_re, w_im, lin_weight, lin_moment, lin_square, vec_moment, vec_square, state_moment, state_square,
):
    n_chan = lax.axis_size("chan")
    n_batch = lax.axis_size("batch")
    own = inputs.shape[0]
    chans = own * n_chan
    toks = inputs.shape[1] // n_chan
    seqs = toks // BUCKET
    part = own // n_batch
    me = lax.axis_index("chan")
    row = lax.axis_index("batch")
    lens = lax.dynamic_slice_in_dim(lengths, me * seqs, seqs)
    places = lax.iota(jnp.int32, BUCKET)
    valid = (places[None, :] < lens[:, None]).astype(jnp.float32).reshape(seqs, 1, BUCKET)
    tables = tuple(jnp.asarray(t) for t in transform_tables())

    def mine(a):
        return lax.dynamic_slice_in_dim(a, row * part, part, 1)

    step_size = jnp.exp(log_step)[..., None]
    decay_rate = step_size * jnp.exp(log_decay)
    turn_rate = step_size * frequency
    powers, total, moment = doubled_powers(decay_rate, turn_rate)
    params = jnp.stack([mine(a).reshape(LAYERS * part // 2, -1) for a in powers + [w_re / total, w_im / total]], 1)
    params = jnp.pad(params, ((0, 0), (0, -params.shape[1] % 8), (0, 0)))
    w_own = mine(lin_weight).transpose(0, 2, 1, 3).reshape(LAYERS, 2 * part, chans).astype(jnp.bfloat16)
    vec_own = jnp.stack([ln_gain, ln_bias, skip_gain, lin_bias[:, 0], lin_bias[:, 1]], 1)
    vec_own = jnp.pad(vec_own, ((0, 0), (0, 3), (0, LANES - own))).reshape(8 * LAYERS, LANES)
    out_delta, in_delta, state_all, lin_all, vec_all, *_ = train(
        valid, params, tables, vec_own, inputs, cotangent, w_own, n_chan, n_batch
    )
    output = inputs.astype(jnp.float32) + out_delta.astype(jnp.float32)
    input_grad = cotangent.astype(jnp.float32) + in_delta.astype(jnp.float32)

    state_all = state_all.reshape(n_batch, LAYERS, part // 2, 8, 2, LANES // 2)
    state_all = state_all.transpose(3, 1, 0, 2, 4, 5).reshape(8, LAYERS, own, -1) / total
    c_re, c_im, d_re, d_im = [state_all[k] for k in range(4)]
    turn_grad = -(w_re * d_im + w_im * d_re)
    decay_grad = ((w_re * c_re - w_im * c_im) * (moment / total) - (w_re * d_re - w_im * d_im)) * decay_rate
    state_total = jnp.stack([decay_grad, turn_grad * step_size, c_re, -c_im], 1)
    step_total = jnp.sum(decay_grad + turn_grad * turn_rate, -1)
    lin_total = lin_all.reshape(n_batch, LAYERS, 2, part, chans).transpose(1, 0, 3, 2, 4).reshape(LAYERS, own, 2, chans)
    vec_sum = jnp.sum(vec_all, 0)[: 5 * LAYERS, :own].reshape(LAYERS, 5, own)
    vec_total = jnp.stack([vec_sum[:, 0], vec_sum[:, 1], step_total, vec_sum[:, 2], vec_sum[:, 3], vec_sum[:, 4]], 1)

    vec_old = jnp.stack([ln_gain, ln_bias, log_step, skip_gain, lin_bias[:, 0], lin_bias[:, 1]], 1)
    state_old = jnp.stack([log_decay, frequency, w_re, w_im], 1)
    lin_first, lin_second, lin_new = adam(lin_weight, lin_total, lin_moment, lin_square, 0.05)
    vec_first, vec_second, vec_new = adam(vec_old, vec_total, vec_moment, vec_square, 0.2)
    state_first, state_second, state_new = adam(state_old, state_total, state_moment, state_square, 0.2)
    return (
        output, input_grad, lin_first, lin_second, lin_new, vec_first, vec_second, vec_new,
        state_first, state_second, state_new,
    )


def tables(length):
    full_width = 2 * length
    row_ids = lax.iota(jnp.int32, length)[:, None]
    col_ids = lax.iota(jnp.int32, length)[None, :]
    turn_all = (row_ids * col_ids % full_width).astype(jnp.float32) * (2.0 * math.pi / full_width)
    cosine = jnp.cos(turn_all)
    sine_table = jnp.sin(turn_all)
    weights = jnp.where(lax.iota(jnp.int32, length) == 0, 1.0, 2.0).astype(jnp.float32)[None, :]
    alternate = (1 - 2 * (lax.iota(jnp.int32, length) % 2)).astype(jnp.float32)
    return (cosine, sine_table, cosine * weights, sine_table * weights, alternate)


def mixer(normed, log_decay, frequency, w_re, w_im, log_step, skip_gain):
    top_prec = lax.Precision.HIGHEST
    chan_count = normed.shape[0]
    seq_count = normed.shape[1] // BUCKET
    step_size = jnp.exp(log_step)[:, None]
    decay_rate = step_size * jnp.exp(log_decay)
    turn_rate = step_size * frequency
    places = lax.iota(jnp.float32, BUCKET)
    decay_all = jnp.exp(-decay_rate[..., None] * places)
    soft = decay_all / jnp.sum(decay_all, -1, keepdims=True)
    phase_all = turn_rate[..., None] * places
    kernel = jnp.sum(
        (w_re[..., None] * jnp.cos(phase_all) - w_im[..., None] * jnp.sin(phase_all)) * soft, 1
    )
    cosine, sine_table, cos_back, sin_back, alternate = tables(BUCKET)
    signal = normed.reshape(chan_count, seq_count, BUCKET)
    sig_re = jnp.einsum("csl,lk->csk", signal, cosine, precision=top_prec)
    sig_im = -jnp.einsum("csl,lk->csk", signal, sine_table, precision=top_prec)
    sig_top = jnp.sum(signal * alternate, -1)
    ker_re = jnp.dot(kernel, cosine, precision=top_prec)[:, None, :]
    ker_im = -jnp.dot(kernel, sine_table, precision=top_prec)[:, None, :]
    ker_top = jnp.sum(kernel * alternate, -1)[:, None]
    prod_re = sig_re * ker_re - sig_im * ker_im
    prod_im = sig_re * ker_im + sig_im * ker_re
    prod_top = sig_top * ker_top
    conv_out = jnp.einsum("csk,lk->csl", prod_re, cos_back, precision=top_prec)
    conv_out = conv_out - jnp.einsum("csk,lk->csl", prod_im, sin_back, precision=top_prec)
    conv_out = conv_out + prod_top[..., None] * alternate
    conv_out = conv_out / (2.0 * BUCKET)
    pre_act = conv_out.reshape(normed.shape) + skip_gain[:, None] * normed
    return jax.nn.gelu(pre_act)


def wide_local(
    inputs,
    lengths,
    cotangent,
    ln_gain,
    ln_bias,
    log_step,
    skip_gain,
    lin_bias,
    log_decay,
    frequency,
    w_re,
    w_im,
    lin_weight,
    lin_moment,
    lin_square,
    vec_moment,
    vec_square,
    state_moment,
    state_square,
):
    chan_total = inputs.shape[0] * lax.axis_size("chan")
    tok_count = inputs.shape[1]
    places = lax.iota(jnp.int32, BUCKET)
    valid = (places[None, :] < lengths[:, None]).astype(jnp.float32).reshape(1, tok_count)
    weights_low = lin_weight.astype(jnp.bfloat16)
    stream = inputs.astype(jnp.float32)
    saved = []
    for layer_idx in range(LAYERS):
        sums = lax.psum((jnp.sum(stream, 0), jnp.sum(stream * stream, 0)), "chan")
        mean_val = sums[0] / chan_total
        variance = sums[1] / chan_total - mean_val * mean_val
        inv_std = lax.rsqrt(variance + 1e-05)[None, :]
        centred = (stream - mean_val[None, :]) * inv_std
        normed = centred * ln_gain[layer_idx][:, None] + ln_bias[layer_idx][:, None]
        activated, mixer_back = jax.vjp(
            mixer,
            normed,
            log_decay[layer_idx],
            frequency[layer_idx],
            w_re[layer_idx],
            w_im[layer_idx],
            log_step[layer_idx],
            skip_gain[layer_idx],
        )
        act_low = activated.astype(jnp.bfloat16)
        act_all = lax.all_gather(act_low, "chan", axis=0, tiled=True)
        mixed = jnp.einsum(
            "ht,cjh->cjt", act_all, weights_low[layer_idx], preferred_element_type=jnp.float32
        )
        kept = act_all
        mixed = mixed + lin_bias[layer_idx].T[:, :, None]
        gate_in = mixed[:, 0]
        gate_val = mixed[:, 1]
        stream = stream + valid * gate_in * jax.nn.sigmoid(gate_val)
        saved.append((centred, inv_std, mixer_back, kept, gate_in, gate_val))
    back_stream = cotangent.astype(jnp.float32)
    lin_grads = [None] * LAYERS
    vec_grads = [None] * LAYERS
    state_grads = [None] * LAYERS
    for layer_idx in reversed(range(LAYERS)):
        centred, inv_std, mixer_back, kept, gate_in, gate_val = saved[layer_idx]
        sigma = jax.nn.sigmoid(gate_val)
        gated_back = back_stream * valid
        grad_mixed = jnp.stack(
            [gated_back * sigma, gated_back * gate_in * sigma * (1.0 - sigma)], 1
        ).astype(jnp.bfloat16)
        bias_grad = jnp.sum(grad_mixed.astype(jnp.float32), 2).T
        weight_grad = jnp.einsum(
            "ht,cjt->cjh", kept, grad_mixed, preferred_element_type=jnp.float32
        )
        act_part = jnp.einsum(
            "cjt,cjh->ht", grad_mixed, weights_low[layer_idx], preferred_element_type=jnp.float32
        )
        act_grad = lax.psum_scatter(act_part, "chan", scatter_dimension=0, tiled=True)
        normed_grad, decay_grad, freq_grad, re_grad, im_grad, step_grad, skip_grad = mixer_back(
            act_grad
        )
        gain_grad = jnp.sum(normed_grad * centred, 1)
        shift_grad = jnp.sum(normed_grad, 1)
        centred_grad = normed_grad * ln_gain[layer_idx][:, None]
        back_sums = lax.psum((jnp.sum(centred_grad, 0), jnp.sum(centred_grad * centred, 0)), "chan")
        back_stream = back_stream + inv_std * (
            centred_grad
            - back_sums[0][None, :] / chan_total
            - centred * back_sums[1][None, :] / chan_total
        )
        lin_grads[layer_idx] = weight_grad
        vec_grads[layer_idx] = jnp.stack(
            [gain_grad, shift_grad, step_grad, skip_grad, bias_grad[0], bias_grad[1]]
        )
        state_grads[layer_idx] = jnp.stack([decay_grad, freq_grad, re_grad, im_grad])
    lin_total, vec_total, state_total = lax.psum(
        (jnp.stack(lin_grads), jnp.stack(vec_grads), jnp.stack(state_grads)), "batch"
    )
    vec_old = jnp.stack([ln_gain, ln_bias, log_step, skip_gain, lin_bias[:, 0], lin_bias[:, 1]], 1)
    state_old = jnp.stack([log_decay, frequency, w_re, w_im], 1)
    lin_first, lin_second, lin_new = adam(lin_weight, lin_total, lin_moment, lin_square, 0.05)
    vec_first, vec_second, vec_new = adam(vec_old, vec_total, vec_moment, vec_square, 0.2)
    state_first, state_second, state_new = adam(
        state_old, state_total, state_moment, state_square, 0.2
    )
    return (
        stream,
        back_stream,
        lin_first,
        lin_second,
        lin_new,
        vec_first,
        vec_second,
        vec_new,
        state_first,
        state_second,
        state_new,
    )


def suits(own_seqs, chans, n_chan, n_batch):
    powers = n_chan & (n_chan - 1) == 0 and n_batch & (n_batch - 1) == 0
    return powers and own_seqs == 2 * n_chan and (n_chan, n_batch) == (8, 4) and chans == 16 * n_chan * n_batch


def solution(mesh):
    in_specs = (
        P("chan", "batch"),
        P("batch"),
        P("chan", "batch"),
        P(None, "chan"),
        P(None, "chan"),
        P(None, "chan"),
        P(None, "chan"),
        P(None, None, "chan"),
        P(None, "chan", None),
        P(None, "chan", None),
        P(None, "chan", None),
        P(None, "chan", None),
        P(None, "chan", None, None),
        P(None, "chan", None, None),
        P(None, "chan", None, None),
        P(None, None, "chan"),
        P(None, None, "chan"),
        P(None, None, "chan", None),
        P(None, None, "chan", None),
    )
    out_specs = (
        P("chan", "batch"),
        P("chan", "batch"),
        P(None, "chan", None, None),
        P(None, "chan", None, None),
        P(None, "chan", None, None),
        P(None, None, "chan"),
        P(None, None, "chan"),
        P(None, None, "chan"),
        P(None, None, "chan", None),
        P(None, None, "chan", None),
        P(None, None, "chan", None),
    )
    n_chan = mesh.shape["chan"]

    def run(*args):
        own_seqs = args[1].shape[0] // mesh.shape["batch"]
        fits = suits(own_seqs, args[3].shape[1], n_chan, mesh.shape["batch"])
        body = local if fits else wide_local
        return jax.shard_map(body, mesh=mesh, in_specs=in_specs, out_specs=out_specs, check_vma=False)(*args)

    return run
```

```python
import functools
import math

import jax
import jax.numpy as jnp
import numpy as np
from jax import lax
from jax.experimental import pallas as pl
from jax.experimental.pallas import tpu as pltpu
from jax.sharding import PartitionSpec as P

LAYERS = 2
BUCKET = 1024
STEP = 10


QUARTER = BUCKET // 4
HALF_ROOT = math.sqrt(0.5)
STEP_ROWS = 16
UNROLL = 4
CONV_ROWS = 512
CHUNK_ROWS = 256
MAT_ROWS = 512
LIN_ROWS = 256
ROOM = 59 * 2**20
GROUPS = ((0, 256), (256, 256), (512, 512), (1024, 512), (1536, 512))
GELU_A = math.sqrt(2.0 / math.pi)
GELU_B = GELU_A * 0.044715


def transform_tables():
    place = np.arange(QUARTER)[:, None]
    to_spec, to_time = [], []
    for residue in (0, 4):
        bins = np.arange(QUARTER // 2)[None, :]
        turn = (8 * bins + residue) * place % (2 * BUCKET) * (math.pi / BUCKET)
        cosine, sine = np.cos(turn), -np.sin(turn)
        weights = np.full_like(cosine, 2.0)
        if residue == 0:
            sine[:, 0] = 1 - 2 * (place[:, 0] % 2)
            weights[:, 0] = 1.0
        to_spec.append(np.concatenate([cosine, sine], 1))
        to_time.append(np.concatenate([cosine * weights, sine * weights], 1).T / (2 * BUCKET))
    for residue in (1, 2, 3):
        bins = np.arange(QUARTER)[None, :]
        turn = (8 * bins + residue) * place % (2 * BUCKET) * (math.pi / BUCKET)
        cosine, sine = np.cos(turn), np.sin(turn)
        sign = 1.0 if residue == 3 else -1.0
        to_spec.append(np.block([[cosine, -sine], [sign * sine, sign * cosine]]))
        to_time.append(np.block([[cosine.T, sine.T], [-sine.T, cosine.T]]) / BUCKET)
    small = [np.stack(side[:2]).astype(jnp.bfloat16) for side in (to_spec, to_time)]
    large = [np.stack(side[2:]).astype(jnp.bfloat16) for side in (to_spec, to_time)]
    return small[0], large[0], small[1], large[1]


def quarters(x):
    return [x[:, q * QUARTER : (q + 1) * QUARTER] for q in range(4)]


def fold(x0, x1, x2, x3):
    even, odd = x0 + x2, x1 + x3
    diff = x1 - x3
    turned, tilted = diff * HALF_ROOT, odd * HALF_ROOT
    return even + odd, even - odd, x0 + turned, x2 + tilted, x0 - x2, diff, x0 - turned, x2 - tilted


def unfold(y0, y4, r1, i1, r2, i2, r3, i3):
    even, odd = y0 + y4, y0 - y4
    r_sum, r_diff, i_sum, i_diff = r1 + r3, r1 - r3, i1 + i3, i1 - i3
    return (
        even + (r2 + r_sum),
        odd - i2 + (r_diff - i_sum) * HALF_ROOT,
        even - (r2 + i_diff),
        odd + i2 - (r_diff + i_sum) * HALF_ROOT,
    )


def dot(a, b):
    return jnp.dot(a, b, preferred_element_type=jnp.float32)


def product(a, b, first, conj):
    half = a.shape[1] // 2
    ar, ai, br, bi = a[:, :half], a[:, half:], b[:, :half], b[:, half:]
    cross = ai * bi
    if conj:
        imag = ar * bi - ai * br
    else:
        imag = ar * bi + ai * br
    if first:
        lone = lax.broadcasted_iota(jnp.int32, cross.shape, 1) == 0
        imag = jnp.where(lone, cross, imag)
        cross = jnp.where(lone, 0.0, cross)
    real = ar * br + cross if conj else ar * br - cross
    return jnp.concatenate([real, imag], 1)


def table_of(small, large, group):
    return small[group] if group < 2 else large[group - 2]


def put_folded(dest, rows, parts):
    lower = pl.ds(rows.start + dest.shape[0] // 2, rows.size)
    for k, part in enumerate(parts):
        dest[rows if k < 4 else lower, k % 4 * QUARTER : (k % 4 + 1) * QUARTER] = part.astype(dest.dtype)


def get_folded(src, rows, at, width):
    if at >= BUCKET:
        rows, at = pl.ds(rows.start + src.shape[0] // 2, rows.size), at - BUCKET
    return src[rows, at : at + width]


def get_unfolded(src, rows):
    return unfold(*[src[rows, k * QUARTER : (k + 1) * QUARTER] for k in range(8)])


def steps(total, size, body):
    def one(k, carry):
        body(pl.ds(pl.multiple_of(k * size, size), size), k)
        return carry

    lax.fori_loop(0, total // size, one, 0, unroll=UNROLL if size == STEP_ROWS else 1)


def kernel_spectrum(ker, folded, spec, small, large, chunk):
    chans = ker.shape[0]

    def fold_rows(rows, _):
        put_folded(folded, rows, fold(*quarters(ker[rows, :].astype(jnp.float32))))

    steps(chans, STEP_ROWS, fold_rows)

    def transform_rows(rows, _):
        for g, (at, width) in enumerate(GROUPS):
            spec[rows, at : at + width] = dot(get_folded(folded, rows, at, width), table_of(small, large, g))

    steps(chans, chunk, transform_rows)


def token_stats(stream, chans):
    def add(k, carry):
        v = stream[pl.ds(pl.multiple_of(k * STEP_ROWS, STEP_ROWS), STEP_ROWS), :].astype(jnp.float32)
        return carry + v[:8] + v[8:]

    total = lax.fori_loop(0, chans // STEP_ROWS, add, jnp.zeros((8, BUCKET), jnp.float32), unroll=UNROLL)
    mean_val = jnp.sum(total, 0, keepdims=True) / chans

    def add_square(k, carry):
        v = stream[pl.ds(pl.multiple_of(k * STEP_ROWS, STEP_ROWS), STEP_ROWS), :].astype(jnp.float32) - mean_val
        v = v * v
        return carry + v[:8] + v[8:]

    total = lax.fori_loop(0, chans // STEP_ROWS, add_square, jnp.zeros((8, BUCKET), jnp.float32), unroll=UNROLL)
    return mean_val, lax.rsqrt(jnp.sum(total, 0, keepdims=True) / chans + 1e-05)


def lanes(x):
    total = x[:, :128]
    for k in range(1, x.shape[1] // 128):
        total = total + x[:, k * 128 : (k + 1) * 128]
    return total


GAIN, SHIFT, SKIP, BIAS_IN, BIAS_VAL = range(5)
MESH = pl.DeviceIdType.MESH


def bit_of(index, place):
    return lax.rem(lax.div(index, 1 << place), 2)


def flip(index, place):
    return index + (1 - 2 * bit_of(index, place)) * (1 << place)


def peers_of(n_chan):
    me, row = lax.axis_index("chan"), lax.axis_index("batch")
    others = []
    for k in range(1, n_chan):
        other = me
        for place in range(n_chan.bit_length() - 1):
            other = flip(other, place) if k >> place & 1 else other
        others.append(other)
    return me, row, others


def greet(targets, between):
    barrier = pltpu.get_barrier_semaphore()
    for target in targets:
        pl.semaphore_signal(barrier, inc=1, device_id=target, device_id_type=MESH)
    between()
    pl.semaphore_wait(barrier, len(targets))


LANES = 128
POWERS = 8
LOW_STAGE = 1


def halving(n_chan, n_batch):
    me, row = lax.axis_index("chan"), lax.axis_index("batch")
    chan_bits, batch_bits = n_chan.bit_length() - 1, n_batch.bit_length() - 1
    out = [(bit_of(me, k), (row, flip(me, k))) for k in reversed(range(chan_bits))]
    return out + [(bit_of(row, k), (flip(row, k), me)) for k in reversed(range(batch_bits))]


def mode_rows(raw):
    step_size = jnp.exp(raw[4])
    decay_rate, turn_rate = step_size * jnp.exp(raw[0]), step_size * raw[1]
    spans = [2.0**k for k in range(BUCKET.bit_length() - 1)]
    sizes = [jnp.exp(-span * decay_rate) for span in spans]
    total, moment = jnp.ones_like(decay_rate), jnp.zeros_like(decay_rate)
    for span, size in zip(spans, sizes):
        moment = moment * (1.0 + size) + span * size * total
        total = total * (1.0 + size)
    rows = []
    for span, size in list(zip(spans, sizes))[:POWERS]:
        rows += [size * jnp.cos(span * turn_rate), size * jnp.sin(span * turn_rate)]
    inverse = 1.0 / total
    return rows + [raw[2] * inverse, raw[3] * inverse, inverse, moment * inverse, decay_rate, turn_rate, step_size, raw[2], raw[3]]


def times(a, b):
    return a[0] * b[0] - a[1] * b[1], a[0] * b[1] + a[1] * b[0]


def columns_of(rows):
    pad = jnp.zeros((LANES - rows.shape[0], LANES), jnp.float32)
    return jnp.transpose(jnp.concatenate([rows, pad], 0))


def near_powers(params):
    lane = lax.broadcasted_iota(jnp.int32, (params.shape[0], LANES), 1)
    value = None
    for k in range(POWERS - 1):
        power = params[:, 2 * k : 2 * k + 1], params[:, 2 * k + 1 : 2 * k + 2]
        here = (lane & (1 << k)) != 0
        if value is None:
            value = jnp.where(here, power[0], 1.0), jnp.where(here, power[1], 0.0)
        else:
            moved = times(value, power)
            value = jnp.where(here, moved[0], value[0]), jnp.where(here, moved[1], value[1])
    far = params[:, 2 * POWERS - 2 : 2 * POWERS - 1], params[:, 2 * POWERS - 1 : 2 * POWERS]
    return value, tuple(jnp.broadcast_to(f, lane.shape) for f in far)


def halves(x):
    half = x.shape[0] // 2
    return [jnp.sum(x[:half], 0, keepdims=True), jnp.sum(x[half:], 0, keepdims=True)]


def kernel_rows(params):
    value, far = near_powers(params)
    value = times(value, (params[:, 2 * POWERS : 2 * POWERS + 1], params[:, 2 * POWERS + 1 : 2 * POWERS + 2]))
    out = [halves(value[0])]
    for _ in range(1, BUCKET // LANES):
        value = times(value, far)
        out.append(halves(value[0]))
    return [jnp.concatenate([row[c] for row in out], 0) for c in range(2)]


def state_rows(modes, grads):
    params = columns_of(modes)
    value, far = near_powers(params)
    half = params.shape[0] // 2
    place = lax.broadcasted_iota(jnp.int32, (1, LANES), 1).astype(jnp.float32)
    plain = weighted = None
    for k in reversed(range(BUCKET // LANES)):
        rows = [g[:, k * LANES : (k + 1) * LANES] for g in grads]
        g = jnp.concatenate([jnp.broadcast_to(r, (half, LANES)) for r in rows], 0)
        w = jnp.concatenate([jnp.broadcast_to(r * (place + float(k * LANES)), (half, LANES)) for r in rows], 0)
        if plain is None:
            plain, weighted = (g, jnp.zeros_like(g)), (w, jnp.zeros_like(g))
        else:
            plain, weighted = times(plain, far), times(weighted, far)
            plain, weighted = (plain[0] + g, plain[1]), (weighted[0] + w, weighted[1])
    cols = times(plain, value) + times(weighted, value)
    lane = lax.broadcasted_iota(jnp.int32, value[0].shape, 1)
    out = jnp.zeros_like(value[0])
    for k, col in enumerate(cols):
        out = jnp.where(lane == k, jnp.sum(col, 1, keepdims=True), out)
    out = jnp.transpose(out)
    at = 2 * POWERS + 2
    inverse, moment, decay_rate, turn_rate, step_size, w_re, w_im = [modes[at + k : at + k + 1] for k in range(7)]
    c_re, c_im, d_re, d_im = [out[k : k + 1] * inverse for k in range(4)]
    turn_grad = -(w_re * d_im + w_im * d_re)
    decay_grad = ((w_re * c_re - w_im * c_im) * moment - (w_re * d_re - w_im * d_im)) * decay_rate
    result = [decay_grad, turn_grad * step_size, c_re, -c_im, decay_grad + turn_grad * turn_rate]
    return jnp.concatenate(result + [jnp.zeros_like(c_re)] * 3, 0)


def remote(src, dst, send, recv, target):
    return pltpu.make_async_remote_copy(
        src_ref=src, dst_ref=dst, send_sem=send, recv_sem=recv, device_id=target, device_id_type=MESH
    )


def halving_bits(n_chan, n_batch):
    return n_chan.bit_length() + n_batch.bit_length() - 2


def whole(a):
    return pl.BlockSpec(a.shape, lambda t, n=a.ndim: (0,) * n, pipeline_mode=pl.Buffered(1))


ANYWHERE = pl.BlockSpec(memory_space=pl.ANY)
GATHER_ORDER = (((0,), (1, 2), (3,), (4,)), ((0,), (3,), (1, 2), (4,)))


def train_kernel(
    n_chan, n_batch, mask, raw, fs, fl, ts, tl, vec_mine, x_own, cot_own, w_own,
    out_all, in_all, state_all, lin_all, vec_all, cot_all, ker_all, w_all,
    hat_far, pre_far, act_far, sigma_far, slope_far, spec_far,
    params, x_low, hats, pres, acts, sigmas, slopes, specs, stats, streams, ker_spec, spec_grad, mixed, folded, pre_grad, back_low,
    w_near, loaded, sums, vecs, vec_in, ker_rows, ker_low,
    lin_grad, vec_grad, vec_cols, vec_rows, vec_got, vec_own,
    ker_sums, ker_sent, ker_got, lin_sums, lin_sent, lin_got, low_sent, low_got, ker_final, lin_final, state_own,
    move_send, move_recv, move_own, gather_send, gather_recv, gather_own, load_sem, far_sem,
    part_send, part_recv, ready, vec_send, vec_recv, vec_sem, all_send, all_recv, all_own,
):
    step = pl.program_id(0)
    layers, seqs = stats.shape[:2]
    chans = x_low.shape[1]
    own = chans // n_chan
    part = ker_final.shape[1]
    forward_steps = layers * seqs
    me, row, others = peers_of(n_chan)
    rows_of = [lax.rem(row + k, n_batch) for k in range(1, n_batch)]
    above = halving(n_chan, n_batch)
    path = list(reversed(above))
    bits, batch_bits = len(path), n_batch.bit_length() - 1
    total = 1 << bits
    core_bit = path[0][0]
    top, bottom = layers - 1, 0
    mine = pl.ds(pl.multiple_of(me * own, own), own)

    def trade(kind, k, source, dest):
        copies = [pltpu.make_async_copy(source(me), dest, move_own.at[kind, k])]
        for j, other in enumerate(others):
            copies.append(remote(source(other), dest, move_send.at[kind, k, j], move_recv.at[kind, k, j], (row, other)))
        return copies

    def columns(device, k):
        return pl.ds(pl.multiple_of((device * seqs + k) * BUCKET, BUCKET), BUCKET)

    def x_moves(k):
        return trade(0, k, lambda device: x_own.at[:, columns(device, k)], x_low.at[k, mine])

    def cot_moves(k):
        return trade(1, k, lambda device: cot_own.at[:, columns(device, k)], cot_all.at[k, mine])

    def rows_for(device):
        return pl.ds(pl.multiple_of(device * own, own), own)

    def out_moves(k):
        return trade(2, k, lambda device: back_low.at[k, rows_for(device)], out_all.at[:, columns(me, k)])

    def in_moves(k):
        return trade(3, k, lambda device: back_low.at[k, rows_for(device)], in_all.at[:, columns(me, k)])

    def run(copies):
        for copy in copies:
            copy.start()

    def finish_all(copies):
        for copy in copies:
            copy.wait()

    place = tuple(bit for bit, _ in above)

    def held(kind, i, s):
        order = GATHER_ORDER[kind]
        done = [d for group in order[:s] for d in group]
        ref = (ker_all if kind == 0 else w_all).at[i]
        ref = ref.at[tuple(slice(None) if d in done else place[d] for d in range(bits))]
        slot = sum((1 << len(group)) - 1 for group in order[:s])
        copies = []
        for mask in range(1, 1 << len(order[s])):
            chan, batch = me, row
            for t, d in enumerate(order[s]):
                if mask >> t & 1 and d < bits - batch_bits:
                    chan = flip(chan, bits - batch_bits - 1 - d)
                elif mask >> t & 1:
                    batch = flip(batch, bits - 1 - d)
            k, slot = 2 * i + kind, slot + 1
            copies.append(remote(ref, ref, gather_send.at[k, slot - 1], gather_recv.at[k, slot - 1], (batch, chan)))
        return copies

    def gather_next(i, s):
        for kind in (1, 0):
            finish_all(held(kind, i, s))
            if s + 1 < len(GATHER_ORDER[kind]):
                run(held(kind, i, s + 1))

    def vec_in_moves():
        copies = [pltpu.make_async_copy(vec_mine, vec_in.at[me], gather_own.at[2 * layers])]
        for k, other in enumerate(others):
            copies.append(remote(vec_mine, vec_in.at[me], vec_send.at[1, k], vec_recv.at[1, k], (row, other)))
        return copies

    def make_kernels(i):
        def make(h, carry):
            first_row, second_row = kernel_rows(columns_of(params[i * part // 2 + h]))
            ker_rows[2 * h] = first_row
            ker_rows[2 * h + 1] = second_row
            return carry

        lax.fori_loop(0, part // 2, make, 0, unroll=4)
        for k in range(BUCKET // LANES):
            ker_low[i, :, k * LANES : (k + 1) * LANES] = ker_rows[:, k, :].astype(jnp.bfloat16)
        return pltpu.make_async_copy(ker_low.at[i], ker_all.at[(i,) + place], gather_own.at[2 * i])

    def load_kernels(layer):
        copy = pltpu.make_async_copy(ker_all.at[layer].reshape(chans, BUCKET), loaded, load_sem)
        copy.start()
        copy.wait()
        kernel_spectrum(loaded, folded, ker_spec, fs, fl, CONV_ROWS)

    def far_copies(k, back):
        pairs = zip((hats, pres, acts, sigmas, slopes, specs), (hat_far, pre_far, act_far, sigma_far, slope_far, spec_far))
        copies = []
        for j, (near, far) in enumerate(pairs):
            ends = (far.at[k], near.at[k]) if back else (near.at[k], far.at[k])
            copies.append(pltpu.make_async_copy(*ends, far_sem.at[j, k]))
        return copies

    groups = [[0], [1], [2, 3], [4]]
    count, at, gone = [], [0], 0
    for group in groups:
        gone += len(group)
        count.append(total >> gone)
        at.append(at[-1] + count[-1] * ((1 << len(group)) - 1))
    last_stage = len(groups) - 1

    def side(s, mask):
        chan, batch, index = me, row, 0
        for t, dim in enumerate(groups[s]):
            bit = path[dim][0]
            across = mask >> t & 1
            index = index + (1 - bit if across else bit) * (1 << t)
            if across and dim < batch_bits:
                batch = flip(batch, dim)
            elif across:
                chan = flip(chan, dim - batch_bits)
        return (batch, chan), index

    def masks(s):
        return range(1, 1 << len(groups[s]))

    def kept_rows(b):
        return spec_grad[pl.ds(pl.multiple_of(b * part, part), part), :BUCKET]

    def sums_at(s):
        return sum(count[1 : s + 1])

    def slot(kind, s, mask, sent):
        first = (mask - 1) * count[s]
        if kind == 0 or s == 0:
            return at[s] + first
        if s == LOW_STAGE:
            return first
        return first + at[s] - at[LOW_STAGE + 1] + (0 if sent else at[LOW_STAGE])

    def stage(kind, layer, s, mask):
        to, got = pl.ds(slot(kind, s, mask, True), count[s]), pl.ds(slot(kind, s, mask, False), count[s])
        if kind == 0:
            src, dst = ker_sent.at[to], ker_got.at[got]
        elif s == 0:
            src, dst = lin_grad.at[layer, :, 1 - core_bit], lin_got.at[got]
        elif s == LOW_STAGE:
            src, dst = low_sent.at[to], low_got.at[got]
        else:
            src, dst = lin_sent.at[to], lin_got.at[got]
        k = at_peer[s] + mask - 1
        return remote(src, dst, part_send.at[kind, k], part_recv.at[kind, k], side(s, mask)[0])

    at_peer = [0]
    for s in range(len(groups)):
        at_peer.append(at_peer[-1] + (1 << len(groups[s])) - 1)

    def begin(kind, layer, s):
        for mask in masks(s):
            if layer != layers - 1:
                pl.semaphore_wait(ready.at[kind, at_peer[s] + mask - 1], 1)
            stage(kind, layer, s, mask).start()

    def advance(kind, layer, s):
        for mask in masks(s):
            stage(kind, layer, s, mask).wait()

        def value(b):
            if kind == 0:
                result = kept_rows(b) if s == 0 else ker_sums[sums_at(s - 1) + b]
            else:
                result = lin_grad[layer, b, core_bit] if s == 0 else lin_sums[sums_at(s - 1) + b]
            for mask in masks(s):
                got = ker_got if kind == 0 else low_got if s == LOW_STAGE else lin_got
                result = result + got[slot(kind, s, mask, False) + b].astype(jnp.float32)
            return result

        if s == last_stage:
            final = ker_final if kind == 0 else lin_final
            final[layer] = value(0)
        else:
            wide = 1 << len(groups[s + 1])

            def one(b, carry):
                sums = ker_sums if kind == 0 else lin_sums
                sums[sums_at(s) + b] = value(wide * b + side(s + 1, 0)[1])
                for mask in masks(s + 1):
                    moved = value(wide * b + side(s + 1, mask)[1])
                    to = slot(kind, s + 1, mask, True) + b
                    if kind == 0:
                        ker_sent[to] = moved.astype(jnp.bfloat16)
                    elif s + 1 == LOW_STAGE:
                        low_sent[to] = moved.astype(jnp.bfloat16)
                    else:
                        lin_sent[to] = moved
                return carry

            lax.fori_loop(0, count[s + 1], one, 0)
        if layer == layers - 1:
            for mask in masks(s):
                there = side(s, mask)[0]
                pl.semaphore_signal(ready.at[kind, at_peer[s] + mask - 1], inc=1, device_id=there, device_id_type=MESH)
        if s < last_stage:
            begin(kind, layer, s + 1)

    def spread(own_ref, everyone, k):
        copies = [pltpu.make_async_copy(own_ref, everyone.at[row], all_own.at[k])]
        for j, other in enumerate(rows_of):
            copies.append(remote(own_ref, everyone.at[row], all_send.at[k, j], all_recv.at[k, j], (other, me)))
        return copies

    def spreads(kind, layer):
        if kind == 0:
            half = pl.ds(layer * part // 2, part // 2)
            return spread(state_own.at[half], state_all.at[:, half], layer)
        return spread(lin_final.at[layer], lin_all.at[:, layer], layers + layer)

    def vec_moves():
        copies = [pltpu.make_async_copy(vec_rows.at[me], vec_got.at[me], vec_sem)]
        for k, other in enumerate(others):
            copies.append(remote(vec_rows.at[other], vec_got.at[me], vec_send.at[0, k], vec_recv.at[0, k], (row, other)))
        return copies

    def states(layer):
        def one(h, carry):
            at = layer * part // 2 + h
            state_own[at] = state_rows(params[at], [ker_final[layer, pl.ds(2 * h + c, 1), :] for c in range(2)])
            return carry

        lax.fori_loop(0, part // 2, one, 0, unroll=4)

    @pl.when(step == 0)
    def _():
        locals_ = [pltpu.make_async_copy(w_own.at[i], w_all.at[(i,) + place], gather_own.at[2 * i + 1]) for i in range(layers)]

        def prepare():
            run(locals_)
            for k, value in enumerate(mode_rows([raw[k] for k in range(5)])):
                params[:, k, :] = value
            copy = make_kernels(0)
            copy.start()
            finish_all(locals_ + [copy])

        greet([(row, other) for other in others] + [(other, me) for other in rows_of], prepare)
        run(held(0, 0, 0) + held(1, 0, 0) + vec_in_moves())
        moves = x_moves(0)
        run(moves[:4])
        gather_next(0, 0)
        run(moves[4:])
        for i in range(1, layers):
            copy = make_kernels(i)
            copy.start()
            copy.wait()
        gather_next(0, 1)
        gather_next(0, 2)
        run(x_moves(1))
        for i in range(1, layers):
            run(held(1, i, 0) + held(0, i, 0))
        gather_next(0, 3)
        finish_all(vec_in_moves())
        for i in range(layers):
            for c in range(n_chan):
                vecs[i, c * own : (c + 1) * own, :] = columns_of(vec_in[c, 8 * i : 8 * i + 8, :])[:own]
        vec_cols[...] = jnp.zeros_like(vec_cols)
        finish_all(x_moves(0))

    @pl.when(step == 1)
    def _():
        for k in range(1, seqs):
            finish_all(x_moves(k))
        run(cot_moves(0))

    @pl.when(step < forward_steps)
    def _():
        layer, seq = lax.div(step, seqs), lax.rem(step, seqs)
        stream, hat_out, pre_out, act_out = streams.at[seq], hats.at[seq], pres.at[seq], acts.at[seq]
        sigma_out, slope_out, spec_out, first = sigmas.at[seq], slopes.at[seq], specs.at[seq], x_low.at[seq]
        stat, vec, weight = stats.at[layer, seq], vecs.at[layer], w_near.at[layer]
        hat, mixed = pre_grad, spec_grad

        @pl.when(layer == 0)
        def _():
            def widen(rows, _):
                stream[rows, :] = first[rows, :].astype(jnp.float32)

            steps(chans, STEP_ROWS, widen)

        @pl.when(seq == 0)
        def _():
            copy = pltpu.make_async_copy(w_all.at[layer].reshape(2 * chans, chans), weight, load_sem)
            copy.start()
            copy.wait()
            load_kernels(layer)

        @pl.when(layer > 0)
        def _():
            finish_all(far_copies(seq, False))

        mean_val, inv_std = token_stats(stream, chans)
        stat[0:1, :] = mean_val
        stat[1:2, :] = inv_std

        def normalise(rows, _):
            v = (stream[rows, :] - stat[0:1, :]) * stat[1:2, :]
            hat[rows, :] = v
            hat_out[rows, :] = v.astype(hat_out.dtype)
            v = v * vec[rows, GAIN : GAIN + 1] + vec[rows, SHIFT : SHIFT + 1]
            put_folded(folded, rows, fold(*quarters(v)))

        steps(chans, STEP_ROWS, normalise)

        @pl.when(step == forward_steps - 2)
        def _():
            for k in range(1, seqs):
                run(cot_moves(k))

        def convolve(rows, _):
            for g, (at, width) in enumerate(GROUPS):
                spec = dot(get_folded(folded, rows, at, width), table_of(fs, fl, g))
                spec_out[rows, at : at + width] = spec.astype(jnp.bfloat16)
                both = product(ker_spec[rows, at : at + width], spec, g == 0, False)
                mixed[rows, at : at + width] = dot(both.astype(jnp.bfloat16), table_of(ts, tl, g))

        steps(chans, CONV_ROWS, convolve)

        @pl.when(step == 0)
        def _():
            gather_next(1, 0)

        @pl.when(step == 1)
        def _():
            gather_next(1, 2)

        def activate(rows, _):
            gain, shift, skip = [vec[rows, k : k + 1] for k in (GAIN, SHIFT, SKIP)]
            gain, shift = gain * skip, shift * skip
            for q, value in enumerate(get_unfolded(mixed, rows)):
                cols = slice(q * QUARTER, (q + 1) * QUARTER)
                pre = value + (gain * hat[rows, cols] + shift)
                pre_out[rows, cols] = pre.astype(pre_out.dtype)
                soft = jnp.tanh(pre * (GELU_A + GELU_B * (pre * pre)))
                act_out[rows, cols] = (0.5 * pre * (1.0 + soft)).astype(jnp.bfloat16)

        steps(chans, STEP_ROWS, activate)

        block = 2 * LIN_ROWS
        for t in range(4):
            cols = slice(t * QUARTER, (t + 1) * QUARTER)

            def linear(rows, k, cols=cols):
                mixed[:block, :QUARTER] = dot(weight[rows, :], act_out[:, cols])
                for o in range(LIN_ROWS // 16):
                    at = pl.ds(pl.multiple_of(k * LIN_ROWS + o * 16, 16), 16)
                    gate = mixed[o * 32 : o * 32 + 16, :QUARTER] + vec[at, BIAS_IN : BIAS_IN + 1]
                    value = mixed[o * 32 + 16 : o * 32 + 32, :QUARTER] + vec[at, BIAS_VAL : BIAS_VAL + 1]
                    sigma = 0.5 * jnp.tanh(0.5 * value) + 0.5
                    gated = gate * sigma
                    sigma_out[at, cols] = sigma.astype(sigma_out.dtype)
                    slope_out[at, cols] = (gated - gated * sigma).astype(slope_out.dtype)
                    moved = stream[at, cols] + mask[seq, :, cols] * gated
                    stream[at, cols] = moved
                    back_low[seq, at, cols] = (moved - first[at, cols].astype(jnp.float32)).astype(jnp.bfloat16)

            steps(2 * chans, block, linear)

        @pl.when(step == 0)
        def _():
            gather_next(1, 1)

        @pl.when(step == 1)
        def _():
            gather_next(1, 3)

        @pl.when(layer == 0)
        def _():
            run(far_copies(seq, False))

    @pl.when(step >= forward_steps)
    def _():
        turn, seq = lax.div(step - forward_steps, seqs), lax.rem(step - forward_steps, seqs)
        layer = layers - 1 - turn
        back, hat, pre, act = streams.at[seq], hats.at[seq], pres.at[seq], acts.at[seq]
        sigma_in, slope_in, spec, first = sigmas.at[seq], slopes.at[seq], specs.at[seq], x_low.at[seq]
        stat, vec = stats.at[layer, seq], vecs.at[layer]
        next_layer = (turn == 1) & (seq == 0)
        ends = (turn == layers - 1) & (seq == seqs - 1)

        for k in range(seqs):

            @pl.when((turn == 0) & (seq == k))
            def _(k=k):
                finish_all(cot_moves(k))
                copy = pltpu.make_async_copy(cot_all.at[k], x_low.at[k], load_sem)
                copy.start()
                if k > 0:
                    run(out_moves(k))
                copy.wait()

            @pl.when((turn == 1) & (seq == k))
            def _(k=k):
                finish_all(far_copies(k, True))

        @pl.when((turn == 0) & (seq > 0))
        def _():
            run(far_copies(seq - 1, True))

        @pl.when((turn == 1) & (seq == 0))
        def _():
            run(far_copies(seqs - 1, True))

        @pl.when(turn == 0)
        def _():
            def widen(rows, _):
                back[rows, :] = first[rows, :].astype(jnp.float32)

            steps(chans, STEP_ROWS, widen)

        @pl.when(seq == 0)
        def _():
            @pl.when(turn > 0)
            def _():
                load_kernels(layer)

            for k in range(4):
                cols = slice(k * QUARTER, (k + 1) * QUARTER)
                loaded[:, cols] = jnp.transpose(w_near[layer, cols, :])
            vec_grad[...] = jnp.zeros_like(vec_grad)

        def gates(rows, k):
            gated = back[rows, :] * mask[seq]
            left = (gated * sigma_in[rows, :].astype(jnp.float32)).astype(jnp.bfloat16)
            right = (gated * slope_in[rows, :].astype(jnp.float32)).astype(jnp.bfloat16)
            at = pl.multiple_of(k * 32, 32)
            folded[pl.ds(at, 16), :] = left
            folded[pl.ds(at + 16, 16), :] = right
            vec_grad[3, rows, :] += lanes(left.astype(jnp.float32))
            vec_grad[4, rows, :] += lanes(right.astype(jnp.float32))

        steps(chans, STEP_ROWS, gates)

        width = 2 * chans // total
        blocks = MAT_ROWS // (2 * width)

        def lin_back(rows, k):
            value = lax.dot_general(
                folded[rows, :], act[...], (((1,), (1,)), ((), ())), preferred_element_type=jnp.float32
            ).reshape(blocks, 2, width, chans)
            at = pl.ds(k * blocks, blocks)

            @pl.when(seq == 0)
            def _():
                lin_grad[layer, at] = value

            @pl.when(seq > 0)
            def _():
                lin_grad[layer, at] += value

        steps(2 * chans, MAT_ROWS, lin_back)

        @pl.when(ends)
        def _():
            begin(1, bottom, 0)

        def act_back(rows, _):
            for t in range(4):
                cols = slice(t * QUARTER, (t + 1) * QUARTER)
                pre_grad[rows, cols] = dot(loaded[rows, :], folded[:, cols])

        steps(chans, MAT_ROWS, act_back)

        def gelu_back(rows, _):
            skip_sum = jnp.zeros((STEP_ROWS, 128), jnp.float32)
            outs = []
            for q in range(4):
                cols = slice(q * QUARTER, (q + 1) * QUARTER)
                p = pre[rows, cols].astype(jnp.float32)
                square = p * p
                soft = jnp.tanh(p * (GELU_A + GELU_B * square))
                slope = 0.5 * (1.0 + soft) + (0.5 * p) * (1.0 - soft * soft) * (GELU_A + (3.0 * GELU_B) * square)
                grad = pre_grad[rows, cols] * slope
                pre_grad[rows, cols] = grad
                norm = hat[rows, cols].astype(jnp.float32) * vec[rows, GAIN : GAIN + 1] + vec[rows, SHIFT : SHIFT + 1]
                skip_sum = skip_sum + lanes(grad * norm)
                outs.append(grad)
            vec_grad[2, rows, :] += skip_sum
            put_folded(folded, rows, fold(*outs))

        steps(chans, STEP_ROWS, gelu_back)

        @pl.when((turn == 0) & (seq == 0))
        def _():
            run(out_moves(0))

        @pl.when(next_layer)
        def _():
            for kind in (0, 1):
                advance(kind, top, 0)

        sums[...] = jnp.zeros_like(sums)

        @pl.when(seq == 0)
        def _():
            spec_grad[...] = jnp.zeros_like(spec_grad)

        def correlate(rows, chunk):
            for g, (at, width) in enumerate(GROUPS):
                grad = dot(get_folded(folded, rows, at, width), table_of(fs, fl, g))
                spec_grad[rows, at : at + width] += product(
                    spec[rows, at : at + width].astype(jnp.float32), grad, g == 0, True
                )
                both = product(ker_spec[rows, at : at + width], grad, g == 0, True)
                mixed[:, at : at + width] = dot(both.astype(jnp.bfloat16), table_of(ts, tl, g))

            def norm_back(k, carry):
                here = pl.ds(pl.multiple_of(k * STEP_ROWS, STEP_ROWS), STEP_ROWS)
                rows = pl.ds(pl.multiple_of(chunk * CHUNK_ROWS + k * STEP_ROWS, STEP_ROWS), STEP_ROWS)
                skip = vec[rows, SKIP : SKIP + 1]
                gain = vec[rows, GAIN : GAIN + 1]
                gain_sum = jnp.zeros((STEP_ROWS, 128), jnp.float32)
                shift_sum = jnp.zeros((STEP_ROWS, 128), jnp.float32)
                plain, weighted = [], []
                for q, part in enumerate(get_unfolded(mixed, here)):
                    cols = slice(q * QUARTER, (q + 1) * QUARTER)
                    grad = part + skip * pre_grad[rows, cols]
                    both = grad * hat[rows, cols].astype(jnp.float32)
                    gain_sum = gain_sum + lanes(both)
                    shift_sum = shift_sum + lanes(grad)
                    cent = grad * gain
                    pre_grad[rows, cols] = cent
                    both = both * gain
                    plain.append(cent[:8] + cent[8:])
                    weighted.append(both[:8] + both[8:])
                vec_grad[0, rows, :] += gain_sum
                vec_grad[1, rows, :] += shift_sum
                return carry[0] + jnp.concatenate(plain, 1), carry[1] + jnp.concatenate(weighted, 1)

            zero = jnp.zeros((8, BUCKET), jnp.float32)
            plain, weighted = lax.fori_loop(0, CHUNK_ROWS // STEP_ROWS, norm_back, (zero, zero), unroll=2)
            sums[0:8, :] += plain
            sums[8:16, :] += weighted

        steps(chans, CHUNK_ROWS, correlate)

        @pl.when(seq == seqs - 1)
        def _():
            def to_time(rows, _):
                for g, (at, width) in enumerate(GROUPS):
                    low = spec_grad[rows, at : at + width].astype(jnp.bfloat16)
                    ker_spec[rows, at : at + width] = dot(low, table_of(ts, tl, g))

            steps(chans, CONV_ROWS, to_time)

            def block_rows(b):
                return pl.ds(pl.multiple_of(b * part, part), part)

            def write(b, carry):
                for q, value in enumerate(get_unfolded(ker_spec, block_rows(2 * b + core_bit))):
                    spec_grad[block_rows(b), q * QUARTER : (q + 1) * QUARTER] = value
                for q, value in enumerate(get_unfolded(ker_spec, block_rows(2 * b + 1 - core_bit))):
                    ker_sent[b, :, q * QUARTER : (q + 1) * QUARTER] = value.astype(jnp.bfloat16)
                return carry

            lax.fori_loop(0, total // 2, write, 0)

        for i in range(layers):

            @pl.when((turn == i) & (seq == seqs - 1))
            def _(i=i):
                layer = layers - 1 - i
                begin(0, layer, 0)
                if layer == layers - 1:
                    begin(1, layer, 0)
                else:
                    advance(1, layer, 0)
                    for kind in (0, 1):
                        advance(kind, top, 2)

        mean_plain = jnp.sum(sums[0:8, :], 0, keepdims=True) / chans
        mean_weighted = jnp.sum(sums[8:16, :], 0, keepdims=True) / chans
        sums[0:1, :] = mean_plain
        sums[8:9, :] = mean_weighted

        @pl.when(next_layer)
        def _():
            for kind in (0, 1):
                advance(kind, top, 1)

        for k in range(seqs):

            @pl.when((turn == layers - 1) & (seq == k))
            def _(k=k):
                finish_all(out_moves(k))

        def finish(rows, _):
            scaled = hat[rows, :].astype(jnp.float32) * sums[8:9, :]
            moved = back[rows, :] + stat[1:2, :] * (pre_grad[rows, :] - sums[0:1, :] - scaled)
            back[rows, :] = moved

        def leave(rows, _):
            scaled = hat[rows, :].astype(jnp.float32) * sums[8:9, :]
            moved = back[rows, :] + stat[1:2, :] * (pre_grad[rows, :] - sums[0:1, :] - scaled)
            back_low[seq, rows, :] = (moved - first[rows, :].astype(jnp.float32)).astype(jnp.bfloat16)

        @pl.when(turn < layers - 1)
        def _():
            steps(chans, STEP_ROWS, finish)

        @pl.when(turn == layers - 1)
        def _():
            steps(chans, STEP_ROWS, leave)

        for k in range(seqs):

            @pl.when((turn == layers - 1) & (seq == k))
            def _(k=k):
                run(in_moves(k))

        for i in range(layers):

            @pl.when((turn == i) & (seq == seqs - 1))
            def _(i=i):
                layer = layers - 1 - i

                def vec_columns(rows, _):
                    lane = lax.broadcasted_iota(jnp.int32, (STEP_ROWS, LANES), 1)
                    out = vec_cols[rows, :]
                    for kind in range(5):
                        out = jnp.where(lane == layer * 5 + kind, jnp.sum(vec_grad[kind, rows, :], 1, keepdims=True), out)
                    vec_cols[rows, :] = out

                steps(chans, STEP_ROWS, vec_columns)

        @pl.when(ends)
        def _():
            for c in range(n_chan):
                vec_rows[c] = columns_of(vec_cols[c * own : (c + 1) * own, :])[:16]
            run(vec_moves())
            advance(0, bottom, 0)
            advance(1, bottom, 1)
            for kind in (0, 1):
                advance(kind, top, last_stage)
            run(spreads(1, top))
            advance(0, bottom, 1)
            states(top)
            run(spreads(0, top))
            finish_all(vec_moves())
            vec_own[...] = jnp.sum(vec_got[...], 0)
            run(spread(vec_own, vec_all, 2 * layers))
            for s in range(2, last_stage + 1):
                for kind in (1, 0):
                    advance(kind, bottom, s)
            run(spreads(1, bottom))
            states(bottom)
            run(spreads(0, bottom))
            for k in range(seqs):
                finish_all(in_moves(k))
            for i in range(layers):
                for copy in spreads(0, i) + spreads(1, i):
                    copy.wait()
            for copy in spread(vec_own, vec_all, 2 * layers):
                copy.wait()


def train(mask, raw, tables, vec_mine, x_own, cot_own, w_own, n_chan, n_batch):
    own, group = x_own.shape
    chans, toks = own * n_chan, group // n_chan
    seqs, layers = toks // BUCKET, w_own.shape[0]
    bits = halving_bits(n_chan, n_batch)
    total = 1 << bits
    part = chans // total
    low_count, peers = total >> (LOW_STAGE + 1), bits + 1
    shape, low, full = jax.ShapeDtypeStruct, jnp.bfloat16, jnp.float32
    vmem, dma = pltpu.VMEM, pltpu.SemaphoreType.DMA
    there = (2,) * bits
    slots, wide = (seqs, chans, BUCKET), (seqs, chans, 2 * BUCKET)
    return pl.pallas_call(
        functools.partial(train_kernel, n_chan, n_batch),
        grid=(2 * layers * seqs,),
        in_specs=[whole(a) for a in (mask, raw, *tables, vec_mine)] + [ANYWHERE] * 3,
        out_specs=[ANYWHERE] * 14,
        out_shape=[
            shape((own, group), low),
            shape((own, group), low),
            shape((n_batch, layers * part // 2, 8, LANES), full),
            shape((n_batch, layers, 2 * part, chans), full),
            shape((n_batch, 16, LANES), full),
            shape(slots, low),
            shape((layers,) + there + (part, BUCKET), low),
            shape((layers,) + there + (2 * part, chans), low),
        ]
        + [shape(slots, low)] * 5
        + [shape(wide, low)],
        scratch_shapes=[vmem((layers * part // 2, 32, LANES), full)]
        + [vmem(slots, low)] * 6
        + [
            vmem(wide, low),
            vmem((layers, seqs, 8, BUCKET), full),
            vmem(slots, full),
            vmem((chans, 2 * BUCKET), full),
            vmem((chans, 2 * BUCKET), full),
            vmem((CHUNK_ROWS, 2 * BUCKET), full),
            vmem((2 * chans, BUCKET), low),
            vmem((chans, BUCKET), full),
            vmem(slots, low),
            vmem((layers, 2 * chans, chans), low),
            vmem((chans, BUCKET), low),
            vmem((16, BUCKET), full),
            vmem((layers, chans, LANES), full),
            vmem((n_chan, 16, LANES), full),
            vmem((part, BUCKET // LANES, LANES), full),
            vmem((layers, part, BUCKET), low),
            vmem((layers, total // 2, 2, 2 * part, chans), full),
            vmem((5, chans, LANES), full),
            vmem((chans, LANES), full),
            vmem((n_chan, 16, LANES), full),
            vmem((n_chan, 16, LANES), full),
            vmem((16, LANES), full),
            vmem((3 * total // 8, part, BUCKET), full),
            vmem((total, part, BUCKET), low),
            vmem((total, part, BUCKET), low),
            vmem((3 * total // 8, 2 * part, chans), full),
            vmem((low_count, 2 * part, chans), full),
            vmem((total - low_count, 2 * part, chans), full),
            vmem((low_count, 2 * part, chans), low),
            vmem((low_count, 2 * part, chans), low),
            vmem((layers, part, BUCKET), full),
            vmem((layers, 2 * part, chans), full),
            vmem((layers * part // 2, 8, LANES), full),
            dma((4, seqs, n_chan - 1)), dma((4, seqs, n_chan - 1)), dma((4, seqs)),
            dma((2 * layers, peers)), dma((2 * layers, peers)), dma((2 * layers + 1,)),
            dma, dma((6, seqs)),
            dma((2, peers)), dma((2, peers)), pltpu.SemaphoreType.REGULAR((2, peers)),
            dma((2, n_chan - 1)), dma((2, n_chan - 1)), dma,
            dma((2 * layers + 1, n_batch - 1)), dma((2 * layers + 1, n_batch - 1)), dma((2 * layers + 1,)),
        ],
        compiler_params=pltpu.CompilerParams(vmem_limit_bytes=ROOM, collective_id=1, has_side_effects=True),
        cost_estimate=pl.CostEstimate(flops=60 * 10**9, bytes_accessed=60 * 2**20, transcendentals=0),
        name="train",
    )(mask, raw, *tables, vec_mine, x_own, cot_own, w_own)


def adam(weight, grad, first, second, rate):
    first_new = 0.9 * first + 0.1 * grad
    second_new = 0.999 * second + 0.001 * grad * grad
    fixed_first = first_new / (1.0 - 0.9**STEP)
    fixed_second = second_new / (1.0 - 0.999**STEP)
    new_weight = weight - rate * (fixed_first / (jnp.sqrt(fixed_second) + 1e-08) + 0.01 * weight)
    return (first_new, second_new, new_weight)


def local(
    inputs, lengths, cotangent, ln_gain, ln_bias, log_step, skip_gain, lin_bias, log_decay, frequency,
    w_re, w_im, lin_weight, lin_moment, lin_square, vec_moment, vec_square, state_moment, state_square,
):
    n_chan = lax.axis_size("chan")
    n_batch = lax.axis_size("batch")
    own = inputs.shape[0]
    chans = own * n_chan
    toks = inputs.shape[1] // n_chan
    seqs = toks // BUCKET
    part = own // n_batch
    me = lax.axis_index("chan")
    row = lax.axis_index("batch")
    lens = lax.dynamic_slice_in_dim(lengths, me * seqs, seqs)
    places = lax.iota(jnp.int32, BUCKET)
    valid = (places[None, :] < lens[:, None]).astype(jnp.float32).reshape(seqs, 1, BUCKET)
    tables = tuple(jnp.asarray(t) for t in transform_tables())

    def mine(a):
        return lax.dynamic_slice_in_dim(a, row * part, part, 1)

    step_all = jnp.broadcast_to(log_step[..., None], log_decay.shape)
    raw = jnp.stack([mine(a) for a in (log_decay, frequency, w_re, w_im, step_all)])
    raw = raw.reshape(5, LAYERS * part // 2, LANES)
    w_own = mine(lin_weight).transpose(0, 2, 1, 3).reshape(LAYERS, 2 * part, chans).astype(jnp.bfloat16)
    vec_own = jnp.stack([ln_gain, ln_bias, skip_gain, lin_bias[:, 0], lin_bias[:, 1]], 1)
    vec_own = jnp.pad(vec_own, ((0, 0), (0, 3), (0, LANES - own))).reshape(8 * LAYERS, LANES)
    out_delta, in_delta, state_all, lin_all, vec_all, *_ = train(
        valid, raw, tables, vec_own, inputs, cotangent, w_own, n_chan, n_batch
    )
    output = inputs.astype(jnp.float32) + out_delta.astype(jnp.float32)
    input_grad = cotangent.astype(jnp.float32) + in_delta.astype(jnp.float32)

    state_all = state_all.reshape(n_batch, LAYERS, part // 2, 8, 2, LANES // 2)
    state_all = state_all.transpose(1, 3, 0, 2, 4, 5).reshape(LAYERS, 8, own, -1)
    state_total = state_all[:, :4]
    step_total = jnp.sum(state_all[:, 4], -1)
    lin_total = lin_all.reshape(n_batch, LAYERS, 2, part, chans).transpose(1, 0, 3, 2, 4).reshape(LAYERS, own, 2, chans)
    vec_sum = jnp.sum(vec_all, 0)[: 5 * LAYERS, :own].reshape(LAYERS, 5, own)
    vec_total = jnp.stack([vec_sum[:, 0], vec_sum[:, 1], step_total, vec_sum[:, 2], vec_sum[:, 3], vec_sum[:, 4]], 1)

    vec_old = jnp.stack([ln_gain, ln_bias, log_step, skip_gain, lin_bias[:, 0], lin_bias[:, 1]], 1)
    state_old = jnp.stack([log_decay, frequency, w_re, w_im], 1)
    lin_first, lin_second, lin_new = adam(lin_weight, lin_total, lin_moment, lin_square, 0.05)
    vec_first, vec_second, vec_new = adam(vec_old, vec_total, vec_moment, vec_square, 0.2)
    state_first, state_second, state_new = adam(state_old, state_total, state_moment, state_square, 0.2)
    return (
        output, input_grad, lin_first, lin_second, lin_new, vec_first, vec_second, vec_new,
        state_first, state_second, state_new,
    )


def tables(length):
    full_width = 2 * length
    row_ids = lax.iota(jnp.int32, length)[:, None]
    col_ids = lax.iota(jnp.int32, length)[None, :]
    turn_all = (row_ids * col_ids % full_width).astype(jnp.float32) * (2.0 * math.pi / full_width)
    cosine = jnp.cos(turn_all)
    sine_table = jnp.sin(turn_all)
    weights = jnp.where(lax.iota(jnp.int32, length) == 0, 1.0, 2.0).astype(jnp.float32)[None, :]
    alternate = (1 - 2 * (lax.iota(jnp.int32, length) % 2)).astype(jnp.float32)
    return (cosine, sine_table, cosine * weights, sine_table * weights, alternate)


def mixer(normed, log_decay, frequency, w_re, w_im, log_step, skip_gain):
    top_prec = lax.Precision.HIGHEST
    chan_count = normed.shape[0]
    seq_count = normed.shape[1] // BUCKET
    step_size = jnp.exp(log_step)[:, None]
    decay_rate = step_size * jnp.exp(log_decay)
    turn_rate = step_size * frequency
    places = lax.iota(jnp.float32, BUCKET)
    decay_all = jnp.exp(-decay_rate[..., None] * places)
    soft = decay_all / jnp.sum(decay_all, -1, keepdims=True)
    phase_all = turn_rate[..., None] * places
    kernel = jnp.sum(
        (w_re[..., None] * jnp.cos(phase_all) - w_im[..., None] * jnp.sin(phase_all)) * soft, 1
    )
    cosine, sine_table, cos_back, sin_back, alternate = tables(BUCKET)
    signal = normed.reshape(chan_count, seq_count, BUCKET)
    sig_re = jnp.einsum("csl,lk->csk", signal, cosine, precision=top_prec)
    sig_im = -jnp.einsum("csl,lk->csk", signal, sine_table, precision=top_prec)
    sig_top = jnp.sum(signal * alternate, -1)
    ker_re = jnp.dot(kernel, cosine, precision=top_prec)[:, None, :]
    ker_im = -jnp.dot(kernel, sine_table, precision=top_prec)[:, None, :]
    ker_top = jnp.sum(kernel * alternate, -1)[:, None]
    prod_re = sig_re * ker_re - sig_im * ker_im
    prod_im = sig_re * ker_im + sig_im * ker_re
    prod_top = sig_top * ker_top
    conv_out = jnp.einsum("csk,lk->csl", prod_re, cos_back, precision=top_prec)
    conv_out = conv_out - jnp.einsum("csk,lk->csl", prod_im, sin_back, precision=top_prec)
    conv_out = conv_out + prod_top[..., None] * alternate
    conv_out = conv_out / (2.0 * BUCKET)
    pre_act = conv_out.reshape(normed.shape) + skip_gain[:, None] * normed
    return jax.nn.gelu(pre_act)


def wide_local(
    inputs,
    lengths,
    cotangent,
    ln_gain,
    ln_bias,
    log_step,
    skip_gain,
    lin_bias,
    log_decay,
    frequency,
    w_re,
    w_im,
    lin_weight,
    lin_moment,
    lin_square,
    vec_moment,
    vec_square,
    state_moment,
    state_square,
):
    chan_total = inputs.shape[0] * lax.axis_size("chan")
    tok_count = inputs.shape[1]
    places = lax.iota(jnp.int32, BUCKET)
    valid = (places[None, :] < lengths[:, None]).astype(jnp.float32).reshape(1, tok_count)
    weights_low = lin_weight.astype(jnp.bfloat16)
    stream = inputs.astype(jnp.float32)
    saved = []
    for layer_idx in range(LAYERS):
        sums = lax.psum((jnp.sum(stream, 0), jnp.sum(stream * stream, 0)), "chan")
        mean_val = sums[0] / chan_total
        variance = sums[1] / chan_total - mean_val * mean_val
        inv_std = lax.rsqrt(variance + 1e-05)[None, :]
        centred = (stream - mean_val[None, :]) * inv_std
        normed = centred * ln_gain[layer_idx][:, None] + ln_bias[layer_idx][:, None]
        activated, mixer_back = jax.vjp(
            mixer,
            normed,
            log_decay[layer_idx],
            frequency[layer_idx],
            w_re[layer_idx],
            w_im[layer_idx],
            log_step[layer_idx],
            skip_gain[layer_idx],
        )
        act_low = activated.astype(jnp.bfloat16)
        act_all = lax.all_gather(act_low, "chan", axis=0, tiled=True)
        mixed = jnp.einsum(
            "ht,cjh->cjt", act_all, weights_low[layer_idx], preferred_element_type=jnp.float32
        )
        kept = act_all
        mixed = mixed + lin_bias[layer_idx].T[:, :, None]
        gate_in = mixed[:, 0]
        gate_val = mixed[:, 1]
        stream = stream + valid * gate_in * jax.nn.sigmoid(gate_val)
        saved.append((centred, inv_std, mixer_back, kept, gate_in, gate_val))
    back_stream = cotangent.astype(jnp.float32)
    lin_grads = [None] * LAYERS
    vec_grads = [None] * LAYERS
    state_grads = [None] * LAYERS
    for layer_idx in reversed(range(LAYERS)):
        centred, inv_std, mixer_back, kept, gate_in, gate_val = saved[layer_idx]
        sigma = jax.nn.sigmoid(gate_val)
        gated_back = back_stream * valid
        grad_mixed = jnp.stack(
            [gated_back * sigma, gated_back * gate_in * sigma * (1.0 - sigma)], 1
        ).astype(jnp.bfloat16)
        bias_grad = jnp.sum(grad_mixed.astype(jnp.float32), 2).T
        weight_grad = jnp.einsum(
            "ht,cjt->cjh", kept, grad_mixed, preferred_element_type=jnp.float32
        )
        act_part = jnp.einsum(
            "cjt,cjh->ht", grad_mixed, weights_low[layer_idx], preferred_element_type=jnp.float32
        )
        act_grad = lax.psum_scatter(act_part, "chan", scatter_dimension=0, tiled=True)
        normed_grad, decay_grad, freq_grad, re_grad, im_grad, step_grad, skip_grad = mixer_back(
            act_grad
        )
        gain_grad = jnp.sum(normed_grad * centred, 1)
        shift_grad = jnp.sum(normed_grad, 1)
        centred_grad = normed_grad * ln_gain[layer_idx][:, None]
        back_sums = lax.psum((jnp.sum(centred_grad, 0), jnp.sum(centred_grad * centred, 0)), "chan")
        back_stream = back_stream + inv_std * (
            centred_grad
            - back_sums[0][None, :] / chan_total
            - centred * back_sums[1][None, :] / chan_total
        )
        lin_grads[layer_idx] = weight_grad
        vec_grads[layer_idx] = jnp.stack(
            [gain_grad, shift_grad, step_grad, skip_grad, bias_grad[0], bias_grad[1]]
        )
        state_grads[layer_idx] = jnp.stack([decay_grad, freq_grad, re_grad, im_grad])
    lin_total, vec_total, state_total = lax.psum(
        (jnp.stack(lin_grads), jnp.stack(vec_grads), jnp.stack(state_grads)), "batch"
    )
    vec_old = jnp.stack([ln_gain, ln_bias, log_step, skip_gain, lin_bias[:, 0], lin_bias[:, 1]], 1)
    state_old = jnp.stack([log_decay, frequency, w_re, w_im], 1)
    lin_first, lin_second, lin_new = adam(lin_weight, lin_total, lin_moment, lin_square, 0.05)
    vec_first, vec_second, vec_new = adam(vec_old, vec_total, vec_moment, vec_square, 0.2)
    state_first, state_second, state_new = adam(
        state_old, state_total, state_moment, state_square, 0.2
    )
    return (
        stream,
        back_stream,
        lin_first,
        lin_second,
        lin_new,
        vec_first,
        vec_second,
        vec_new,
        state_first,
        state_second,
        state_new,
    )


def suits(own_seqs, chans, n_chan, n_batch):
    powers = n_chan & (n_chan - 1) == 0 and n_batch & (n_batch - 1) == 0
    return powers and own_seqs == 2 * n_chan and (n_chan, n_batch) == (8, 4) and chans == 16 * n_chan * n_batch


def solution(mesh):
    in_specs = (
        P("chan", "batch"),
        P("batch"),
        P("chan", "batch"),
        P(None, "chan"),
        P(None, "chan"),
        P(None, "chan"),
        P(None, "chan"),
        P(None, None, "chan"),
        P(None, "chan", None),
        P(None, "chan", None),
        P(None, "chan", None),
        P(None, "chan", None),
        P(None, "chan", None, None),
        P(None, "chan", None, None),
        P(None, "chan", None, None),
        P(None, None, "chan"),
        P(None, None, "chan"),
        P(None, None, "chan", None),
        P(None, None, "chan", None),
    )
    out_specs = (
        P("chan", "batch"),
        P("chan", "batch"),
        P(None, "chan", None, None),
        P(None, "chan", None, None),
        P(None, "chan", None, None),
        P(None, None, "chan"),
        P(None, None, "chan"),
        P(None, None, "chan"),
        P(None, None, "chan", None),
        P(None, None, "chan", None),
        P(None, None, "chan", None),
    )
    n_chan = mesh.shape["chan"]

    def run(*args):
        own_seqs = args[1].shape[0] // mesh.shape["batch"]
        fits = suits(own_seqs, args[3].shape[1], n_chan, mesh.shape["batch"])
        body = local if fits else wide_local
        return jax.shard_map(body, mesh=mesh, in_specs=in_specs, out_specs=out_specs, check_vma=False)(*args)

    return run
```

```python
import functools
import math

import jax
import jax.numpy as jnp
import numpy as np
from jax import lax
from jax.experimental import pallas as pl
from jax.experimental.pallas import tpu as pltpu
from jax.sharding import PartitionSpec as P

LAYERS = 2
BUCKET = 1024
STEP = 10


QUARTER = BUCKET // 4
HALF_ROOT = math.sqrt(0.5)
STEP_ROWS = 16
UNROLL = 4
CONV_ROWS = 512
CHUNK_ROWS = 256
MAT_ROWS = 512
LIN_ROWS = 256
ROOM = 59 * 2**20
GROUPS = ((0, 256), (256, 256), (512, 512), (1024, 512), (1536, 512))
GELU_A = math.sqrt(2.0 / math.pi)
GELU_B = GELU_A * 0.044715


def transform_tables():
    place = np.arange(QUARTER)[:, None]
    to_spec, to_time = [], []
    for residue in (0, 4):
        bins = np.arange(QUARTER // 2)[None, :]
        turn = (8 * bins + residue) * place % (2 * BUCKET) * (math.pi / BUCKET)
        cosine, sine = np.cos(turn), -np.sin(turn)
        weights = np.full_like(cosine, 2.0)
        if residue == 0:
            sine[:, 0] = 1 - 2 * (place[:, 0] % 2)
            weights[:, 0] = 1.0
        to_spec.append(np.concatenate([cosine, sine], 1))
        to_time.append(np.concatenate([cosine * weights, sine * weights], 1).T / (2 * BUCKET))
    for residue in (1, 2, 3):
        bins = np.arange(QUARTER)[None, :]
        turn = (8 * bins + residue) * place % (2 * BUCKET) * (math.pi / BUCKET)
        cosine, sine = np.cos(turn), np.sin(turn)
        sign = 1.0 if residue == 3 else -1.0
        to_spec.append(np.block([[cosine, -sine], [sign * sine, sign * cosine]]))
        to_time.append(np.block([[cosine.T, sine.T], [-sine.T, cosine.T]]) / BUCKET)
    small = [np.stack(side[:2]).astype(jnp.bfloat16) for side in (to_spec, to_time)]
    large = [np.stack(side[2:]).astype(jnp.bfloat16) for side in (to_spec, to_time)]
    return small[0], large[0], small[1], large[1]


def quarters(x):
    return [x[:, q * QUARTER : (q + 1) * QUARTER] for q in range(4)]


def fold(x0, x1, x2, x3):
    even, odd = x0 + x2, x1 + x3
    diff = x1 - x3
    turned, tilted = diff * HALF_ROOT, odd * HALF_ROOT
    return even + odd, even - odd, x0 + turned, x2 + tilted, x0 - x2, diff, x0 - turned, x2 - tilted


def unfold(y0, y4, r1, i1, r2, i2, r3, i3):
    even, odd = y0 + y4, y0 - y4
    r_sum, r_diff, i_sum, i_diff = r1 + r3, r1 - r3, i1 + i3, i1 - i3
    return (
        even + (r2 + r_sum),
        odd - i2 + (r_diff - i_sum) * HALF_ROOT,
        even - (r2 + i_diff),
        odd + i2 - (r_diff + i_sum) * HALF_ROOT,
    )


def dot(a, b):
    return jnp.dot(a, b, preferred_element_type=jnp.float32)


def product(a, b, first, conj):
    half = a.shape[1] // 2
    ar, ai, br, bi = a[:, :half], a[:, half:], b[:, :half], b[:, half:]
    cross = ai * bi
    if conj:
        imag = ar * bi - ai * br
    else:
        imag = ar * bi + ai * br
    if first:
        lone = lax.broadcasted_iota(jnp.int32, cross.shape, 1) == 0
        imag = jnp.where(lone, cross, imag)
        cross = jnp.where(lone, 0.0, cross)
    real = ar * br + cross if conj else ar * br - cross
    return jnp.concatenate([real, imag], 1)


def table_of(small, large, group):
    return small[group] if group < 2 else large[group - 2]


def put_folded(dest, rows, parts):
    lower = pl.ds(rows.start + dest.shape[0] // 2, rows.size)
    for k, part in enumerate(parts):
        dest[rows if k < 4 else lower, k % 4 * QUARTER : (k % 4 + 1) * QUARTER] = part.astype(dest.dtype)


def get_folded(src, rows, at, width):
    if at >= BUCKET:
        rows, at = pl.ds(rows.start + src.shape[0] // 2, rows.size), at - BUCKET
    return src[rows, at : at + width]


def get_unfolded(src, rows):
    return unfold(*[src[rows, k * QUARTER : (k + 1) * QUARTER] for k in range(8)])


def steps(total, size, body):
    def one(k, carry):
        body(pl.ds(pl.multiple_of(k * size, size), size), k)
        return carry

    lax.fori_loop(0, total // size, one, 0, unroll=UNROLL if size == STEP_ROWS else 1)


def kernel_spectrum(ker, folded, spec, small, large, chunk):
    chans = ker.shape[0]

    def fold_rows(rows, _):
        put_folded(folded, rows, fold(*quarters(ker[rows, :].astype(jnp.float32))))

    steps(chans, STEP_ROWS, fold_rows)

    def transform_rows(rows, _):
        for g, (at, width) in enumerate(GROUPS):
            spec[rows, at : at + width] = dot(get_folded(folded, rows, at, width), table_of(small, large, g))

    steps(chans, chunk, transform_rows)


def token_stats(stream, chans):
    def add(k, carry):
        v = stream[pl.ds(pl.multiple_of(k * STEP_ROWS, STEP_ROWS), STEP_ROWS), :].astype(jnp.float32)
        return carry + v[:8] + v[8:]

    total = lax.fori_loop(0, chans // STEP_ROWS, add, jnp.zeros((8, BUCKET), jnp.float32), unroll=UNROLL)
    mean_val = jnp.sum(total, 0, keepdims=True) / chans

    def add_square(k, carry):
        v = stream[pl.ds(pl.multiple_of(k * STEP_ROWS, STEP_ROWS), STEP_ROWS), :].astype(jnp.float32) - mean_val
        v = v * v
        return carry + v[:8] + v[8:]

    total = lax.fori_loop(0, chans // STEP_ROWS, add_square, jnp.zeros((8, BUCKET), jnp.float32), unroll=UNROLL)
    return mean_val, lax.rsqrt(jnp.sum(total, 0, keepdims=True) / chans + 1e-05)


def lanes(x):
    total = x[:, :128]
    for k in range(1, x.shape[1] // 128):
        total = total + x[:, k * 128 : (k + 1) * 128]
    return total


GAIN, SHIFT, SKIP, BIAS_IN, BIAS_VAL = range(5)
MESH = pl.DeviceIdType.MESH


def bit_of(index, place):
    return lax.rem(lax.div(index, 1 << place), 2)


def flip(index, place):
    return index + (1 - 2 * bit_of(index, place)) * (1 << place)


def peers_of(n_chan):
    me, row = lax.axis_index("chan"), lax.axis_index("batch")
    others = []
    for k in range(1, n_chan):
        other = me
        for place in range(n_chan.bit_length() - 1):
            other = flip(other, place) if k >> place & 1 else other
        others.append(other)
    return me, row, others


def greet(targets, between):
    barrier = pltpu.get_barrier_semaphore()
    for target in targets:
        pl.semaphore_signal(barrier, inc=1, device_id=target, device_id_type=MESH)
    between()
    pl.semaphore_wait(barrier, len(targets))


LANES = 128
POWERS = 8
LOW_STAGE = 1


def halving(n_chan, n_batch):
    me, row = lax.axis_index("chan"), lax.axis_index("batch")
    chan_bits, batch_bits = n_chan.bit_length() - 1, n_batch.bit_length() - 1
    out = [(bit_of(me, k), (row, flip(me, k))) for k in reversed(range(chan_bits))]
    return out + [(bit_of(row, k), (flip(row, k), me)) for k in reversed(range(batch_bits))]


def mode_rows(raw):
    step_size = jnp.exp(raw[4])
    decay_rate, turn_rate = step_size * jnp.exp(raw[0]), step_size * raw[1]
    spans = [2.0**k for k in range(BUCKET.bit_length() - 1)]
    sizes = [jnp.exp(-span * decay_rate) for span in spans]
    total, moment = jnp.ones_like(decay_rate), jnp.zeros_like(decay_rate)
    for span, size in zip(spans, sizes):
        moment = moment * (1.0 + size) + span * size * total
        total = total * (1.0 + size)
    rows = []
    for span, size in list(zip(spans, sizes))[:POWERS]:
        rows += [size * jnp.cos(span * turn_rate), size * jnp.sin(span * turn_rate)]
    inverse = 1.0 / total
    return rows + [raw[2] * inverse, raw[3] * inverse, inverse, moment * inverse, decay_rate, turn_rate, step_size, raw[2], raw[3]]


def times(a, b):
    return a[0] * b[0] - a[1] * b[1], a[0] * b[1] + a[1] * b[0]


def columns_of(rows):
    pad = jnp.zeros((LANES - rows.shape[0], LANES), jnp.float32)
    return jnp.transpose(jnp.concatenate([rows, pad], 0))


def near_powers(params):
    lane = lax.broadcasted_iota(jnp.int32, (params.shape[0], LANES), 1)
    value = None
    for k in range(POWERS - 1):
        power = params[:, 2 * k : 2 * k + 1], params[:, 2 * k + 1 : 2 * k + 2]
        here = (lane & (1 << k)) != 0
        if value is None:
            value = jnp.where(here, power[0], 1.0), jnp.where(here, power[1], 0.0)
        else:
            moved = times(value, power)
            value = jnp.where(here, moved[0], value[0]), jnp.where(here, moved[1], value[1])
    far = params[:, 2 * POWERS - 2 : 2 * POWERS - 1], params[:, 2 * POWERS - 1 : 2 * POWERS]
    return value, tuple(jnp.broadcast_to(f, lane.shape) for f in far)


def halves(x):
    half = x.shape[0] // 2
    return [jnp.sum(x[:half], 0, keepdims=True), jnp.sum(x[half:], 0, keepdims=True)]


def kernel_rows(params):
    value, far = near_powers(params)
    value = times(value, (params[:, 2 * POWERS : 2 * POWERS + 1], params[:, 2 * POWERS + 1 : 2 * POWERS + 2]))
    out = [halves(value[0])]
    for _ in range(1, BUCKET // LANES):
        value = times(value, far)
        out.append(halves(value[0]))
    return [jnp.concatenate([row[c] for row in out], 0) for c in range(2)]


def state_rows(modes, grads):
    params = columns_of(modes)
    value, far = near_powers(params)
    half = params.shape[0] // 2
    place = lax.broadcasted_iota(jnp.int32, (1, LANES), 1).astype(jnp.float32)
    plain = weighted = None
    for k in reversed(range(BUCKET // LANES)):
        rows = [g[:, k * LANES : (k + 1) * LANES] for g in grads]
        g = jnp.concatenate([jnp.broadcast_to(r, (half, LANES)) for r in rows], 0)
        w = jnp.concatenate([jnp.broadcast_to(r * (place + float(k * LANES)), (half, LANES)) for r in rows], 0)
        if plain is None:
            plain, weighted = (g, jnp.zeros_like(g)), (w, jnp.zeros_like(g))
        else:
            plain, weighted = times(plain, far), times(weighted, far)
            plain, weighted = (plain[0] + g, plain[1]), (weighted[0] + w, weighted[1])
    cols = times(plain, value) + times(weighted, value)
    lane = lax.broadcasted_iota(jnp.int32, value[0].shape, 1)
    out = jnp.zeros_like(value[0])
    for k, col in enumerate(cols):
        out = jnp.where(lane == k, jnp.sum(col, 1, keepdims=True), out)
    out = jnp.transpose(out)
    at = 2 * POWERS + 2
    inverse, moment, decay_rate, turn_rate, step_size, w_re, w_im = [modes[at + k : at + k + 1] for k in range(7)]
    c_re, c_im, d_re, d_im = [out[k : k + 1] * inverse for k in range(4)]
    turn_grad = -(w_re * d_im + w_im * d_re)
    decay_grad = ((w_re * c_re - w_im * c_im) * moment - (w_re * d_re - w_im * d_im)) * decay_rate
    result = [decay_grad, turn_grad * step_size, c_re, -c_im, decay_grad + turn_grad * turn_rate]
    return jnp.concatenate(result + [jnp.zeros_like(c_re)] * 3, 0)


def remote(src, dst, send, recv, target):
    return pltpu.make_async_remote_copy(
        src_ref=src, dst_ref=dst, send_sem=send, recv_sem=recv, device_id=target, device_id_type=MESH
    )


def halving_bits(n_chan, n_batch):
    return n_chan.bit_length() + n_batch.bit_length() - 2


def whole(a):
    return pl.BlockSpec(a.shape, lambda t, n=a.ndim: (0,) * n, pipeline_mode=pl.Buffered(1))


ANYWHERE = pl.BlockSpec(memory_space=pl.ANY)
GATHER_ORDER = (((0,), (1, 2), (3,), (4,)), ((0,), (3,), (1, 2), (4,)))


def train_kernel(
    n_chan, n_batch, mask, raw, fs, fl, ts, tl, vec_mine, x_own, cot_own, w_own,
    out_all, in_all, state_all, lin_all, vec_all, cot_all, ker_all, w_all,
    hat_far, pre_far, act_far, sigma_far, slope_far, spec_far,
    params, x_low, hats, pres, acts, sigmas, slopes, specs, stats, streams, ker_spec, spec_grad, mixed, folded, pre_grad, back_low,
    w_near, loaded, sums, vecs, vec_in, ker_rows, ker_low,
    lin_grad, vec_grad, vec_cols, vec_rows, vec_got, vec_own,
    ker_sums, ker_sent, ker_got, lin_sums, lin_sent, lin_got, low_sent, low_got, ker_final, lin_final, state_own,
    move_send, move_recv, move_own, gather_send, gather_recv, gather_own, load_sem, far_sem,
    part_send, part_recv, ready, vec_send, vec_recv, vec_sem, all_send, all_recv, all_own,
):
    step = pl.program_id(0)
    layers, seqs = stats.shape[:2]
    chans = x_low.shape[1]
    own = chans // n_chan
    part = ker_final.shape[1]
    forward_steps = layers * seqs
    me, row, others = peers_of(n_chan)
    rows_of = [lax.rem(row + k, n_batch) for k in range(1, n_batch)]
    above = halving(n_chan, n_batch)
    path = list(reversed(above))
    bits, batch_bits = len(path), n_batch.bit_length() - 1
    total = 1 << bits
    core_bit = path[0][0]
    near = n_chan // 2
    top, bottom = layers - 1, 0
    mine = pl.ds(pl.multiple_of(me * own, own), own)

    def trade(kind, k, source, dest):
        copies = [pltpu.make_async_copy(source(me), dest, move_own.at[kind, k])]
        for j, other in enumerate(others):
            copies.append(remote(source(other), dest, move_send.at[kind, k, j], move_recv.at[kind, k, j], (row, other)))
        return copies

    def columns(device, k):
        return pl.ds(pl.multiple_of((device * seqs + k) * BUCKET, BUCKET), BUCKET)

    def x_moves(k):
        return trade(0, k, lambda device: x_own.at[:, columns(device, k)], x_low.at[k, mine])

    def cot_moves(k):
        return trade(1, k, lambda device: cot_own.at[:, columns(device, k)], cot_all.at[k, mine])

    def rows_for(device):
        return pl.ds(pl.multiple_of(device * own, own), own)

    def out_moves(k):
        return trade(2, k, lambda device: back_low.at[k, rows_for(device)], out_all.at[:, columns(me, k)])

    def in_moves(k):
        return trade(3, k, lambda device: back_low.at[k, rows_for(device)], in_all.at[:, columns(me, k)])

    def run(copies):
        for copy in copies:
            copy.start()

    def finish_all(copies):
        for copy in copies:
            copy.wait()

    place = tuple(bit for bit, _ in above)

    def held(kind, i, s):
        order = GATHER_ORDER[kind]
        done = [d for group in order[:s] for d in group]
        ref = (ker_all if kind == 0 else w_all).at[i]
        ref = ref.at[tuple(slice(None) if d in done else place[d] for d in range(bits))]
        slot = sum((1 << len(group)) - 1 for group in order[:s])
        copies = []
        for mask in range(1, 1 << len(order[s])):
            chan, batch = me, row
            for t, d in enumerate(order[s]):
                if mask >> t & 1 and d < bits - batch_bits:
                    chan = flip(chan, bits - batch_bits - 1 - d)
                elif mask >> t & 1:
                    batch = flip(batch, bits - 1 - d)
            k, slot = 2 * i + kind, slot + 1
            copies.append(remote(ref, ref, gather_send.at[k, slot - 1], gather_recv.at[k, slot - 1], (batch, chan)))
        return copies

    def gather_next(i, s):
        for kind in (1, 0):
            finish_all(held(kind, i, s))
            if s + 1 < len(GATHER_ORDER[kind]):
                run(held(kind, i, s + 1))

    def vec_in_moves():
        copies = [pltpu.make_async_copy(vec_mine, vec_in.at[me], gather_own.at[2 * layers])]
        for k, other in enumerate(others):
            copies.append(remote(vec_mine, vec_in.at[me], vec_send.at[1, k], vec_recv.at[1, k], (row, other)))
        return copies

    def make_kernels(i):
        def make(h, carry):
            first_row, second_row = kernel_rows(columns_of(params[i * part // 2 + h]))
            ker_rows[2 * h] = first_row
            ker_rows[2 * h + 1] = second_row
            return carry

        lax.fori_loop(0, part // 2, make, 0, unroll=4)
        for k in range(BUCKET // LANES):
            ker_low[i, :, k * LANES : (k + 1) * LANES] = ker_rows[:, k, :].astype(jnp.bfloat16)
        return pltpu.make_async_copy(ker_low.at[i], ker_all.at[(i,) + place], gather_own.at[2 * i])

    def load_kernels(layer):
        copy = pltpu.make_async_copy(ker_all.at[layer].reshape(chans, BUCKET), loaded, load_sem)
        copy.start()
        copy.wait()
        kernel_spectrum(loaded, folded, ker_spec, fs, fl, CONV_ROWS)

    def far_copies(k, back):
        pairs = zip((hats, pres, acts, sigmas, slopes, specs), (hat_far, pre_far, act_far, sigma_far, slope_far, spec_far))
        copies = []
        for j, (near, far) in enumerate(pairs):
            ends = (far.at[k], near.at[k]) if back else (near.at[k], far.at[k])
            copies.append(pltpu.make_async_copy(*ends, far_sem.at[j, k]))
        return copies

    groups = [[0], [1], [2, 3], [4]]
    count, at, gone = [], [0], 0
    for group in groups:
        gone += len(group)
        count.append(total >> gone)
        at.append(at[-1] + count[-1] * ((1 << len(group)) - 1))
    last_stage = len(groups) - 1

    def side(s, mask):
        chan, batch, index = me, row, 0
        for t, dim in enumerate(groups[s]):
            bit = path[dim][0]
            across = mask >> t & 1
            index = index + (1 - bit if across else bit) * (1 << t)
            if across and dim < batch_bits:
                batch = flip(batch, dim)
            elif across:
                chan = flip(chan, dim - batch_bits)
        return (batch, chan), index

    def masks(s):
        return range(1, 1 << len(groups[s]))

    def kept_rows(b):
        return spec_grad[pl.ds(pl.multiple_of(b * part, part), part), :BUCKET]

    def sums_at(s):
        return sum(count[1 : s + 1])

    def slot(kind, s, mask, sent):
        first = (mask - 1) * count[s]
        if kind == 0 or s == 0:
            return at[s] + first
        if s == LOW_STAGE:
            return first
        return first + at[s] - at[LOW_STAGE + 1] + (0 if sent else at[LOW_STAGE])

    def stage(kind, layer, s, mask):
        to, got = pl.ds(slot(kind, s, mask, True), count[s]), pl.ds(slot(kind, s, mask, False), count[s])
        if kind == 0:
            src, dst = ker_sent.at[to], ker_got.at[got]
        elif s == 0:
            src, dst = lin_grad.at[layer, :, 1 - core_bit], lin_got.at[got]
        elif s == LOW_STAGE:
            src, dst = low_sent.at[to], low_got.at[got]
        else:
            src, dst = lin_sent.at[to], lin_got.at[got]
        k = at_peer[s] + mask - 1
        return remote(src, dst, part_send.at[kind, k], part_recv.at[kind, k], side(s, mask)[0])

    at_peer = [0]
    for s in range(len(groups)):
        at_peer.append(at_peer[-1] + (1 << len(groups[s])) - 1)

    def begin(kind, layer, s):
        for mask in masks(s):
            if layer != layers - 1:
                pl.semaphore_wait(ready.at[kind, at_peer[s] + mask - 1], 1)
            stage(kind, layer, s, mask).start()

    def advance(kind, layer, s):
        for mask in masks(s):
            stage(kind, layer, s, mask).wait()

        def value(b):
            if kind == 0:
                result = kept_rows(b) if s == 0 else ker_sums[sums_at(s - 1) + b]
            else:
                result = lin_grad[layer, b, core_bit] if s == 0 else lin_sums[sums_at(s - 1) + b]
            for mask in masks(s):
                got = ker_got if kind == 0 else low_got if s == LOW_STAGE else lin_got
                result = result + got[slot(kind, s, mask, False) + b].astype(jnp.float32)
            return result

        if s == last_stage:
            final = ker_final if kind == 0 else lin_final
            final[layer] = value(0)
        else:
            wide = 1 << len(groups[s + 1])

            def one(b, carry):
                sums = ker_sums if kind == 0 else lin_sums
                sums[sums_at(s) + b] = value(wide * b + side(s + 1, 0)[1])
                for mask in masks(s + 1):
                    moved = value(wide * b + side(s + 1, mask)[1])
                    to = slot(kind, s + 1, mask, True) + b
                    if kind == 0:
                        ker_sent[to] = moved.astype(jnp.bfloat16)
                    elif s + 1 == LOW_STAGE:
                        low_sent[to] = moved.astype(jnp.bfloat16)
                    else:
                        lin_sent[to] = moved
                return carry

            lax.fori_loop(0, count[s + 1], one, 0)
        if layer == layers - 1:
            for mask in masks(s):
                there = side(s, mask)[0]
                pl.semaphore_signal(ready.at[kind, at_peer[s] + mask - 1], inc=1, device_id=there, device_id_type=MESH)
        if s < last_stage:
            begin(kind, layer, s + 1)

    def spread(own_ref, everyone, k):
        copies = [pltpu.make_async_copy(own_ref, everyone.at[row], all_own.at[k])]
        for j, other in enumerate(rows_of):
            copies.append(remote(own_ref, everyone.at[row], all_send.at[k, j], all_recv.at[k, j], (other, me)))
        return copies

    def spreads(kind, layer):
        if kind == 0:
            half = pl.ds(layer * part // 2, part // 2)
            return spread(state_own.at[half], state_all.at[:, half], layer)
        return spread(lin_final.at[layer], lin_all.at[:, layer], layers + layer)

    def vec_moves():
        copies = [pltpu.make_async_copy(vec_rows.at[me], vec_got.at[me], vec_sem)]
        for k, other in enumerate(others):
            copies.append(remote(vec_rows.at[other], vec_got.at[me], vec_send.at[0, k], vec_recv.at[0, k], (row, other)))
        return copies

    def states(layer):
        def one(h, carry):
            at = layer * part // 2 + h
            state_own[at] = state_rows(params[at], [ker_final[layer, pl.ds(2 * h + c, 1), :] for c in range(2)])
            return carry

        lax.fori_loop(0, part // 2, one, 0, unroll=4)

    @pl.when(step == 0)
    def _():
        locals_ = [pltpu.make_async_copy(w_own.at[i], w_all.at[(i,) + place], gather_own.at[2 * i + 1]) for i in range(layers)]

        greet([(row, other) for other in others] + [(other, me) for other in rows_of], lambda: run(locals_))
        finish_all(locals_)
        run(held(1, 0, 0))
        run(x_moves(0))
        for k, value in enumerate(mode_rows([raw[k] for k in range(5)])):
            params[:, k, :] = value
        copy = make_kernels(0)
        copy.start()
        copy.wait()
        run(held(0, 0, 0) + vec_in_moves())
        for i in range(1, layers):
            copy = make_kernels(i)
            copy.start()
            copy.wait()
        gather_next(0, 0)
        gather_next(0, 1)
        run(x_moves(1))
        gather_next(0, 2)
        for i in range(1, layers):
            run(held(1, i, 0) + held(0, i, 0))
        gather_next(0, 3)
        finish_all(vec_in_moves())
        for i in range(layers):
            for c in range(n_chan):
                vecs[i, c * own : (c + 1) * own, :] = columns_of(vec_in[c, 8 * i : 8 * i + 8, :])[:own]
        vec_cols[...] = jnp.zeros_like(vec_cols)
        finish_all(x_moves(0))

    @pl.when(step == 1)
    def _():
        for k in range(1, seqs):
            finish_all(x_moves(k))
        run(cot_moves(0))

    @pl.when(step < forward_steps)
    def _():
        layer, seq = lax.div(step, seqs), lax.rem(step, seqs)
        stream, hat_out, pre_out, act_out = streams.at[seq], hats.at[seq], pres.at[seq], acts.at[seq]
        sigma_out, slope_out, spec_out, first = sigmas.at[seq], slopes.at[seq], specs.at[seq], x_low.at[seq]
        stat, vec, weight = stats.at[layer, seq], vecs.at[layer], w_near.at[layer]
        hat, mixed = pre_grad, spec_grad

        @pl.when(layer == 0)
        def _():
            def widen(rows, _):
                stream[rows, :] = first[rows, :].astype(jnp.float32)

            steps(chans, STEP_ROWS, widen)

        @pl.when(seq == 0)
        def _():
            copy = pltpu.make_async_copy(w_all.at[layer].reshape(2 * chans, chans), weight, load_sem)
            copy.start()
            copy.wait()
            load_kernels(layer)

        @pl.when(layer > 0)
        def _():
            finish_all(far_copies(seq, False))

        mean_val, inv_std = token_stats(stream, chans)
        stat[0:1, :] = mean_val
        stat[1:2, :] = inv_std

        def normalise(rows, _):
            v = (stream[rows, :] - stat[0:1, :]) * stat[1:2, :]
            hat[rows, :] = v
            hat_out[rows, :] = v.astype(hat_out.dtype)
            v = v * vec[rows, GAIN : GAIN + 1] + vec[rows, SHIFT : SHIFT + 1]
            put_folded(folded, rows, fold(*quarters(v)))

        steps(chans, STEP_ROWS, normalise)

        @pl.when(step == forward_steps - 2)
        def _():
            for k in range(1, seqs):
                run(cot_moves(k))

        def convolve(rows, _):
            for g, (at, width) in enumerate(GROUPS):
                spec = dot(get_folded(folded, rows, at, width), table_of(fs, fl, g))
                spec_out[rows, at : at + width] = spec.astype(jnp.bfloat16)
                both = product(ker_spec[rows, at : at + width], spec, g == 0, False)
                mixed[rows, at : at + width] = dot(both.astype(jnp.bfloat16), table_of(ts, tl, g))

        steps(chans, CONV_ROWS, convolve)

        @pl.when(step == 0)
        def _():
            gather_next(1, 0)

        @pl.when(step == 1)
        def _():
            gather_next(1, 2)

        def activate(rows, _):
            gain, shift, skip = [vec[rows, k : k + 1] for k in (GAIN, SHIFT, SKIP)]
            gain, shift = gain * skip, shift * skip
            for q, value in enumerate(get_unfolded(mixed, rows)):
                cols = slice(q * QUARTER, (q + 1) * QUARTER)
                pre = value + (gain * hat[rows, cols] + shift)
                pre_out[rows, cols] = pre.astype(pre_out.dtype)
                soft = jnp.tanh(pre * (GELU_A + GELU_B * (pre * pre)))
                act_out[rows, cols] = (0.5 * pre * (1.0 + soft)).astype(jnp.bfloat16)

        steps(chans, STEP_ROWS, activate)

        block = 2 * LIN_ROWS
        for t in range(4):
            cols = slice(t * QUARTER, (t + 1) * QUARTER)

            def linear(rows, k, cols=cols):
                mixed[:block, :QUARTER] = dot(weight[rows, :], act_out[:, cols])
                for o in range(LIN_ROWS // 16):
                    at = pl.ds(pl.multiple_of(k * LIN_ROWS + o * 16, 16), 16)
                    gate = mixed[o * 32 : o * 32 + 16, :QUARTER] + vec[at, BIAS_IN : BIAS_IN + 1]
                    value = mixed[o * 32 + 16 : o * 32 + 32, :QUARTER] + vec[at, BIAS_VAL : BIAS_VAL + 1]
                    sigma = 0.5 * jnp.tanh(0.5 * value) + 0.5
                    gated = gate * sigma
                    sigma_out[at, cols] = sigma.astype(sigma_out.dtype)
                    slope_out[at, cols] = (gated - gated * sigma).astype(slope_out.dtype)
                    moved = stream[at, cols] + mask[me * seqs + seq, :, cols] * gated
                    stream[at, cols] = moved
                    back_low[seq, at, cols] = (moved - first[at, cols].astype(jnp.float32)).astype(jnp.bfloat16)

            steps(2 * chans, block, linear)

        @pl.when(step == 0)
        def _():
            gather_next(1, 1)

        @pl.when(step == 1)
        def _():
            gather_next(1, 3)

        @pl.when(layer == 0)
        def _():
            run(far_copies(seq, False))

    @pl.when(step >= forward_steps)
    def _():
        turn, seq = lax.div(step - forward_steps, seqs), lax.rem(step - forward_steps, seqs)
        layer = layers - 1 - turn
        back, hat, pre, act = streams.at[seq], hats.at[seq], pres.at[seq], acts.at[seq]
        sigma_in, slope_in, spec, first = sigmas.at[seq], slopes.at[seq], specs.at[seq], x_low.at[seq]
        stat, vec = stats.at[layer, seq], vecs.at[layer]
        next_layer = (turn == 1) & (seq == 0)
        ends = (turn == layers - 1) & (seq == seqs - 1)

        for k in range(seqs):

            @pl.when((turn == 0) & (seq == k))
            def _(k=k):
                finish_all(cot_moves(k))
                copy = pltpu.make_async_copy(cot_all.at[k], x_low.at[k], load_sem)
                copy.start()
                if k > 0:
                    run(out_moves(k))
                copy.wait()

            @pl.when((turn == 1) & (seq == k))
            def _(k=k):
                finish_all(far_copies(k, True))

        @pl.when((turn == 0) & (seq > 0))
        def _():
            run(far_copies(seq - 1, True))

        @pl.when((turn == 1) & (seq == 0))
        def _():
            run(far_copies(seqs - 1, True))

        @pl.when(turn == 0)
        def _():
            def widen(rows, _):
                back[rows, :] = first[rows, :].astype(jnp.float32)

            steps(chans, STEP_ROWS, widen)

        @pl.when(seq == 0)
        def _():
            @pl.when(turn > 0)
            def _():
                load_kernels(layer)

            for k in range(4):
                cols = slice(k * QUARTER, (k + 1) * QUARTER)
                loaded[:, cols] = jnp.transpose(w_near[layer, cols, :])
            vec_grad[...] = jnp.zeros_like(vec_grad)

        def gates(rows, k):
            gated = back[rows, :] * mask[me * seqs + seq]
            left = (gated * sigma_in[rows, :].astype(jnp.float32)).astype(jnp.bfloat16)
            right = (gated * slope_in[rows, :].astype(jnp.float32)).astype(jnp.bfloat16)
            at = pl.multiple_of(k * 32, 32)
            folded[pl.ds(at, 16), :] = left
            folded[pl.ds(at + 16, 16), :] = right
            vec_grad[3, rows, :] += lanes(left.astype(jnp.float32))
            vec_grad[4, rows, :] += lanes(right.astype(jnp.float32))

        steps(chans, STEP_ROWS, gates)

        width = 2 * chans // total
        blocks = MAT_ROWS // (2 * width)

        def lin_back(rows, k):
            value = lax.dot_general(
                folded[rows, :], act[...], (((1,), (1,)), ((), ())), preferred_element_type=jnp.float32
            ).reshape(blocks, 2, width, chans)
            at = pl.ds(k * blocks, blocks)

            @pl.when(seq == 0)
            def _():
                lin_grad[layer, at] = value

            @pl.when(seq > 0)
            def _():
                lin_grad[layer, at] += value

        steps(2 * chans, MAT_ROWS, lin_back)

        @pl.when(ends)
        def _():
            begin(1, bottom, 0)

        def act_back(rows, _):
            for t in range(4):
                cols = slice(t * QUARTER, (t + 1) * QUARTER)
                pre_grad[rows, cols] = dot(loaded[rows, :], folded[:, cols])

        steps(chans, MAT_ROWS, act_back)

        def gelu_back(rows, _):
            skip_sum = jnp.zeros((STEP_ROWS, 128), jnp.float32)
            outs = []
            for q in range(4):
                cols = slice(q * QUARTER, (q + 1) * QUARTER)
                p = pre[rows, cols].astype(jnp.float32)
                square = p * p
                soft = jnp.tanh(p * (GELU_A + GELU_B * square))
                slope = 0.5 * (1.0 + soft) + (0.5 * p) * (1.0 - soft * soft) * (GELU_A + (3.0 * GELU_B) * square)
                grad = pre_grad[rows, cols] * slope
                pre_grad[rows, cols] = grad
                norm = hat[rows, cols].astype(jnp.float32) * vec[rows, GAIN : GAIN + 1] + vec[rows, SHIFT : SHIFT + 1]
                skip_sum = skip_sum + lanes(grad * norm)
                outs.append(grad)
            vec_grad[2, rows, :] += skip_sum
            put_folded(folded, rows, fold(*outs))

        steps(chans, STEP_ROWS, gelu_back)

        @pl.when((turn == 0) & (seq == 0))
        def _():
            run(out_moves(0))

        @pl.when(next_layer)
        def _():
            for kind in (0, 1):
                advance(kind, top, 0)

        sums[...] = jnp.zeros_like(sums)

        @pl.when(seq == 0)
        def _():
            spec_grad[...] = jnp.zeros_like(spec_grad)

        def correlate(rows, chunk):
            for g, (at, width) in enumerate(GROUPS):
                grad = dot(get_folded(folded, rows, at, width), table_of(fs, fl, g))
                spec_grad[rows, at : at + width] += product(
                    spec[rows, at : at + width].astype(jnp.float32), grad, g == 0, True
                )
                both = product(ker_spec[rows, at : at + width], grad, g == 0, True)
                mixed[:, at : at + width] = dot(both.astype(jnp.bfloat16), table_of(ts, tl, g))

            def norm_back(k, carry):
                here = pl.ds(pl.multiple_of(k * STEP_ROWS, STEP_ROWS), STEP_ROWS)
                rows = pl.ds(pl.multiple_of(chunk * CHUNK_ROWS + k * STEP_ROWS, STEP_ROWS), STEP_ROWS)
                skip = vec[rows, SKIP : SKIP + 1]
                gain = vec[rows, GAIN : GAIN + 1]
                gain_sum = jnp.zeros((STEP_ROWS, 128), jnp.float32)
                shift_sum = jnp.zeros((STEP_ROWS, 128), jnp.float32)
                plain, weighted = [], []
                for q, part in enumerate(get_unfolded(mixed, here)):
                    cols = slice(q * QUARTER, (q + 1) * QUARTER)
                    grad = part + skip * pre_grad[rows, cols]
                    both = grad * hat[rows, cols].astype(jnp.float32)
                    gain_sum = gain_sum + lanes(both)
                    shift_sum = shift_sum + lanes(grad)
                    cent = grad * gain
                    pre_grad[rows, cols] = cent
                    both = both * gain
                    plain.append(cent[:8] + cent[8:])
                    weighted.append(both[:8] + both[8:])
                vec_grad[0, rows, :] += gain_sum
                vec_grad[1, rows, :] += shift_sum
                return carry[0] + jnp.concatenate(plain, 1), carry[1] + jnp.concatenate(weighted, 1)

            zero = jnp.zeros((8, BUCKET), jnp.float32)
            plain, weighted = lax.fori_loop(0, CHUNK_ROWS // STEP_ROWS, norm_back, (zero, zero), unroll=2)
            sums[0:8, :] += plain
            sums[8:16, :] += weighted

        steps(chans, CHUNK_ROWS, correlate)

        @pl.when(seq == seqs - 1)
        def _():
            def to_time(rows, _):
                for g, (at, width) in enumerate(GROUPS):
                    low = spec_grad[rows, at : at + width].astype(jnp.bfloat16)
                    ker_spec[rows, at : at + width] = dot(low, table_of(ts, tl, g))

            steps(chans, CONV_ROWS, to_time)

            def block_rows(b):
                return pl.ds(pl.multiple_of(b * part, part), part)

            def write(b, carry):
                for q, value in enumerate(get_unfolded(ker_spec, block_rows(2 * b + core_bit))):
                    spec_grad[block_rows(b), q * QUARTER : (q + 1) * QUARTER] = value
                for q, value in enumerate(get_unfolded(ker_spec, block_rows(2 * b + 1 - core_bit))):
                    ker_sent[b, :, q * QUARTER : (q + 1) * QUARTER] = value.astype(jnp.bfloat16)
                return carry

            lax.fori_loop(0, total // 2, write, 0)

        for i in range(layers):

            @pl.when((turn == i) & (seq == seqs - 1))
            def _(i=i):
                layer = layers - 1 - i
                begin(0, layer, 0)
                if layer == layers - 1:
                    begin(1, layer, 0)
                else:
                    advance(1, layer, 0)
                    for kind in (0, 1):
                        advance(kind, top, 2)

        mean_plain = jnp.sum(sums[0:8, :], 0, keepdims=True) / chans
        mean_weighted = jnp.sum(sums[8:16, :], 0, keepdims=True) / chans
        sums[0:1, :] = mean_plain
        sums[8:9, :] = mean_weighted

        @pl.when(next_layer)
        def _():
            for kind in (0, 1):
                advance(kind, top, 1)

        for k in range(seqs):

            @pl.when((turn == layers - 1) & (seq == k))
            def _(k=k):
                finish_all(out_moves(k))

        def finish(rows, _):
            scaled = hat[rows, :].astype(jnp.float32) * sums[8:9, :]
            moved = back[rows, :] + stat[1:2, :] * (pre_grad[rows, :] - sums[0:1, :] - scaled)
            back[rows, :] = moved

        def leave(rows, _):
            scaled = hat[rows, :].astype(jnp.float32) * sums[8:9, :]
            moved = back[rows, :] + stat[1:2, :] * (pre_grad[rows, :] - sums[0:1, :] - scaled)
            back_low[seq, rows, :] = (moved - first[rows, :].astype(jnp.float32)).astype(jnp.bfloat16)

        @pl.when(turn < layers - 1)
        def _():
            steps(chans, STEP_ROWS, finish)

        @pl.when(turn == layers - 1)
        def _():
            steps(chans, STEP_ROWS, leave)

        for k in range(seqs):

            @pl.when((turn == layers - 1) & (seq == k))
            def _(k=k):
                run(in_moves(k) if k < seqs - 1 else in_moves(k)[:near])

        for i in range(layers):

            @pl.when((turn == i) & (seq == seqs - 1))
            def _(i=i):
                layer = layers - 1 - i

                def vec_columns(rows, _):
                    lane = lax.broadcasted_iota(jnp.int32, (STEP_ROWS, LANES), 1)
                    out = vec_cols[rows, :]
                    for kind in range(5):
                        out = jnp.where(lane == layer * 5 + kind, jnp.sum(vec_grad[kind, rows, :], 1, keepdims=True), out)
                    vec_cols[rows, :] = out

                steps(chans, STEP_ROWS, vec_columns)

        @pl.when(ends)
        def _():
            for c in range(n_chan):
                vec_rows[c] = columns_of(vec_cols[c * own : (c + 1) * own, :])[:16]
            run(vec_moves())
            advance(0, bottom, 0)
            advance(1, bottom, 1)
            for kind in (0, 1):
                advance(kind, top, last_stage)
            run(spreads(1, top))
            advance(0, bottom, 1)
            run(in_moves(seqs - 1)[near:])
            states(top)
            run(spreads(0, top))
            finish_all(vec_moves())
            vec_own[...] = jnp.sum(vec_got[...], 0)
            run(spread(vec_own, vec_all, 2 * layers))
            for s in range(2, last_stage + 1):
                for kind in (1, 0):
                    advance(kind, bottom, s)
            run(spreads(1, bottom))
            states(bottom)
            run(spreads(0, bottom))
            for k in range(seqs):
                finish_all(in_moves(k))
            for i in range(layers):
                for copy in spreads(0, i) + spreads(1, i):
                    copy.wait()
            for copy in spread(vec_own, vec_all, 2 * layers):
                copy.wait()


def train(mask, raw, tables, vec_mine, x_own, cot_own, w_own, n_chan, n_batch):
    own, group = x_own.shape
    chans, toks = own * n_chan, group // n_chan
    seqs, layers = toks // BUCKET, w_own.shape[0]
    bits = halving_bits(n_chan, n_batch)
    total = 1 << bits
    part = chans // total
    low_count, peers = total >> (LOW_STAGE + 1), bits + 1
    shape, low, full = jax.ShapeDtypeStruct, jnp.bfloat16, jnp.float32
    vmem, dma = pltpu.VMEM, pltpu.SemaphoreType.DMA
    there = (2,) * bits
    slots, wide = (seqs, chans, BUCKET), (seqs, chans, 2 * BUCKET)
    return pl.pallas_call(
        functools.partial(train_kernel, n_chan, n_batch),
        grid=(2 * layers * seqs,),
        in_specs=[whole(a) for a in (mask, raw, *tables, vec_mine)] + [ANYWHERE] * 3,
        out_specs=[ANYWHERE] * 14,
        out_shape=[
            shape((own, group), low),
            shape((own, group), low),
            shape((n_batch, layers * part // 2, 8, LANES), full),
            shape((n_batch, layers, 2 * part, chans), full),
            shape((n_batch, 16, LANES), full),
            shape(slots, low),
            shape((layers,) + there + (part, BUCKET), low),
            shape((layers,) + there + (2 * part, chans), low),
        ]
        + [shape(slots, low)] * 5
        + [shape(wide, low)],
        scratch_shapes=[vmem((layers * part // 2, 32, LANES), full)]
        + [vmem(slots, low)] * 6
        + [
            vmem(wide, low),
            vmem((layers, seqs, 8, BUCKET), full),
            vmem(slots, full),
            vmem((chans, 2 * BUCKET), full),
            vmem((chans, 2 * BUCKET), full),
            vmem((CHUNK_ROWS, 2 * BUCKET), full),
            vmem((2 * chans, BUCKET), low),
            vmem((chans, BUCKET), full),
            vmem(slots, low),
            vmem((layers, 2 * chans, chans), low),
            vmem((chans, BUCKET), low),
            vmem((16, BUCKET), full),
            vmem((layers, chans, LANES), full),
            vmem((n_chan, 16, LANES), full),
            vmem((part, BUCKET // LANES, LANES), full),
            vmem((layers, part, BUCKET), low),
            vmem((layers, total // 2, 2, 2 * part, chans), full),
            vmem((5, chans, LANES), full),
            vmem((chans, LANES), full),
            vmem((n_chan, 16, LANES), full),
            vmem((n_chan, 16, LANES), full),
            vmem((16, LANES), full),
            vmem((3 * total // 8, part, BUCKET), full),
            vmem((total, part, BUCKET), low),
            vmem((total, part, BUCKET), low),
            vmem((3 * total // 8, 2 * part, chans), full),
            vmem((low_count, 2 * part, chans), full),
            vmem((total - low_count, 2 * part, chans), full),
            vmem((low_count, 2 * part, chans), low),
            vmem((low_count, 2 * part, chans), low),
            vmem((layers, part, BUCKET), full),
            vmem((layers, 2 * part, chans), full),
            vmem((layers * part // 2, 8, LANES), full),
            dma((4, seqs, n_chan - 1)), dma((4, seqs, n_chan - 1)), dma((4, seqs)),
            dma((2 * layers, peers)), dma((2 * layers, peers)), dma((2 * layers + 1,)),
            dma, dma((6, seqs)),
            dma((2, peers)), dma((2, peers)), pltpu.SemaphoreType.REGULAR((2, peers)),
            dma((2, n_chan - 1)), dma((2, n_chan - 1)), dma,
            dma((2 * layers + 1, n_batch - 1)), dma((2 * layers + 1, n_batch - 1)), dma((2 * layers + 1,)),
        ],
        compiler_params=pltpu.CompilerParams(vmem_limit_bytes=ROOM, collective_id=1, has_side_effects=True),
        cost_estimate=pl.CostEstimate(flops=60 * 10**9, bytes_accessed=60 * 2**20, transcendentals=0),
        name="train",
    )(mask, raw, *tables, vec_mine, x_own, cot_own, w_own)


def adam(weight, grad, first, second, rate):
    first_new = 0.9 * first + 0.1 * grad
    second_new = 0.999 * second + 0.001 * grad * grad
    fixed_first = first_new / (1.0 - 0.9**STEP)
    fixed_second = second_new / (1.0 - 0.999**STEP)
    new_weight = weight - rate * (fixed_first / (jnp.sqrt(fixed_second) + 1e-08) + 0.01 * weight)
    return (first_new, second_new, new_weight)


def local(
    inputs, lengths, cotangent, ln_gain, ln_bias, log_step, skip_gain, lin_bias, log_decay, frequency,
    w_re, w_im, lin_weight, lin_moment, lin_square, vec_moment, vec_square, state_moment, state_square,
):
    n_chan = lax.axis_size("chan")
    n_batch = lax.axis_size("batch")
    own = inputs.shape[0]
    chans = own * n_chan
    toks = inputs.shape[1] // n_chan
    seqs = toks // BUCKET
    part = own // n_batch
    row = lax.axis_index("batch")
    places = lax.iota(jnp.int32, BUCKET)
    valid = (places[None, None, :] < lengths[:, None, None]).astype(jnp.float32)
    tables = tuple(jnp.asarray(t) for t in transform_tables())

    def mine(a):
        return lax.dynamic_slice_in_dim(a, row * part, part, 1)

    step_all = jnp.broadcast_to(log_step[..., None], log_decay.shape)
    raw = jnp.stack([mine(a) for a in (log_decay, frequency, w_re, w_im, step_all)])
    raw = raw.reshape(5, LAYERS * part // 2, LANES)
    w_own = mine(lin_weight).transpose(0, 2, 1, 3).reshape(LAYERS, 2 * part, chans).astype(jnp.bfloat16)
    vec_own = jnp.stack([ln_gain, ln_bias, skip_gain, lin_bias[:, 0], lin_bias[:, 1]], 1)
    vec_own = jnp.pad(vec_own, ((0, 0), (0, 3), (0, LANES - own))).reshape(8 * LAYERS, LANES)
    out_delta, in_delta, state_all, lin_all, vec_all, *_ = train(
        valid, raw, tables, vec_own, inputs, cotangent, w_own, n_chan, n_batch
    )
    output = inputs.astype(jnp.float32) + out_delta.astype(jnp.float32)
    input_grad = cotangent.astype(jnp.float32) + in_delta.astype(jnp.float32)

    state_all = state_all.reshape(n_batch, LAYERS, part // 2, 8, 2, LANES // 2)
    state_all = state_all.transpose(1, 3, 0, 2, 4, 5).reshape(LAYERS, 8, own, -1)
    state_total = state_all[:, :4]
    step_total = jnp.sum(state_all[:, 4], -1)
    lin_total = lin_all.reshape(n_batch, LAYERS, 2, part, chans).transpose(1, 0, 3, 2, 4).reshape(LAYERS, own, 2, chans)
    vec_sum = jnp.sum(vec_all, 0)[: 5 * LAYERS, :own].reshape(LAYERS, 5, own)
    vec_total = jnp.stack([vec_sum[:, 0], vec_sum[:, 1], step_total, vec_sum[:, 2], vec_sum[:, 3], vec_sum[:, 4]])

    vec_old = jnp.stack([ln_gain, ln_bias, log_step, skip_gain, lin_bias[:, 0], lin_bias[:, 1]])
    state_old = jnp.stack([log_decay, frequency, w_re, w_im], 1)
    lin_first, lin_second, lin_new = adam(lin_weight, lin_total, lin_moment, lin_square, 0.05)
    turned = [a.transpose(1, 0, 2) for a in (vec_moment, vec_square)]
    vec_first, vec_second, vec_new = [a.transpose(1, 0, 2) for a in adam(vec_old, vec_total, *turned, 0.2)]
    state_first, state_second, state_new = adam(state_old, state_total, state_moment, state_square, 0.2)
    return (
        output, input_grad, lin_first, lin_second, lin_new, vec_first, vec_second, vec_new,
        state_first, state_second, state_new,
    )


def tables(length):
    full_width = 2 * length
    row_ids = lax.iota(jnp.int32, length)[:, None]
    col_ids = lax.iota(jnp.int32, length)[None, :]
    turn_all = (row_ids * col_ids % full_width).astype(jnp.float32) * (2.0 * math.pi / full_width)
    cosine = jnp.cos(turn_all)
    sine_table = jnp.sin(turn_all)
    weights = jnp.where(lax.iota(jnp.int32, length) == 0, 1.0, 2.0).astype(jnp.float32)[None, :]
    alternate = (1 - 2 * (lax.iota(jnp.int32, length) % 2)).astype(jnp.float32)
    return (cosine, sine_table, cosine * weights, sine_table * weights, alternate)


def mixer(normed, log_decay, frequency, w_re, w_im, log_step, skip_gain):
    top_prec = lax.Precision.HIGHEST
    chan_count = normed.shape[0]
    seq_count = normed.shape[1] // BUCKET
    step_size = jnp.exp(log_step)[:, None]
    decay_rate = step_size * jnp.exp(log_decay)
    turn_rate = step_size * frequency
    places = lax.iota(jnp.float32, BUCKET)
    decay_all = jnp.exp(-decay_rate[..., None] * places)
    soft = decay_all / jnp.sum(decay_all, -1, keepdims=True)
    phase_all = turn_rate[..., None] * places
    kernel = jnp.sum(
        (w_re[..., None] * jnp.cos(phase_all) - w_im[..., None] * jnp.sin(phase_all)) * soft, 1
    )
    cosine, sine_table, cos_back, sin_back, alternate = tables(BUCKET)
    signal = normed.reshape(chan_count, seq_count, BUCKET)
    sig_re = jnp.einsum("csl,lk->csk", signal, cosine, precision=top_prec)
    sig_im = -jnp.einsum("csl,lk->csk", signal, sine_table, precision=top_prec)
    sig_top = jnp.sum(signal * alternate, -1)
    ker_re = jnp.dot(kernel, cosine, precision=top_prec)[:, None, :]
    ker_im = -jnp.dot(kernel, sine_table, precision=top_prec)[:, None, :]
    ker_top = jnp.sum(kernel * alternate, -1)[:, None]
    prod_re = sig_re * ker_re - sig_im * ker_im
    prod_im = sig_re * ker_im + sig_im * ker_re
    prod_top = sig_top * ker_top
    conv_out = jnp.einsum("csk,lk->csl", prod_re, cos_back, precision=top_prec)
    conv_out = conv_out - jnp.einsum("csk,lk->csl", prod_im, sin_back, precision=top_prec)
    conv_out = conv_out + prod_top[..., None] * alternate
    conv_out = conv_out / (2.0 * BUCKET)
    pre_act = conv_out.reshape(normed.shape) + skip_gain[:, None] * normed
    return jax.nn.gelu(pre_act)


def wide_local(
    inputs,
    lengths,
    cotangent,
    ln_gain,
    ln_bias,
    log_step,
    skip_gain,
    lin_bias,
    log_decay,
    frequency,
    w_re,
    w_im,
    lin_weight,
    lin_moment,
    lin_square,
    vec_moment,
    vec_square,
    state_moment,
    state_square,
):
    chan_total = inputs.shape[0] * lax.axis_size("chan")
    tok_count = inputs.shape[1]
    places = lax.iota(jnp.int32, BUCKET)
    valid = (places[None, :] < lengths[:, None]).astype(jnp.float32).reshape(1, tok_count)
    weights_low = lin_weight.astype(jnp.bfloat16)
    stream = inputs.astype(jnp.float32)
    saved = []
    for layer_idx in range(LAYERS):
        sums = lax.psum((jnp.sum(stream, 0), jnp.sum(stream * stream, 0)), "chan")
        mean_val = sums[0] / chan_total
        variance = sums[1] / chan_total - mean_val * mean_val
        inv_std = lax.rsqrt(variance + 1e-05)[None, :]
        centred = (stream - mean_val[None, :]) * inv_std
        normed = centred * ln_gain[layer_idx][:, None] + ln_bias[layer_idx][:, None]
        activated, mixer_back = jax.vjp(
            mixer,
            normed,
            log_decay[layer_idx],
            frequency[layer_idx],
            w_re[layer_idx],
            w_im[layer_idx],
            log_step[layer_idx],
            skip_gain[layer_idx],
        )
        act_low = activated.astype(jnp.bfloat16)
        act_all = lax.all_gather(act_low, "chan", axis=0, tiled=True)
        mixed = jnp.einsum(
            "ht,cjh->cjt", act_all, weights_low[layer_idx], preferred_element_type=jnp.float32
        )
        kept = act_all
        mixed = mixed + lin_bias[layer_idx].T[:, :, None]
        gate_in = mixed[:, 0]
        gate_val = mixed[:, 1]
        stream = stream + valid * gate_in * jax.nn.sigmoid(gate_val)
        saved.append((centred, inv_std, mixer_back, kept, gate_in, gate_val))
    back_stream = cotangent.astype(jnp.float32)
    lin_grads = [None] * LAYERS
    vec_grads = [None] * LAYERS
    state_grads = [None] * LAYERS
    for layer_idx in reversed(range(LAYERS)):
        centred, inv_std, mixer_back, kept, gate_in, gate_val = saved[layer_idx]
        sigma = jax.nn.sigmoid(gate_val)
        gated_back = back_stream * valid
        grad_mixed = jnp.stack(
            [gated_back * sigma, gated_back * gate_in * sigma * (1.0 - sigma)], 1
        ).astype(jnp.bfloat16)
        bias_grad = jnp.sum(grad_mixed.astype(jnp.float32), 2).T
        weight_grad = jnp.einsum(
            "ht,cjt->cjh", kept, grad_mixed, preferred_element_type=jnp.float32
        )
        act_part = jnp.einsum(
            "cjt,cjh->ht", grad_mixed, weights_low[layer_idx], preferred_element_type=jnp.float32
        )
        act_grad = lax.psum_scatter(act_part, "chan", scatter_dimension=0, tiled=True)
        normed_grad, decay_grad, freq_grad, re_grad, im_grad, step_grad, skip_grad = mixer_back(
            act_grad
        )
        gain_grad = jnp.sum(normed_grad * centred, 1)
        shift_grad = jnp.sum(normed_grad, 1)
        centred_grad = normed_grad * ln_gain[layer_idx][:, None]
        back_sums = lax.psum((jnp.sum(centred_grad, 0), jnp.sum(centred_grad * centred, 0)), "chan")
        back_stream = back_stream + inv_std * (
            centred_grad
            - back_sums[0][None, :] / chan_total
            - centred * back_sums[1][None, :] / chan_total
        )
        lin_grads[layer_idx] = weight_grad
        vec_grads[layer_idx] = jnp.stack(
            [gain_grad, shift_grad, step_grad, skip_grad, bias_grad[0], bias_grad[1]]
        )
        state_grads[layer_idx] = jnp.stack([decay_grad, freq_grad, re_grad, im_grad])
    lin_total, vec_total, state_total = lax.psum(
        (jnp.stack(lin_grads), jnp.stack(vec_grads), jnp.stack(state_grads)), "batch"
    )
    vec_old = jnp.stack([ln_gain, ln_bias, log_step, skip_gain, lin_bias[:, 0], lin_bias[:, 1]], 1)
    state_old = jnp.stack([log_decay, frequency, w_re, w_im], 1)
    lin_first, lin_second, lin_new = adam(lin_weight, lin_total, lin_moment, lin_square, 0.05)
    vec_first, vec_second, vec_new = adam(vec_old, vec_total, vec_moment, vec_square, 0.2)
    state_first, state_second, state_new = adam(
        state_old, state_total, state_moment, state_square, 0.2
    )
    return (
        stream,
        back_stream,
        lin_first,
        lin_second,
        lin_new,
        vec_first,
        vec_second,
        vec_new,
        state_first,
        state_second,
        state_new,
    )


def suits(own_seqs, chans, n_chan, n_batch):
    powers = n_chan & (n_chan - 1) == 0 and n_batch & (n_batch - 1) == 0
    return powers and own_seqs == 2 * n_chan and (n_chan, n_batch) == (8, 4) and chans == 16 * n_chan * n_batch


def solution(mesh):
    in_specs = (
        P("chan", "batch"),
        P("batch"),
        P("chan", "batch"),
        P(None, "chan"),
        P(None, "chan"),
        P(None, "chan"),
        P(None, "chan"),
        P(None, None, "chan"),
        P(None, "chan", None),
        P(None, "chan", None),
        P(None, "chan", None),
        P(None, "chan", None),
        P(None, "chan", None, None),
        P(None, "chan", None, None),
        P(None, "chan", None, None),
        P(None, None, "chan"),
        P(None, None, "chan"),
        P(None, None, "chan", None),
        P(None, None, "chan", None),
    )
    out_specs = (
        P("chan", "batch"),
        P("chan", "batch"),
        P(None, "chan", None, None),
        P(None, "chan", None, None),
        P(None, "chan", None, None),
        P(None, None, "chan"),
        P(None, None, "chan"),
        P(None, None, "chan"),
        P(None, None, "chan", None),
        P(None, None, "chan", None),
        P(None, None, "chan", None),
    )
    n_chan = mesh.shape["chan"]

    def run(*args):
        own_seqs = args[1].shape[0] // mesh.shape["batch"]
        fits = suits(own_seqs, args[3].shape[1], n_chan, mesh.shape["batch"])
        body = local if fits else wide_local
        return jax.shard_map(body, mesh=mesh, in_specs=in_specs, out_specs=out_specs, check_vma=False)(*args)

    return run
```
